32 devices in a mesh: stream: 2 (over x), batch: 16 (over z, y, core).
Axes of the slice: x: 2, y: 2, z: 4, core: 2. Of those that a mesh axis runs over, the one named last changes fastest.
Arguments:
- inputs: bfloat16 [2, 32, 512, 768], P('stream', 'batch'), may hold values from -6 to 6
- lengths: int32 [2, 32, 16], P('stream', 'batch'), may hold values from 1 to 64, 512 in all within a row
- positives: int32 [512], P('batch'), may hold values from 0 to 511, each once
- query_weight: bfloat16 [768, 768], replicated, may hold values from -0.21875 to 0.21875
- query_bias: bfloat16 [768], replicated, may hold values from -3 to 3
- key_weight: bfloat16 [768, 768], replicated, may hold values from -0.21875 to 0.21875
- value_weight: bfloat16 [768, 768], replicated, may hold values from -0.21875 to 0.21875
- value_bias: bfloat16 [768], replicated, may hold values from -3 to 3
- output_weight: bfloat16 [768, 768], replicated, may hold values from -1.25 to 1.25
- output_bias: bfloat16 [768], replicated, may hold values from -3 to 3
- first_gain: bfloat16 [768], replicated, may hold values from 0.099609375 to 1.8984375
- first_shift: bfloat16 [768], replicated, may hold values from -1.75 to 1.75
- up_weight: bfloat16 [768, 3072], replicated, may hold values from -0.21875 to 0.21875
- up_bias: bfloat16 [3072], replicated, may hold values from -3 to 3
- down_weight: bfloat16 [3072, 768], replicated, may hold values from -0.109375 to 0.109375
- down_bias: bfloat16 [768], replicated, may hold values from -3 to 3
- second_gain: bfloat16 [768], replicated, may hold values from 0.099609375 to 1.8984375
- second_shift: bfloat16 [768], replicated, may hold values from -0.625 to 0.625
Outputs:
- contrast_terms: float32 [2, 512], P('stream', 'batch')
- input_grad: float32 [2, 32, 512, 768], P('stream', 'batch')
- query_weight_grad: float32 [768, 768], replicated
- query_bias_grad: float32 [768], replicated
- key_weight_grad: float32 [768, 768], replicated
- value_weight_grad: float32 [768, 768], replicated
- value_bias_grad: float32 [768], replicated
- output_weight_grad: float32 [768, 768], replicated
- output_bias_grad: float32 [768], replicated
- first_gain_grad: float32 [768], replicated
- first_shift_grad: float32 [768], replicated
- up_weight_grad: float32 [768, 3072], replicated
- up_bias_grad: float32 [3072], replicated
- down_weight_grad: float32 [3072, 768], replicated
- down_bias_grad: float32 [768], replicated
- second_gain_grad: float32 [768], replicated
- second_shift_grad: float32 [768], replicated
The draws below stay inside these ranges and needn't reach their ends.
Inputs may be any that keep to these rules, and one draw needn't show every extreme that they name: `positives`: every document index is the positive of exactly one query. The 16 lengths of a packed row sum to 512.
All inputs are finite; a program needn't handle non-finite values.
Results may differ from the reference program's by a relative error of at most 0.01345.
Values may be sent and summed in bfloat16 or wider, within the bound.
No kernel may reach another device: no remote copies, remote signals or barrier semaphores. Data moves between devices by JAX's collectives and lax.ppermute only.
A program may use at most 256 MiB of HBM per device.

```python
import math
import jax
import jax.numpy as jnp
import numpy as np
from jax import lax

D = 768
HEAD_DIM = 64
FF = 3072
SEQ = 512
SEGS = 16
MOST = 64
ROWS_DEV = 2
ROWS = 32
QUERIES = 512


def level_of(key, shape, pieces, least, largest):
    def one(position, parts):
        draws = jax.random.uniform(jax.random.fold_in(jax.random.fold_in(key, 6), position), (parts,), jnp.float32, least / len(pieces), largest / len(pieces))
        return jnp.repeat(jnp.exp(draws), shape[position] // parts).reshape((-1,) + (1,) * (len(shape) - position - 1))

    loudness = one(*pieces[0])
    for cut in pieces[1:]:
        loudness = loudness * one(*cut)
    return loudness


def split_up(amount, total, limit, lean):
    weights = [(1 << 20) // math.isqrt(standing ** lean) + 1 for standing in range(2, amount + 1)]
    spare, holding = total - limit - (amount - 1), [1] * (amount - 1)
    while spare > 0:
        movable = [i for i in range(amount - 1) if holding[i] < limit]
        mass, budget = sum([weights[i] for i in movable]), spare
        for i in movable:
            addition = min(limit - holding[i], max(1, budget * weights[i] // mass), spare)
            holding[i] = holding[i] + addition
            spare = spare - addition
    return np.array([limit] + holding)


def ragged_sizes(rng, count, total, most, skew):
    if count == 2:
        one = jax.random.randint(rng, (), max(1, total - most), min(most, total - 1) + 1)
        return jnp.stack([one, total - one])
    sizes = jnp.asarray(split_up(count, total, most, skew), jnp.int32)
    couples = (count - 1) // 2
    source_of, taker = sizes[1:1 + 2 * couples:2], sizes[2:2 + 2 * couples:2]
    slack = jnp.minimum(source_of - 1, most - taker)
    moved = jax.random.randint(jax.random.fold_in(rng, 1), (couples,), 0, 1 << 20) % (slack + 1)
    sizes = sizes.at[1:1 + 2 * couples:2].set(source_of - moved).at[2:2 + 2 * couples:2].set(taker + moved)
    return sizes[jax.random.permutation(jax.random.fold_in(rng, 2), count)]


def scatter_about(own_key, shape, scale, most, pieces=(), kind=jnp.bfloat16):
    drawn = jax.random.normal(own_key, shape, jnp.float32) * scale
    if len(pieces) > 0:
        drawn = level_of(own_key, shape, pieces, -0.22, 0.18) * drawn
    return jnp.clip(drawn, min=-most, max=most).astype(kind)


def setup_inputs(seed: int = 0) -> dict:
    key_of = jax.random.split(jax.random.key(seed), 19)
    return {
        "inputs": scatter_about(key_of[0], (2, ROWS, SEQ, D), 1.0, 6.0, ((0, 2), (1, 16))),
        "lengths": jax.vmap(lambda own: ragged_sizes(own, SEGS, SEQ, MOST, 1))(jax.random.split(key_of[1], 2 * ROWS)).reshape((2, ROWS, SEGS)).astype(jnp.int32),
        "positives": jax.random.permutation(key_of[2], QUERIES).astype(jnp.int32),
        "query_weight": scatter_about(key_of[3], (D, D), D ** -0.5, 0.21875),
        "query_bias": scatter_about(key_of[4], (D,), 0.5, 3.0),
        "key_weight": scatter_about(key_of[5], (D, D), D ** -0.5, 0.21875),
        "value_weight": scatter_about(key_of[6], (D, D), D ** -0.5, 0.21875),
        "value_bias": scatter_about(key_of[7], (D,), 0.5, 3.0),
        "output_weight": scatter_about(key_of[8], (D, D), (D // 32) ** -0.5, 1.25),
        "output_bias": scatter_about(key_of[9], (D,), 0.5, 3.0),
        "first_gain": jnp.clip(1.0 + 0.18 * jax.random.normal(key_of[10], (D,), jnp.float32), 0.099609375, 1.8984375).astype(jnp.bfloat16),
        "first_shift": scatter_about(key_of[11], (D,), 0.3, 1.75),
        "up_weight": scatter_about(key_of[12], (D, FF), D ** -0.5, 0.21875),
        "up_bias": scatter_about(key_of[13], (FF,), 0.5, 3.0),
        "down_weight": scatter_about(key_of[14], (FF, D), FF ** -0.5, 0.109375),
        "down_bias": scatter_about(key_of[15], (D,), 0.5, 3.0),
        "second_gain": jnp.clip(1.0 + 0.18 * jax.random.normal(key_of[16], (D,), jnp.float32), 0.099609375, 1.8984375).astype(jnp.bfloat16),
        "second_shift": scatter_about(key_of[17], (D,), 0.1, 0.625),
    }


@jax.custom_vjp
def low(v):
    return lax.optimization_barrier(v.astype(jnp.bfloat16)).astype(jnp.float32)

@jax.custom_vjp
def low_back(v):
    return v

def low_keep(v):
    return (low(v), None)

def low_pass(kept, grad):
    return (grad,)

def back_keep(v):
    return (v, None)

def back_low(kept, grad):
    return (low(grad),)
low.defvjp(low_keep, low_pass)
low_back.defvjp(back_keep, back_low)

def both_ways(values):
    return low(low_back(values))

def matmul(former, latter):
    return jnp.matmul(former, latter, precision=lax.Precision.HIGHEST)

def layer_norm(values, norm_gain, norm_shift):
    centred = values - lax.optimization_barrier(jnp.mean(values, axis=-1, keepdims=True))
    spread = lax.optimization_barrier(jnp.mean(centred * centred, axis=-1, keepdims=True))
    return centred * lax.rsqrt(spread + 1e-12) * norm_gain + norm_shift

def segment_table(row_lengths, row_span):
    seg_ends = jnp.cumsum(row_lengths, axis=-1, dtype=jnp.int32)
    positions = jnp.arange(row_span, dtype=jnp.int32)
    return lax.optimization_barrier(jnp.sum((positions[None, :, None] >= seg_ends[:, None, :]).astype(jnp.int32), axis=-1, dtype=jnp.int32))

def encode(row_block, row_lengths, weights):
    query_weight, query_bias, key_weight, value_weight, value_bias, output_weight, output_bias, first_gain, first_shift, up_weight, up_bias, down_weight, down_bias, second_gain, second_shift = weights
    row_count, row_span, model_width = row_block.shape
    head_count = model_width // HEAD_DIM
    segment = segment_table(row_lengths, row_span)
    query_rows = both_ways(matmul(row_block, query_weight) + query_bias).reshape(row_count, row_span, head_count, HEAD_DIM)
    key_rows = both_ways(matmul(row_block, key_weight)).reshape(row_count, row_span, head_count, HEAD_DIM)
    value_rows = both_ways(matmul(row_block, value_weight) + value_bias).reshape(row_count, row_span, head_count, HEAD_DIM)
    scores = jnp.einsum('bihd,bjhd->bhij', query_rows, key_rows, precision=lax.Precision.HIGHEST) * HEAD_DIM ** (-0.5)
    same_seg = (segment[:, :, None] == segment[:, None, :])[:, None]
    scores = low_back(jnp.where(same_seg, scores, -1000000000.0))
    shifted = scores - lax.optimization_barrier(jnp.max(scores, axis=-1, keepdims=True))
    exponent = jnp.exp(shifted)
    attention = low(exponent / lax.optimization_barrier(jnp.sum(exponent, axis=-1, keepdims=True)))
    context = jnp.einsum('bhij,bjhd->bihd', attention, value_rows, precision=lax.Precision.HIGHEST)
    context = both_ways(context.reshape(row_count, row_span, model_width))
    attended = low_back(matmul(context, output_weight) + output_bias)
    hidden = layer_norm(row_block + attended, first_gain, first_shift)
    preactivation = low_back(matmul(low(hidden), up_weight) + up_bias)
    activation = low(jax.nn.gelu(preactivation, approximate=False))
    branch = low_back(matmul(activation, down_weight) + down_bias)
    result = layer_norm(hidden + branch, second_gain, second_shift)
    membership = (segment[:, None, :] == jnp.arange(SEGS, dtype=jnp.int32)[None, :, None]).astype(jnp.float32)
    pooled = matmul(membership, result) / row_lengths[:, :, None].astype(jnp.float32)
    embedding = pooled * lax.rsqrt(lax.optimization_barrier(jnp.sum(pooled * pooled, axis=-1, keepdims=True)) + 1e-06)
    return both_ways(embedding).reshape(row_count * SEGS, model_width)

def log_sum_exp(values, axis):
    highest = lax.optimization_barrier(jnp.max(values, axis=axis, keepdims=True))
    return jnp.squeeze(jnp.log(lax.optimization_barrier(jnp.sum(jnp.exp(values - highest), axis=axis, keepdims=True))) + highest, axis)

def reference(inputs, lengths, positives, query_weight, query_bias, key_weight, value_weight, value_bias, output_weight, output_bias, first_gain, first_shift, up_weight, up_bias, down_weight, down_bias, second_gain, second_shift):
    weights = tuple((weight.astype(jnp.float32) for weight in (query_weight, query_bias, key_weight, value_weight, value_bias, output_weight, output_bias, first_gain, first_shift, up_weight, up_bias, down_weight, down_bias, second_gain, second_shift)))
    row_data = inputs.astype(jnp.float32)
    groups = 2 * ROWS // ROWS_DEV

    def forward(row_data, weights):
        grouped = row_data.reshape(groups, ROWS_DEV, SEQ, D)
        grouped_lengths = lengths.reshape(groups, ROWS_DEV, SEGS)
        encoder = jax.checkpoint(lambda bundle: encode(bundle[0], bundle[1], weights))
        embeds = lax.map(encoder, (grouped, grouped_lengths)).reshape(2, QUERIES, D)
        logits = matmul(embeds[0], embeds[1].T) / 0.05
        row_logits = low_back(logits)
        column_logits = low_back(logits)
        pair_index = positives[:, None].astype(jnp.int32)
        row_terms = log_sum_exp(row_logits, 1) - jnp.take_along_axis(row_logits, pair_index, axis=-1)[:, 0]
        doc_index = jnp.arange(QUERIES, dtype=jnp.int32)
        doc_target = (positives[:, None] == doc_index[None, :]).astype(jnp.float32)
        column_terms = log_sum_exp(column_logits, 0) - lax.optimization_barrier(jnp.sum(column_logits * doc_target, axis=0))
        loss = (jnp.sum(row_terms) + jnp.sum(column_terms)) / (2.0 * QUERIES)
        return (loss, jnp.stack([row_terms, column_terms]))
    contrast_loss, pullback, contrast_terms = jax.vjp(forward, row_data, weights, has_aux=True)
    input_grad, weight_grads = pullback(jnp.ones_like(contrast_loss))
    return (contrast_terms, input_grad, weight_grads[0], weight_grads[1], weight_grads[2], weight_grads[3], weight_grads[4], weight_grads[5], weight_grads[6], weight_grads[7], weight_grads[8], weight_grads[9], weight_grads[10], weight_grads[11], weight_grads[12], weight_grads[13], weight_grads[14])
```

```python
import functools

import jax
import jax.numpy as jnp
import numpy as np
from jax import lax
from jax.experimental import pallas as pl
from jax.experimental.pallas import tpu as pltpu
from jax.sharding import PartitionSpec as P

HEAD_DIM = 64
VMEM_LIMIT = 56 * 2**20
TILE = 512
LABELS = 16
BOTH = ("stream", "batch")


def link_dims(batch_size):
    bits = batch_size.bit_length() - 1
    main = [("stream", 1), ("batch", 2), ("batch", 1 << (bits - 2)), ("batch", 3 << (bits - 2))]
    rest = [("batch", 1 << j) for j in range(2, bits - 2)]
    return main, rest


def coordinate(dim, stream, batch, batch_size):
    bits = batch_size.bit_length() - 1
    if dim[0] == "stream":
        return stream
    mask = dim[1]
    top = (batch >> (bits - 1)) & 1
    if mask == 3 << (bits - 2):
        return top
    if mask == 1 << (bits - 2):
        return ((batch >> (bits - 2)) & 1) ^ top
    return (batch >> (mask.bit_length() - 1)) & 1


def flipped(dim, stream, batch):
    return (stream ^ 1, batch) if dim[0] == "stream" else (stream, batch ^ dim[1])


def exchange(array, even_dim, odd_dim, sizes):
    pairs = []
    for stream in range(sizes[0]):
        for batch in range(sizes[1]):
            other = flipped(odd_dim if batch & 1 else even_dim, stream, batch)
            pairs.append((stream * sizes[1] + batch, other[0] * sizes[1] + other[1]))
    return lax.ppermute(array, BOTH, pairs)


CORE = ("batch", 1)


def reduce_orders(batch_size):
    (x, y, a, b), rest = link_dims(batch_size)
    return (((x, a, y, b), (y, b, x, a)), ((a, x, b, y), (b, y, a, x))), rest


def gather_orders(batch_size):
    (x, y, a, b), rest = link_dims(batch_size)
    return (tuple(rest) + (a, x, b, y), tuple(rest) + (x, a, y, b))


def block_scalars(sizes):
    stream, batch = lax.axis_index("stream"), lax.axis_index("batch")
    orders, _ = reduce_orders(sizes[1])
    labels = []
    for core in range(2):
        for half in range(2):
            label = 0
            for dim in orders[core][half]:
                label = label * 2 + coordinate(dim, stream, batch, sizes[1])
            labels.append(label)
    return jnp.stack([batch & 1] + labels).astype(jnp.int32)


def full_spec(shape):
    return pl.BlockSpec(shape, lambda *_: (0,) * len(shape))


def put_block(scalars, matrix, product, send_ref, keep_ref):
    core, label = scalars[0], scalars[1 + matrix]
    rows = product.shape[0] // LABELS

    def put(target):
        for own in range(LABELS):
            target[matrix % 2, own ^ label] = product[own * rows : (own + 1) * rows].astype(target.dtype)

    @pl.when(core == matrix // 2)
    def _():
        put(keep_ref)

    @pl.when(core != matrix // 2)
    def _():
        put(send_ref)


def weight_kernel(pairs, scalars, *refs):
    sources, (send_ref, keep_ref) = refs[:-2], refs[-2:]
    width = send_ref.shape[3]
    for matrix, (left, left_at, right, right_at) in enumerate(pairs):
        product = lax.dot_general(
            sources[left][:, left_at : left_at + width],
            sources[right][:, right_at : right_at + width],
            (((0,), (0,)), ((), ())),
            preferred_element_type=jnp.float32,
        )
        put_block(scalars, matrix, product, send_ref, keep_ref)


def weight_grads(scalars, sources, pairs, width, name):
    tokens = sources[0].shape[0]
    shape = (2, LABELS, width // LABELS, width)
    return pl.pallas_call(
        functools.partial(weight_kernel, pairs),
        grid_spec=pltpu.PrefetchScalarGridSpec(
            num_scalar_prefetch=1,
            grid=(1,),
            in_specs=[full_spec(source.shape) for source in sources],
            out_specs=[full_spec(shape)] * 2,
        ),
        out_shape=[jax.ShapeDtypeStruct(shape, jnp.bfloat16)] * 2,
        compiler_params=pltpu.CompilerParams(vmem_limit_bytes=VMEM_LIMIT),
        cost_estimate=pl.CostEstimate(
            flops=8 * tokens * width * width,
            bytes_accessed=2 * sum(s.size for s in sources) + 8 * width * width,
            transcendentals=0,
        ),
        name=name,
    )(scalars, *sources)


def added(former, latter):
    return (former.astype(jnp.float32) + latter.astype(jnp.float32)).astype(jnp.bfloat16)


def reduce_blocks(send, keep, sizes):
    orders, rest = reduce_orders(sizes[1])
    received = exchange(send, CORE, CORE, sizes)
    halves = [added(keep[half], received[half]) for half in range(2)]
    for step in range(4):
        cut = LABELS >> (step + 1)
        arrived = [
            exchange(halves[half][cut:], orders[0][half][step], orders[1][half][step], sizes)
            for half in range(2)
        ]
        halves = [added(halves[half][:cut], arrived[half]) for half in range(2)]
    for dim in rest:
        halves = [added(value, exchange(value, dim, dim, sizes)) for value in halves]
    return halves


def gather_blocks(halves, sizes):
    orders, _ = reduce_orders(sizes[1])
    for step in reversed(range(4)):
        arrived = [
            exchange(halves[half], orders[0][half][step], orders[1][half][step], sizes)
            for half in range(2)
        ]
        halves = [jnp.concatenate([halves[half], arrived[half]], axis=0) for half in range(2)]
    return halves + [exchange(value, CORE, CORE, sizes) for value in halves]


def spread_kernel(wide, scalars, *refs):
    sources, targets = refs[:4], refs[4:]
    core = scalars[0]
    rows, width = sources[0].shape[1:]
    for matrix in range(4):
        label = scalars[1 + matrix] & 3

        def put(source, matrix=matrix, label=label):
            for own in range(4):
                value = source[own ^ label].astype(jnp.float32)
                at = pl.ds(own * rows, rows)
                if wide:
                    targets[0][at, matrix * width : (matrix + 1) * width] = value
                elif len(targets) == 1:
                    targets[0][matrix, at] = value
                else:
                    targets[matrix][at] = value

        @pl.when(core == matrix // 2)
        def _():
            put(sources[matrix % 2])

        @pl.when(core != matrix // 2)
        def _():
            put(sources[2 + matrix % 2])


def spread(scalars, blocks, kind, name):
    _, rows, width = blocks[0].shape
    group = 4 * rows

    def source_spec(place):
        half, foreign = place % 2, place // 2

        def at(i, scalars):
            owner = scalars[0] ^ foreign
            label = jnp.where(owner == 0, scalars[1 + half], scalars[3 + half])
            return (i ^ (label >> 2), 0, 0)

        return pl.BlockSpec((4, rows, width), at)

    if kind == "wide":
        out_specs = [pl.BlockSpec((group, 4 * width), lambda i, s: (i, 0))]
        out_shape = [jax.ShapeDtypeStruct((width, 4 * width), jnp.float32)]
    elif kind == "tall":
        out_specs = [pl.BlockSpec((4, group, width), lambda i, s: (0, i, 0))]
        out_shape = [jax.ShapeDtypeStruct((4, width, width), jnp.float32)]
    else:
        out_specs = [pl.BlockSpec((group, width), lambda i, s: (i, 0))] * 4
        out_shape = [jax.ShapeDtypeStruct((width, width), jnp.float32)] * 4
    return pl.pallas_call(
        functools.partial(spread_kernel, kind == "wide"),
        grid_spec=pltpu.PrefetchScalarGridSpec(
            num_scalar_prefetch=1,
            grid=(LABELS // 4,),
            in_specs=[source_spec(place) for place in range(4)],
            out_specs=out_specs,
        ),
        out_shape=out_shape,
        compiler_params=pltpu.CompilerParams(vmem_limit_bytes=VMEM_LIMIT),
        cost_estimate=pl.CostEstimate(
            flops=0, bytes_accessed=24 * width * width, transcendentals=0
        ),
        name=name,
    )(scalars, *blocks)


def gather_embeddings(own, sizes):
    orders = gather_orders(sizes[1])
    value = own[None]
    for even_dim, odd_dim in zip(*orders, strict=True):
        value = jnp.concatenate([value, exchange(value, even_dim, odd_dim, sizes)], axis=0)
    return value, exchange(value, CORE, CORE, sizes)


def gather_places(sizes):
    orders = gather_orders(sizes[1])
    tables = []
    for order in orders:
        table = []
        for place in range(1 << len(order)):
            at = (0, 0)
            for step, dim in enumerate(order):
                if place >> step & 1:
                    at = flipped(dim, *at)
            table.append(at)
        tables.append(table)
    even, odd = (np.array(table, np.int32) for table in tables)
    batch = lax.axis_index("batch")
    core = (batch & 1).astype(jnp.int32)
    own = jnp.where(core == 0, even, odd)
    foreign = jnp.where(core == 0, odd, even) ^ np.array([[0, 1]], np.int32)
    places = jnp.concatenate([own, foreign], axis=0)
    return places[:, 0], places[:, 1] ^ batch.astype(jnp.int32)


def contrast_kernel(scale, info, other, index, own_ref, foreign_ref, pooled_ref, lengths_ref, terms_ref, grad_ref, all_ref, digits_ref, totals_ref):
    half, texts, wide = own_ref.shape
    width = pooled_ref.shape[1]
    total = all_ref.shape[1]
    query_side, batch = info[0], info[1]

    def place(i, source, offset):
        at = pl.multiple_of(index[offset + i] * texts, texts)
        all_ref[other[offset + i], pl.ds(at, texts)] = source[i, :, :width]

        @pl.when(other[offset + i] == 1)
        def _():
            digits_ref[pl.ds(at, texts)] = source[i, :, width:]

    def place_own(i, carry):
        place(i, own_ref, 0)
        place(i, foreign_ref, half)
        return carry

    lax.fori_loop(0, half, place_own, 0)

    def dots(former, latter):
        return lax.dot_general(former, latter, (((1,), (1,)), ((), ())), preferred_element_type=jnp.float32)

    tile = min(TILE, total)
    totals_ref[...] = jnp.zeros_like(totals_ref)
    for column in range(total // tile):
        latter = all_ref[1, column * tile : (column + 1) * tile]

        def add(i, carry, latter=latter, column=column):
            former = all_ref[0, pl.ds(pl.multiple_of(i * tile, tile), tile)]
            sums = jnp.sum(jnp.exp(dots(former, latter) / 0.05), axis=0, keepdims=True)
            totals_ref[:, column * tile : (column + 1) * tile] += sums
            return carry

        lax.fori_loop(0, total // tile, add, 0)
    mine = all_ref[0, pl.ds(pl.multiple_of(batch * texts, texts), texts)]
    partners = all_ref[1]
    own_digits = own_ref[0, :, width:]
    logits = dots(mine, partners) / 0.05
    exponent = jnp.exp(logits)
    row_total = jnp.sum(exponent, axis=1, keepdims=True)
    own_target = (64.0 * own_digits[:, 0:1].astype(jnp.float32) + own_digits[:, 1:2].astype(jnp.float32)).astype(jnp.int32)
    lane = lax.broadcasted_iota(jnp.int32, (8, 128), 1)
    pick = jnp.where(lane == 0, 64.0, jnp.where(lane == 1, 1.0, 0.0)).astype(jnp.bfloat16)
    all_target = dots(pick, digits_ref[...])[0:1].astype(jnp.int32)
    columns = lax.broadcasted_iota(jnp.int32, (texts, total), 1)
    rows = batch * texts + lax.broadcasted_iota(jnp.int32, (texts, total), 0)
    query_hit = (own_target == columns).astype(jnp.float32)
    doc_hit = (all_target == rows).astype(jnp.float32)
    target = jnp.where(query_side == 1, query_hit, doc_hit)
    chosen = jnp.sum(logits * target, axis=1, keepdims=True)
    terms_ref[...] = jnp.broadcast_to(jnp.log(row_total) - chosen, terms_ref.shape)
    own_low = ((exponent / row_total - target) * scale).astype(jnp.bfloat16)
    cross_low = ((exponent / totals_ref[0:1, :] - target) * scale).astype(jnp.bfloat16)
    gradient = (
        jnp.dot(own_low, partners, preferred_element_type=jnp.float32)
        + jnp.dot(cross_low, partners, preferred_element_type=jnp.float32)
    ) / 0.05
    gradient = gradient.astype(jnp.bfloat16).astype(jnp.float32)
    pooled = pooled_ref[...]
    inverse_norm = lax.rsqrt(jnp.sum(pooled * pooled, axis=1, keepdims=True) + 1e-06)
    embedding = pooled * inverse_norm
    inner = jnp.sum(gradient * embedding, axis=1, keepdims=True)
    grad_ref[...] = inverse_norm * (gradient - embedding * inner) / lengths_ref[:, 0:1]


def contrast(own, foreign, pooled, seg_length, sizes):
    half, texts, wide = own.shape
    width = pooled.shape[1]
    total = sizes[1] * texts
    other, index = gather_places(sizes)
    info = jnp.stack([lax.axis_index("stream") == 0, lax.axis_index("batch")]).astype(jnp.int32)
    lengths = jnp.broadcast_to(seg_length, (texts, 128))
    terms, gradient = pl.pallas_call(
        functools.partial(contrast_kernel, 1.0 / (2.0 * total)),
        grid_spec=pltpu.PrefetchScalarGridSpec(
            num_scalar_prefetch=3,
            grid=(1,),
            in_specs=[
                full_spec(own.shape),
                full_spec(foreign.shape),
                full_spec(pooled.shape),
                full_spec(lengths.shape),
            ],
            out_specs=[full_spec((texts, 128)), full_spec(pooled.shape)],
            scratch_shapes=[
                pltpu.VMEM((2, total, width), jnp.bfloat16),
                pltpu.VMEM((total, wide - width), jnp.bfloat16),
                pltpu.VMEM((8, total), jnp.float32),
            ],
        ),
        out_shape=[
            jax.ShapeDtypeStruct((texts, 128), jnp.float32),
            jax.ShapeDtypeStruct(pooled.shape, jnp.float32),
        ],
        compiler_params=pltpu.CompilerParams(vmem_limit_bytes=VMEM_LIMIT),
        cost_estimate=pl.CostEstimate(
            flops=2 * total * total * width, bytes_accessed=8 * total * width, transcendentals=total * total
        ),
        name="contrast",
    )(info, other, index, own, foreign, pooled, lengths)
    return terms[:, 0], gradient


def sum_vectors(vector, sizes):
    (x, y, a, b), rest = link_dims(sizes[1])
    value = vector.reshape(-1, 128)
    for even_dim, odd_dim in [(d, d) for d in [CORE, x, y, a, b] + rest]:
        value = value + exchange(value, even_dim, odd_dim, sizes)
    return value.reshape(-1)


def layer_norm(values, norm_gain, norm_shift):
    centred = values - jnp.mean(values, axis=-1, keepdims=True)
    factor = lax.rsqrt(jnp.mean(centred * centred, axis=-1, keepdims=True) + 1e-12)
    normed = centred * factor
    return (normed * norm_gain + norm_shift, normed, factor)


def norm_back(gradient, normed, factor, norm_gain):
    inner = gradient * norm_gain
    centred = inner - jnp.mean(inner, axis=-1, keepdims=True)
    return factor * (centred - normed * jnp.mean(inner * normed, axis=-1, keepdims=True))


def product(former, latter):
    return jnp.dot(former, latter, preferred_element_type=jnp.float32)


def transposed(former, latter):
    return lax.dot_general(
        former, latter, (((0,), (0,)), ((), ())), preferred_element_type=jnp.float32
    )


def against(former, latter):
    return lax.dot_general(
        former, latter, (((1,), (1,)), ((), ())), preferred_element_type=jnp.float32
    )


def masked_scores(query_rows, key_rows, same_seg):
    scores = jnp.einsum("bihd,bjhd->bhij", query_rows, key_rows, preferred_element_type=jnp.float32)
    scores = scores * query_rows.shape[-1] ** (-0.5)
    return jnp.where(same_seg, scores, -1000000000.0)


def local(
    inputs,
    lengths,
    positives,
    query_weight,
    query_bias,
    key_weight,
    value_weight,
    value_bias,
    output_weight,
    output_bias,
    first_gain,
    first_shift,
    up_weight,
    up_bias,
    down_weight,
    down_bias,
    second_gain,
    second_shift,
):
    row_count, row_span, model_width = (inputs.shape[1], inputs.shape[2], inputs.shape[3])
    head_count = model_width // HEAD_DIM
    seg_count = lengths.shape[2]
    token_rows = inputs.reshape(row_count * row_span, model_width)
    row_lengths = lengths.reshape(row_count, seg_count)
    seg_ends = jnp.cumsum(row_lengths, axis=-1, dtype=jnp.int32)
    positions = jnp.arange(row_span, dtype=jnp.int32)
    segment = jnp.sum(
        (positions[None, :, None] >= seg_ends[:, None, :]).astype(jnp.int32),
        axis=-1,
        dtype=jnp.int32,
    )
    same_seg = (segment[:, :, None] == segment[:, None, :])[:, None]
    membership = (
        segment[:, None, :] == jnp.arange(seg_count, dtype=jnp.int32)[None, :, None]
    ).astype(jnp.float32)
    seg_length = row_lengths.astype(jnp.float32)[:, :, None]
    four_dims = (row_count, row_span, head_count, HEAD_DIM)
    query_rows = (product(token_rows, query_weight) + query_bias).astype(jnp.bfloat16)
    key_rows = product(token_rows, key_weight).astype(jnp.bfloat16)
    value_rows = (product(token_rows, value_weight) + value_bias).astype(jnp.bfloat16)
    query_four = query_rows.reshape(four_dims)
    key_four = key_rows.reshape(four_dims)
    value_four = value_rows.reshape(four_dims)
    scores = masked_scores(query_four, key_four, same_seg)
    highest = jnp.max(scores, axis=-1, keepdims=True)
    log_total = highest + jnp.log(jnp.sum(jnp.exp(scores - highest), axis=-1, keepdims=True))
    attention_low = jnp.exp(scores - log_total).astype(jnp.bfloat16)
    context = jnp.einsum(
        "bhij,bjhd->bihd", attention_low, value_four, preferred_element_type=jnp.float32
    )
    context = context.reshape(row_count * row_span, model_width).astype(jnp.bfloat16)
    attended = product(context, output_weight) + output_bias
    hidden, first_normed, first_factor = layer_norm(token_rows + attended, first_gain, first_shift)
    hidden_low = hidden.astype(jnp.bfloat16)
    preactivation = product(hidden_low, up_weight) + up_bias
    activation, gelu_back = jax.vjp(
        lambda vector: jax.nn.gelu(vector, approximate=False), preactivation
    )
    activation_low = activation.astype(jnp.bfloat16)
    branch = product(activation_low, down_weight) + down_bias
    result, second_normed, second_factor = layer_norm(hidden + branch, second_gain, second_shift)
    pooled = (
        jnp.einsum(
            "bsi,bid->bsd",
            membership,
            result.reshape(row_count, row_span, model_width),
            precision=lax.Precision.HIGHEST,
        )
        / seg_length
    )
    pooled = pooled.reshape(row_count * seg_count, model_width)
    inverse_norm = lax.rsqrt(jnp.sum(pooled * pooled, axis=-1, keepdims=True) + 1e-06)
    embedding = pooled * inverse_norm
    embedding_low = embedding.astype(jnp.bfloat16)
    sizes = (lax.axis_size("stream"), lax.axis_size("batch"))
    digits = jnp.stack([positives >> 6, positives & 63], axis=1).astype(jnp.bfloat16)
    digits = jnp.pad(digits, ((0, 0), (0, 126)))
    own, foreign = gather_embeddings(jnp.concatenate([embedding_low, digits], axis=1), sizes)
    contrast_terms, pooled_grad = contrast(
        own, foreign, pooled, seg_length.reshape(row_count * seg_count, 1), sizes
    )
    contrast_terms = contrast_terms.reshape(1, row_count * seg_count)
    pooled_grad = pooled_grad.reshape(row_count, seg_count, model_width)
    result_grad = jnp.einsum(
        "bsi,bsd->bid", membership, pooled_grad, precision=lax.Precision.HIGHEST
    )
    result_grad = result_grad.reshape(row_count * row_span, model_width)
    second_gain_grad = jnp.sum(result_grad * second_normed, axis=0)
    second_shift_grad = jnp.sum(result_grad, axis=0)
    second_sum_grad = norm_back(result_grad, second_normed, second_factor, second_gain)
    branch_grad = second_sum_grad.astype(jnp.bfloat16)
    scalars = block_scalars(sizes)
    down_send, down_keep = weight_grads(
        scalars,
        (activation_low, branch_grad),
        [(0, model_width * i, 1, 0) for i in range(4)],
        model_width,
        "down_weight_grad",
    )
    down_share = reduce_blocks(down_send, down_keep, sizes)
    down_bias_grad = jnp.sum(branch_grad.astype(jnp.float32), axis=0)
    (pre_grad,) = gelu_back(against(branch_grad, down_weight))
    pre_low = pre_grad.astype(jnp.bfloat16)
    up_send, up_keep = weight_grads(
        scalars,
        (hidden_low, pre_low),
        [(0, 0, 1, model_width * i) for i in range(4)],
        model_width,
        "up_weight_grad",
    )
    up_share = reduce_blocks(up_send, up_keep, sizes)
    up_bias_grad = jnp.sum(pre_low.astype(jnp.float32), axis=0)
    hidden_grad = second_sum_grad + against(pre_low, up_weight)
    first_gain_grad = jnp.sum(hidden_grad * first_normed, axis=0)
    first_shift_grad = jnp.sum(hidden_grad, axis=0)
    first_sum_grad = norm_back(hidden_grad, first_normed, first_factor, first_gain)
    attended_grad = first_sum_grad.astype(jnp.bfloat16)
    output_bias_grad = jnp.sum(attended_grad.astype(jnp.float32), axis=0)
    context_grad = against(attended_grad, output_weight).astype(jnp.bfloat16).reshape(four_dims)
    attention = jnp.exp(masked_scores(query_four, key_four, same_seg) - log_total)
    attention_again = attention.astype(jnp.bfloat16)
    prob_grad = jnp.einsum(
        "bihd,bjhd->bhij", context_grad, value_four, preferred_element_type=jnp.float32
    )
    value_grad = jnp.einsum(
        "bhij,bihd->bjhd", attention_again, context_grad, preferred_element_type=jnp.float32
    )
    value_grad = value_grad.reshape(row_count * row_span, model_width).astype(jnp.bfloat16)
    score_grad = attention * (prob_grad - jnp.sum(attention * prob_grad, axis=-1, keepdims=True))
    score_grad = score_grad.astype(jnp.bfloat16)
    query_grad = jnp.einsum(
        "bhij,bjhd->bihd", score_grad, key_four, preferred_element_type=jnp.float32
    )
    query_grad = (
        (query_grad * HEAD_DIM ** (-0.5))
        .reshape(row_count * row_span, model_width)
        .astype(jnp.bfloat16)
    )
    key_grad = jnp.einsum(
        "bhij,bihd->bjhd", score_grad, query_four, preferred_element_type=jnp.float32
    )
    key_grad = (
        (key_grad * HEAD_DIM ** (-0.5))
        .reshape(row_count * row_span, model_width)
        .astype(jnp.bfloat16)
    )
    query_bias_grad = jnp.sum(query_grad.astype(jnp.float32), axis=0)
    value_bias_grad = jnp.sum(value_grad.astype(jnp.float32), axis=0)
    input_grad = (
        first_sum_grad
        + against(query_grad, query_weight)
        + against(key_grad, key_weight)
        + against(value_grad, value_weight)
    )
    vector_grads = jnp.concatenate(
        [
            query_bias_grad,
            value_bias_grad,
            output_bias_grad,
            first_gain_grad,
            first_shift_grad,
            down_bias_grad,
            second_gain_grad,
            second_shift_grad,
            up_bias_grad,
        ]
    )
    mixed_send, mixed_keep = weight_grads(
        scalars,
        (token_rows, context, query_grad, key_grad, value_grad, attended_grad),
        [(0, 0, 2, 0), (0, 0, 3, 0), (0, 0, 4, 0), (1, 0, 5, 0)],
        model_width,
        "attention_weight_grads",
    )
    mixed_share = reduce_blocks(mixed_send, mixed_keep, sizes)
    (down_total,) = spread(scalars, gather_blocks(down_share, sizes), "tall", "down_spread")
    (up_total,) = spread(scalars, gather_blocks(up_share, sizes), "wide", "up_spread")
    query_total, key_total, value_total, output_total = spread(
        scalars, gather_blocks(mixed_share, sizes), "separate", "attention_spread"
    )
    hidden_width = up_weight.shape[1]
    summed = sum_vectors(vector_grads, sizes)
    return (
        contrast_terms,
        input_grad.reshape(1, row_count, row_span, model_width),
        query_total,
        summed[0:model_width],
        key_total,
        value_total,
        summed[model_width : 2 * model_width],
        output_total,
        summed[2 * model_width : 3 * model_width],
        summed[3 * model_width : 4 * model_width],
        summed[4 * model_width : 5 * model_width],
        up_total,
        summed[8 * model_width : 8 * model_width + hidden_width],
        down_total.reshape(hidden_width, model_width),
        summed[5 * model_width : 6 * model_width],
        summed[6 * model_width : 7 * model_width],
        summed[7 * model_width : 8 * model_width],
    )


def solution(mesh):
    return jax.shard_map(
        local,
        mesh=mesh,
        in_specs=(
            P("stream", "batch", None, None),
            P("stream", "batch", None),
            P("batch"),
            P(),
            P(),
            P(),
            P(),
            P(),
            P(),
            P(),
            P(),
            P(),
            P(),
            P(),
            P(),
            P(),
            P(),
            P(),
        ),
        out_specs=(
            P("stream", "batch"),
            P("stream", "batch", None, None),
            P(),
            P(),
            P(),
            P(),
            P(),
            P(),
            P(),
            P(),
            P(),
            P(),
            P(),
            P(),
            P(),
            P(),
            P(),
        ),
        check_vma=False,
    )
```

```python
import functools

import jax
import jax.numpy as jnp
import numpy as np
from jax import lax
from jax.experimental import pallas as pl
from jax.experimental.pallas import tpu as pltpu
from jax.sharding import PartitionSpec as P

HEAD_DIM = 64
VMEM_LIMIT = 56 * 2**20
TILE = 512
LABELS = 16
BOTH = ("stream", "batch")


def link_dims(batch_size):
    bits = batch_size.bit_length() - 1
    main = [("stream", 1), ("batch", 2), ("batch", 1 << (bits - 2)), ("batch", 3 << (bits - 2))]
    rest = [("batch", 1 << j) for j in range(2, bits - 2)]
    return main, rest


def coordinate(dim, stream, batch, batch_size):
    bits = batch_size.bit_length() - 1
    if dim[0] == "stream":
        return stream
    mask = dim[1]
    top = (batch >> (bits - 1)) & 1
    if mask == 3 << (bits - 2):
        return top
    if mask == 1 << (bits - 2):
        return ((batch >> (bits - 2)) & 1) ^ top
    return (batch >> (mask.bit_length() - 1)) & 1


def flipped(dim, stream, batch):
    return (stream ^ 1, batch) if dim[0] == "stream" else (stream, batch ^ dim[1])


def exchange(array, even_dim, odd_dim, sizes):
    pairs = []
    for stream in range(sizes[0]):
        for batch in range(sizes[1]):
            other = flipped(odd_dim if batch & 1 else even_dim, stream, batch)
            pairs.append((stream * sizes[1] + batch, other[0] * sizes[1] + other[1]))
    return lax.ppermute(array, BOTH, pairs)


CORE = ("batch", 1)


def reduce_orders(batch_size):
    (x, y, a, b), rest = link_dims(batch_size)
    return (((x, a, y, b), (y, b, x, a)), ((a, x, b, y), (b, y, a, x))), rest


def gather_orders(batch_size):
    (x, y, a, b), rest = link_dims(batch_size)
    return (tuple(rest) + (a, x, b, y), tuple(rest) + (x, a, y, b))


def block_scalars(sizes):
    stream, batch = lax.axis_index("stream"), lax.axis_index("batch")
    orders, _ = reduce_orders(sizes[1])
    labels = []
    for core in range(2):
        for half in range(2):
            label = 0
            for dim in orders[core][half]:
                label = label * 2 + coordinate(dim, stream, batch, sizes[1])
            labels.append(label)
    return jnp.stack([batch & 1] + labels).astype(jnp.int32)


def full_spec(shape):
    return pl.BlockSpec(shape, lambda *_: (0,) * len(shape))


def added(former, latter):
    return (former.astype(jnp.float32) + latter.astype(jnp.float32)).astype(jnp.bfloat16)


def reduce_blocks(send, keep, sizes):
    orders, rest = reduce_orders(sizes[1])
    received = exchange(send, CORE, CORE, sizes)
    halves = [added(keep[half], received[half]) for half in range(2)]
    for step in range(4):
        cut = LABELS >> (step + 1)
        arrived = [
            exchange(halves[half][cut:], orders[0][half][step], orders[1][half][step], sizes)
            for half in range(2)
        ]
        halves = [added(halves[half][:cut], arrived[half]) for half in range(2)]
    for dim in rest:
        halves = [added(value, exchange(value, dim, dim, sizes)) for value in halves]
    return halves


def gather_blocks(halves, sizes):
    orders, _ = reduce_orders(sizes[1])
    for step in reversed(range(4)):
        arrived = [
            exchange(halves[half], orders[0][half][step], orders[1][half][step], sizes)
            for half in range(2)
        ]
        halves = [jnp.concatenate([halves[half], arrived[half]], axis=0) for half in range(2)]
    return halves + [exchange(value, CORE, CORE, sizes) for value in halves]


def spread_kernel(wide, scalars, *refs):
    sources, targets = refs[:4], refs[4:]
    core = scalars[0]
    rows, width = sources[0].shape[1:]
    for matrix in range(4):
        label = scalars[1 + matrix] & 3

        def put(source, matrix=matrix, label=label):
            for own in range(4):
                value = source[own ^ label].astype(jnp.float32)
                at = pl.ds(own * rows, rows)
                if wide:
                    targets[0][at, matrix * width : (matrix + 1) * width] = value
                elif len(targets) == 1:
                    targets[0][matrix, at] = value
                else:
                    targets[matrix][at] = value

        @pl.when(core == matrix // 2)
        def _():
            put(sources[matrix % 2])

        @pl.when(core != matrix // 2)
        def _():
            put(sources[2 + matrix % 2])


def spread(scalars, blocks, kind, name):
    _, rows, width = blocks[0].shape
    group = 4 * rows

    def source_spec(place):
        half, foreign = place % 2, place // 2

        def at(i, scalars):
            owner = scalars[0] ^ foreign
            label = jnp.where(owner == 0, scalars[1 + half], scalars[3 + half])
            return (i ^ (label >> 2), 0, 0)

        return pl.BlockSpec((4, rows, width), at)

    if kind == "wide":
        out_specs = [pl.BlockSpec((group, 4 * width), lambda i, s: (i, 0))]
        out_shape = [jax.ShapeDtypeStruct((width, 4 * width), jnp.float32)]
    elif kind == "tall":
        out_specs = [pl.BlockSpec((4, group, width), lambda i, s: (0, i, 0))]
        out_shape = [jax.ShapeDtypeStruct((4, width, width), jnp.float32)]
    else:
        out_specs = [pl.BlockSpec((group, width), lambda i, s: (i, 0))] * 4
        out_shape = [jax.ShapeDtypeStruct((width, width), jnp.float32)] * 4
    return pl.pallas_call(
        functools.partial(spread_kernel, kind == "wide"),
        grid_spec=pltpu.PrefetchScalarGridSpec(
            num_scalar_prefetch=1,
            grid=(LABELS // 4,),
            in_specs=[source_spec(place) for place in range(4)],
            out_specs=out_specs,
        ),
        out_shape=out_shape,
        compiler_params=pltpu.CompilerParams(vmem_limit_bytes=VMEM_LIMIT),
        cost_estimate=pl.CostEstimate(
            flops=0, bytes_accessed=24 * width * width, transcendentals=0
        ),
        name=name,
    )(scalars, *blocks)


def gather_embeddings(own, sizes):
    orders = gather_orders(sizes[1])
    value = own[None]
    for even_dim, odd_dim in zip(*orders, strict=True):
        value = jnp.concatenate([value, exchange(value, even_dim, odd_dim, sizes)], axis=0)
    return value, exchange(value, CORE, CORE, sizes)


def gather_places(sizes):
    orders = gather_orders(sizes[1])
    tables = []
    for order in orders:
        table = []
        for place in range(1 << len(order)):
            at = (0, 0)
            for step, dim in enumerate(order):
                if place >> step & 1:
                    at = flipped(dim, *at)
            table.append(at)
        tables.append(table)
    even, odd = (np.array(table, np.int32) for table in tables)
    batch = lax.axis_index("batch")
    core = (batch & 1).astype(jnp.int32)
    own = jnp.where(core == 0, even, odd)
    foreign = jnp.where(core == 0, odd, even) ^ np.array([[0, 1]], np.int32)
    places = jnp.concatenate([own, foreign], axis=0)
    return places[:, 0], places[:, 1] ^ batch.astype(jnp.int32)


def contrast_kernel(scale, info, other, index, own_ref, foreign_ref, pooled_ref, lengths_ref, terms_ref, grad_ref, all_ref, digits_ref, totals_ref):
    half, texts, wide = own_ref.shape
    width = pooled_ref.shape[1]
    total = all_ref.shape[1]
    query_side, batch = info[0], info[1]

    def place(i, source, offset):
        at = pl.multiple_of(index[offset + i] * texts, texts)
        all_ref[other[offset + i], pl.ds(at, texts)] = source[i, :, :width]

        @pl.when(other[offset + i] == 1)
        def _():
            digits_ref[pl.ds(at, texts)] = source[i, :, width:]

    def place_own(i, carry):
        place(i, own_ref, 0)
        place(i, foreign_ref, half)
        return carry

    lax.fori_loop(0, half, place_own, 0)

    def dots(former, latter):
        return lax.dot_general(former, latter, (((1,), (1,)), ((), ())), preferred_element_type=jnp.float32)

    tile = min(TILE, total)
    totals_ref[...] = jnp.zeros_like(totals_ref)
    for column in range(total // tile):
        latter = all_ref[1, column * tile : (column + 1) * tile]

        def add(i, carry, latter=latter, column=column):
            former = all_ref[0, pl.ds(pl.multiple_of(i * tile, tile), tile)]
            sums = jnp.sum(jnp.exp(dots(former, latter) / 0.05), axis=0, keepdims=True)
            totals_ref[:, column * tile : (column + 1) * tile] += sums
            return carry

        lax.fori_loop(0, total // tile, add, 0)
    mine = all_ref[0, pl.ds(pl.multiple_of(batch * texts, texts), texts)]
    partners = all_ref[1]
    own_digits = own_ref[0, :, width:]
    logits = dots(mine, partners) / 0.05
    exponent = jnp.exp(logits)
    row_total = jnp.sum(exponent, axis=1, keepdims=True)
    own_target = (64.0 * own_digits[:, 0:1].astype(jnp.float32) + own_digits[:, 1:2].astype(jnp.float32)).astype(jnp.int32)
    lane = lax.broadcasted_iota(jnp.int32, (8, 128), 1)
    pick = jnp.where(lane == 0, 64.0, jnp.where(lane == 1, 1.0, 0.0)).astype(jnp.bfloat16)
    all_target = dots(pick, digits_ref[...])[0:1].astype(jnp.int32)
    columns = lax.broadcasted_iota(jnp.int32, (texts, total), 1)
    rows = batch * texts + lax.broadcasted_iota(jnp.int32, (texts, total), 0)
    query_hit = (own_target == columns).astype(jnp.float32)
    doc_hit = (all_target == rows).astype(jnp.float32)
    target = jnp.where(query_side == 1, query_hit, doc_hit)
    chosen = jnp.sum(logits * target, axis=1, keepdims=True)
    terms_ref[...] = jnp.broadcast_to(jnp.log(row_total) - chosen, terms_ref.shape)
    own_low = ((exponent / row_total - target) * scale).astype(jnp.bfloat16)
    cross_low = ((exponent / totals_ref[0:1, :] - target) * scale).astype(jnp.bfloat16)
    gradient = (
        jnp.dot(own_low, partners, preferred_element_type=jnp.float32)
        + jnp.dot(cross_low, partners, preferred_element_type=jnp.float32)
    ) / 0.05
    gradient = gradient.astype(jnp.bfloat16).astype(jnp.float32)
    pooled = pooled_ref[...]
    inverse_norm = lax.rsqrt(jnp.sum(pooled * pooled, axis=1, keepdims=True) + 1e-06)
    embedding = pooled * inverse_norm
    inner = jnp.sum(gradient * embedding, axis=1, keepdims=True)
    grad_ref[...] = inverse_norm * (gradient - embedding * inner) / lengths_ref[:, 0:1]


def contrast(own, foreign, pooled, seg_length, sizes):
    half, texts, wide = own.shape
    width = pooled.shape[1]
    total = sizes[1] * texts
    other, index = gather_places(sizes)
    info = jnp.stack([lax.axis_index("stream") == 0, lax.axis_index("batch")]).astype(jnp.int32)
    lengths = jnp.broadcast_to(seg_length, (texts, 128))
    terms, gradient = pl.pallas_call(
        functools.partial(contrast_kernel, 1.0 / (2.0 * total)),
        grid_spec=pltpu.PrefetchScalarGridSpec(
            num_scalar_prefetch=3,
            grid=(1,),
            in_specs=[
                full_spec(own.shape),
                full_spec(foreign.shape),
                full_spec(pooled.shape),
                full_spec(lengths.shape),
            ],
            out_specs=[full_spec((texts, 128)), full_spec(pooled.shape)],
            scratch_shapes=[
                pltpu.VMEM((2, total, width), jnp.bfloat16),
                pltpu.VMEM((total, wide - width), jnp.bfloat16),
                pltpu.VMEM((8, total), jnp.float32),
            ],
        ),
        out_shape=[
            jax.ShapeDtypeStruct((texts, 128), jnp.float32),
            jax.ShapeDtypeStruct(pooled.shape, jnp.float32),
        ],
        compiler_params=pltpu.CompilerParams(vmem_limit_bytes=VMEM_LIMIT),
        cost_estimate=pl.CostEstimate(
            flops=2 * total * total * width, bytes_accessed=8 * total * width, transcendentals=total * total
        ),
        name="contrast",
    )(info, other, index, own, foreign, pooled, lengths)
    return terms[:, 0], gradient


def sum_vectors(vector, sizes):
    (x, y, a, b), rest = link_dims(sizes[1])
    value = vector.reshape(-1, 128)
    for even_dim, odd_dim in [(d, d) for d in [CORE, x, y, a, b] + rest]:
        value = value + exchange(value, even_dim, odd_dim, sizes)
    return value.reshape(-1)


BAND = 64
STEP = 128
WINDOW = STEP + 2 * BAND
QUERY_BIAS, VALUE_BIAS, OUTPUT_BIAS, FIRST_GAIN, FIRST_SHIFT, DOWN_BIAS, SECOND_GAIN, SECOND_SHIFT, UP_BIAS = range(9)


def dots(former, latter):
    return lax.dot_general(former, latter, (((1,), (1,)), ((), ())), preferred_element_type=jnp.float32)


def product(former, latter):
    return jnp.dot(former, latter, preferred_element_type=jnp.float32)


def transposed(former, latter):
    return lax.dot_general(former, latter, (((0,), (0,)), ((), ())), preferred_element_type=jnp.float32)


def low(values):
    return values.astype(jnp.bfloat16)


def call(kernel, name, grid, in_specs, out_specs, out_shape, scratch, flops, moved, *args):
    return pl.pallas_call(
        kernel,
        grid_spec=pltpu.PrefetchScalarGridSpec(
            num_scalar_prefetch=1, grid=grid, in_specs=in_specs, out_specs=out_specs, scratch_shapes=scratch
        ),
        out_shape=out_shape,
        compiler_params=pltpu.CompilerParams(vmem_limit_bytes=VMEM_LIMIT),
        cost_estimate=pl.CostEstimate(flops=flops, bytes_accessed=moved, transcendentals=0),
        name=name,
    )(*args)


def shaped(shape, dtype):
    return jax.ShapeDtypeStruct(shape, dtype)


def rows_spec(rows, width):
    return pl.BlockSpec((rows, width), lambda i, *_: (i, 0))


def segment_of(lengths, row, count, shape, dim):
    place = lax.broadcasted_iota(jnp.int32, shape, dim)
    total, ids = 0, jnp.zeros(shape, jnp.int32)
    for j in range(count):
        total = total + lengths[row * count + j]
        ids = ids + (place >= total).astype(jnp.int32)
    return ids


def window_start(block, span):
    return min(max(block * STEP - BAND, 0), span - WINDOW)


def fill_bias(lengths, row, count, span, bias_ref):
    down = segment_of(lengths, row, count, (span, 128), 0)
    along = segment_of(lengths, row, count, (8, span), 1)
    for block in range(span // STEP):
        start = window_start(block, span)
        same = down[block * STEP : (block + 1) * STEP, 0:1] == along[0:1, start : start + WINDOW]
        bias_ref[block] = jnp.where(same, 0.0, -1e9)


def head_masks(scale):
    lane = lax.broadcasted_iota(jnp.int32, (1, 2 * HEAD_DIM), 1)
    first = low(jnp.where(lane < HEAD_DIM, scale, 0.0))
    second = low(jnp.where(lane < HEAD_DIM, 0.0, scale))
    return first, second


def stacked(values, masks):
    return jnp.concatenate([values * masks[0], values * masks[1]], axis=0)


def merged(values):
    lane = lax.broadcasted_iota(jnp.int32, (STEP, 2 * HEAD_DIM), 1)
    return jnp.where(lane < HEAD_DIM, values[:STEP], values[STEP:])


def biased(scores, bias):
    return (scores.reshape(2, STEP, WINDOW) + bias[None]).reshape(2 * STEP, WINDOW)


def normalised(values):
    centred = values - jnp.mean(values, axis=-1, keepdims=True)
    factor = lax.rsqrt(jnp.mean(centred * centred, axis=-1, keepdims=True) + 1e-12)
    return centred * factor, factor


def norm_back(gradient, normed, factor, gain):
    inner = gradient * gain
    centred = inner - jnp.mean(inner, axis=-1, keepdims=True)
    return factor * (centred - normed * jnp.mean(inner * normed, axis=-1, keepdims=True))


def attend_kernel(count, lengths, x_ref, wq_ref, wk_ref, wv_ref, wo_ref, vec_ref, q_ref, k_ref, v_ref, ctx_ref, normed_ref, hidden_ref, aux_ref, bias_ref):
    span, width = x_ref.shape
    row = pl.program_id(0)
    x = x_ref[...]
    q_ref[...] = low(product(x, wq_ref[...]) + vec_ref[QUERY_BIAS : QUERY_BIAS + 1])
    k_ref[...] = low(product(x, wk_ref[...]))
    v_ref[...] = low(product(x, wv_ref[...]) + vec_ref[VALUE_BIAS : VALUE_BIAS + 1])
    fill_bias(lengths, row, count, span, bias_ref)
    masks = head_masks(HEAD_DIM**-0.5)
    aux_ref[...] = jnp.zeros_like(aux_ref)

    def heads(pair, carry):
        at = pl.ds(pl.multiple_of(pair * 2 * HEAD_DIM, 2 * HEAD_DIM), 2 * HEAD_DIM)
        lane = lax.broadcasted_iota(jnp.int32, (STEP, 128), 1)
        for block in range(span // STEP):
            rows = pl.ds(block * STEP, STEP)
            keys = pl.ds(window_start(block, span), WINDOW)
            scores = biased(dots(stacked(q_ref[rows, at], masks), k_ref[keys, at]), bias_ref[block])
            highest = jnp.max(scores, axis=1, keepdims=True)
            exponent = jnp.exp(scores - highest)
            total = jnp.sum(exponent, axis=1, keepdims=True)
            attention = low(exponent * (1.0 / total))
            ctx_ref[rows, at] = low(merged(product(attention, v_ref[keys, at])))
            log_total = highest + jnp.log(total)
            kept = jnp.where(lane == 2 * pair, log_total[:STEP], aux_ref[rows])
            aux_ref[rows] = jnp.where(lane == 2 * pair + 1, log_total[STEP:], kept)
        return carry

    lax.fori_loop(0, width // (2 * HEAD_DIM), heads, 0)
    attended = product(ctx_ref[...], wo_ref[...]) + vec_ref[OUTPUT_BIAS : OUTPUT_BIAS + 1]
    normed, factor = normalised(x.astype(jnp.float32) + attended)
    normed_ref[...] = normed
    hidden_ref[...] = low(normed * vec_ref[FIRST_GAIN : FIRST_GAIN + 1] + vec_ref[FIRST_SHIFT : FIRST_SHIFT + 1])
    lane = lax.broadcasted_iota(jnp.int32, (span, 128), 1)
    aux_ref[...] = jnp.where(lane == 127, factor, aux_ref[...])


def attend(lengths, x, weights, vec, row_count):
    tokens, width = x.shape
    span = tokens // row_count
    square = full_spec((width, width))
    kinds = [jnp.bfloat16] * 4 + [jnp.float32, jnp.bfloat16]
    return call(
        functools.partial(attend_kernel, lengths.size // row_count),
        "attend",
        (row_count,),
        [rows_spec(span, width)] + [square] * 4 + [full_spec(vec.shape)],
        [rows_spec(span, width)] * 6 + [rows_spec(span, 128)],
        [shaped((tokens, width), kind) for kind in kinds] + [shaped((tokens, 128), jnp.float32)],
        [pltpu.VMEM((span // STEP, STEP, WINDOW), jnp.float32)],
        8 * tokens * width * width + 4 * tokens * WINDOW * width,
        8 * width * width + 20 * tokens * width,
        lengths, x, *weights, vec,
    )


def gelu_and_slope(values):
    size = jnp.abs(values)
    part = 1.0 / (1.0 + (0.3275911 * 0.5**0.5) * size)
    bell = jnp.exp(values * values * -0.5)
    series = part * (0.5 * 0.254829592 + part * (-0.5 * 0.284496736 + part * (0.5 * 1.421413741 + part * (-0.5 * 1.453152027 + part * (0.5 * 1.061405429)))))
    tail = series * bell
    share = jnp.where(values < 0.0, tail, 1.0 - tail)
    return values * share, share + values * bell * 0.3989422804014327


def two_parts(values):
    high = low(values)
    return high, low(values - high.astype(jnp.float32))


def membership(lengths, row, count, rows, offset):
    place = lax.broadcasted_iota(jnp.int32, (count, rows), 1) + offset
    text = lax.broadcasted_iota(jnp.int32, (count, rows), 0)
    total = 0
    inside = jnp.zeros((count, rows), jnp.float32)
    for j in range(count):
        start, total = total, total + lengths[row * count + j]
        inside = jnp.where((text == j) & (place >= start) & (place < total), 1.0, inside)
    return low(inside)


def length_column(lengths, row, count):
    text = lax.broadcasted_iota(jnp.int32, (count, 128), 0)
    column = jnp.zeros((count, 128), jnp.float32)
    for j in range(count):
        column = jnp.where(text == j, lengths[row * count + j].astype(jnp.float32), column)
    return column[:, 0:1]


def feed_kernel(count, parts, lengths, normed_ref, hidden_ref, up_ref, down_ref, vec_ref, digits_ref, act_ref, slope_ref, second_ref, factor_ref, pooled_ref, package_ref):
    rows, width = normed_ref.shape
    step = pl.program_id(0)
    row, part = step // parts, step % parts
    hidden_low = hidden_ref[...]
    branch = jnp.zeros((rows, width), jnp.float32)
    for piece in range(up_ref.shape[1] // width):
        at = slice(piece * width, (piece + 1) * width)
        bias = vec_ref[UP_BIAS + piece : UP_BIAS + piece + 1]
        activation, slope = gelu_and_slope(product(hidden_low, up_ref[:, at]) + bias)
        activation = low(activation)
        act_ref[:, at] = activation
        slope_ref[:, at] = low(slope)
        branch = branch + product(activation, down_ref[at])
    hidden = normed_ref[...] * vec_ref[FIRST_GAIN : FIRST_GAIN + 1] + vec_ref[FIRST_SHIFT : FIRST_SHIFT + 1]
    normed, factor = normalised(hidden + branch + vec_ref[DOWN_BIAS : DOWN_BIAS + 1])
    second_ref[...] = normed
    factor_ref[...] = jnp.broadcast_to(factor, factor_ref.shape)
    high, rest = two_parts(normed * vec_ref[SECOND_GAIN : SECOND_GAIN + 1] + vec_ref[SECOND_SHIFT : SECOND_SHIFT + 1])
    inside = membership(lengths, row, count, rows, part * rows)
    sums = product(inside, high) + product(inside, rest)

    @pl.when(part == 0)
    def _():
        pooled_ref[...] = sums

    @pl.when(part != 0)
    def _():
        pooled_ref[...] += sums

    @pl.when(part == parts - 1)
    def _():
        pooled = pooled_ref[...] / length_column(lengths, row, count)
        pooled_ref[...] = pooled
        inverse_norm = lax.rsqrt(jnp.sum(pooled * pooled, axis=1, keepdims=True) + 1e-06)
        package_ref[:, :width] = low(pooled * inverse_norm)
        package_ref[:, width:] = digits_ref[...]


def feed(lengths, normed, hidden_low, up, down, vec, digits, row_count):
    tokens, width = normed.shape
    count = lengths.size // row_count
    rows = 256
    parts = tokens // row_count // rows
    hidden = up.shape[1]
    per_row = lambda wide: pl.BlockSpec((count, wide), lambda i, *_: (i // parts, 0))
    return call(
        functools.partial(feed_kernel, count, parts),
        "feed",
        (tokens // rows,),
        [rows_spec(rows, width), rows_spec(rows, width), full_spec(up.shape), full_spec(down.shape), full_spec(vec.shape), per_row(128)],
        [rows_spec(rows, hidden), rows_spec(rows, hidden), rows_spec(rows, width), rows_spec(rows, 128), per_row(width), per_row(width + 128)],
        [
            shaped((tokens, hidden), jnp.bfloat16),
            shaped((tokens, hidden), jnp.bfloat16),
            shaped((tokens, width), jnp.float32),
            shaped((tokens, 128), jnp.float32),
            shaped((row_count * count, width), jnp.float32),
            shaped((row_count * count, width + 128), jnp.bfloat16),
        ],
        [],
        4 * tokens * width * hidden,
        4 * width * hidden + 4 * tokens * hidden + 10 * tokens * width,
        lengths, normed, hidden_low, up, down, vec, digits,
    )


def sums_of(values):
    return jnp.sum(values, axis=0, keepdims=True)


def second_back_kernel(count, lengths, grad_ref, normed_ref, factor_ref, vec_ref, sum_ref, low_ref, totals_ref):
    span, width = normed_ref.shape
    row = pl.program_id(0)
    inside = membership(lengths, row, count, span, 0)
    high, rest = two_parts(grad_ref[...])
    result_grad = transposed(inside, high) + transposed(inside, rest)
    normed = normed_ref[...]
    second_sum = norm_back(result_grad, normed, factor_ref[:, 0:1], vec_ref[SECOND_GAIN : SECOND_GAIN + 1])
    branch_grad = low(second_sum)
    sum_ref[...] = second_sum
    low_ref[...] = branch_grad

    @pl.when(row == 0)
    def _():
        totals_ref[...] = jnp.zeros_like(totals_ref)

    totals_ref[0:1] += sums_of(branch_grad.astype(jnp.float32))
    totals_ref[1:2] += sums_of(result_grad * normed)
    totals_ref[2:3] += sums_of(result_grad)


def second_back(lengths, grad, normed, factor, vec, row_count):
    tokens, width = normed.shape
    span = tokens // row_count
    count = lengths.size // row_count
    return call(
        functools.partial(second_back_kernel, count),
        "second_norm_back",
        (row_count,),
        [rows_spec(count, width), rows_spec(span, width), rows_spec(span, 128), full_spec(vec.shape)],
        [rows_spec(span, width), rows_spec(span, width), full_spec((8, width))],
        [shaped((tokens, width), jnp.float32), shaped((tokens, width), jnp.bfloat16), shaped((8, width), jnp.float32)],
        [],
        8 * tokens * width,
        10 * tokens * width,
        lengths, grad, normed, factor, vec,
    )


def matrix_at(place, foreign, scalars):
    return 2 * (scalars[0] ^ foreign) + place


def put_rows(scalars, matrix, left, right, out_ref, group=4):
    label = scalars[1 + matrix]
    rows = out_ref.shape[2]
    for first in range(0, LABELS, group):
        piece = low(transposed(left[:, first * rows : (first + group) * rows], right))
        for own in range(group):
            out_ref[0, (first + own) ^ label] = piece[own * rows : (own + 1) * rows]


def blocks_out(width):
    rows = width // LABELS
    return pl.BlockSpec((1, LABELS, rows, width), lambda i, *_: (i, 0, 0, 0)), shaped((2, LABELS, rows, width), jnp.bfloat16)


def down_weight_kernel(foreign, scalars, act_ref, grad_ref, out_ref):
    put_rows(scalars, matrix_at(pl.program_id(0), foreign, scalars), act_ref[...], grad_ref[...], out_ref)


def down_weight(scalars, activation, grad, foreign, name):
    tokens, width = grad.shape
    spec, shape = blocks_out(width)
    return call(
        functools.partial(down_weight_kernel, foreign),
        name,
        (2,),
        [pl.BlockSpec((tokens, width), lambda i, s: (0, matrix_at(i, foreign, s))), full_spec(grad.shape)],
        spec, shape, [],
        4 * tokens * width * width,
        6 * tokens * width + 4 * width * width,
        scalars, activation, grad,
    )


def up_back_kernel(foreign, scalars, grad_ref, slope_ref, hidden_ref, up_ref, down_ref, before_ref, *refs):
    if foreign:
        out_ref, after_ref, totals_ref = refs
    else:
        normed_ref, aux_ref, vec_ref, out_ref, totals_ref, first_ref, low_ref, sums_ref, after_ref = refs
    step = pl.program_id(0)
    pre_grad = low(dots(grad_ref[...], down_ref[...]) * slope_ref[...].astype(jnp.float32))
    totals_ref[0] = jnp.broadcast_to(sums_of(pre_grad.astype(jnp.float32)), totals_ref.shape[1:])
    put_rows(scalars, matrix_at(step, foreign, scalars), hidden_ref[...], pre_grad, out_ref)

    @pl.when(step == 0)
    def _():
        after_ref[...] = before_ref[...] + dots(pre_grad, up_ref[...])

    @pl.when(step != 0)
    def _():
        after_ref[...] += dots(pre_grad, up_ref[...])

    if not foreign:

        @pl.when(step == 1)
        def _():
            hidden_grad, normed = after_ref[...], normed_ref[...]
            first_sum = norm_back(hidden_grad, normed, aux_ref[:, 127:128], vec_ref[FIRST_GAIN : FIRST_GAIN + 1])
            attended_grad = low(first_sum)
            first_ref[...] = first_sum
            low_ref[...] = attended_grad
            sums_ref[...] = jnp.zeros_like(sums_ref)
            sums_ref[0:1] = sums_of(attended_grad.astype(jnp.float32))
            sums_ref[1:2] = sums_of(hidden_grad * normed)
            sums_ref[2:3] = sums_of(hidden_grad)


def up_back(scalars, grad, slope, hidden_low, up, down, before, foreign, name, rest=()):
    tokens, width = grad.shape
    spec, shape = blocks_out(width)
    column = lambda rows: pl.BlockSpec((rows, width), lambda i, s: (0, matrix_at(i, foreign, s)))
    totals = pl.BlockSpec((1, 8, width), lambda i, *_: (i, 0, 0)), shaped((2, 8, width), jnp.float32)
    wide = full_spec((tokens, width))
    in_specs = [wide, column(tokens), wide, column(width), pl.BlockSpec((width, width), lambda i, s: (matrix_at(i, foreign, s), 0)), wide]
    if foreign:
        outs = [(spec, shape), (wide, shaped((tokens, width), jnp.float32)), totals]
        scratch = []
    else:
        in_specs += [wide, full_spec((tokens, 128)), full_spec(rest[2].shape)]
        outs = [(spec, shape), totals, (wide, shaped((tokens, width), jnp.float32)), (wide, shaped((tokens, width), jnp.bfloat16)), (full_spec((8, width)), shaped((8, width), jnp.float32))]
        scratch = [pltpu.VMEM((tokens, width), jnp.float32)]
    return call(
        functools.partial(up_back_kernel, foreign),
        name,
        (2,),
        in_specs, [o[0] for o in outs], [o[1] for o in outs], scratch,
        12 * tokens * width * width,
        16 * tokens * width + 8 * width * width,
        scalars, grad, slope, hidden_low, up, down, before, *rest,
    )


def attend_back_kernel(count, lengths, q_ref, k_ref, v_ref, grad_ref, wo_ref, aux_ref, out_ref, totals_ref, bias_ref, ctx_ref, dk_ref, dv_ref):
    span, width = q_ref.shape
    row = pl.program_id(0)
    grad = grad_ref[...]
    ctx_ref[...] = low(dots(grad, wo_ref[...]))
    out_ref[3] = grad
    fill_bias(lengths, row, count, span, bias_ref)
    scale = HEAD_DIM**-0.5
    scaled, plain = head_masks(scale), head_masks(1.0)
    dk_ref[...] = jnp.zeros_like(dk_ref)
    dv_ref[...] = jnp.zeros_like(dv_ref)

    def heads(pair, carry):
        at = pl.ds(pl.multiple_of(pair * 2 * HEAD_DIM, 2 * HEAD_DIM), 2 * HEAD_DIM)
        lane = lax.broadcasted_iota(jnp.int32, (STEP, 128), 1)
        for block in range(span // STEP):
            rows = pl.ds(block * STEP, STEP)
            keys = pl.ds(window_start(block, span), WINDOW)
            aux = aux_ref[rows]
            log_total = jnp.concatenate(
                [jnp.sum(jnp.where(lane == 2 * pair + half, aux, 0.0), axis=1, keepdims=True) for half in range(2)], axis=0
            )
            queries = stacked(q_ref[rows, at], scaled)
            context_grad = stacked(ctx_ref[rows, at], plain)
            key_rows, value_rows = k_ref[keys, at], v_ref[keys, at]
            attention = jnp.exp(biased(dots(queries, key_rows), bias_ref[block]) - log_total)
            prob_grad = dots(context_grad, value_rows)
            inner = jnp.sum(attention * prob_grad, axis=1, keepdims=True)
            score_grad = low(attention * (prob_grad - inner))
            out_ref[0, rows, at] = low(merged(product(score_grad, key_rows)) * scale)
            dk_ref[keys, at] += transposed(score_grad, queries)
            dv_ref[keys, at] += transposed(low(attention), context_grad)
        return carry

    lax.fori_loop(0, width // (2 * HEAD_DIM), heads, 0)
    out_ref[1] = low(dk_ref[...])
    out_ref[2] = low(dv_ref[...])

    @pl.when(row == 0)
    def _():
        totals_ref[...] = jnp.zeros_like(totals_ref)

    totals_ref[0:1] += sums_of(out_ref[0].astype(jnp.float32))
    totals_ref[1:2] += sums_of(out_ref[2].astype(jnp.float32))


def attend_back(lengths, q, k, v, grad, wo, aux, row_count):
    tokens, width = q.shape
    span = tokens // row_count
    return call(
        functools.partial(attend_back_kernel, lengths.size // row_count),
        "attend_back",
        (row_count,),
        [rows_spec(span, width)] * 4 + [full_spec(wo.shape), rows_spec(span, 128)],
        [pl.BlockSpec((4, span, width), lambda i, *_: (0, i, 0)), full_spec((8, width))],
        [shaped((4, tokens, width), jnp.bfloat16), shaped((8, width), jnp.float32)],
        [
            pltpu.VMEM((span // STEP, STEP, WINDOW), jnp.float32),
            pltpu.VMEM((span, width), jnp.bfloat16),
            pltpu.VMEM((span, width), jnp.float32),
            pltpu.VMEM((span, width), jnp.float32),
        ],
        2 * tokens * width * width + 10 * tokens * WINDOW * width,
        16 * tokens * width + 2 * width * width,
        lengths, q, k, v, grad, wo, aux,
    )


def mixed_weight_kernel(foreign, scalars, x_ref, ctx_ref, grad_ref, out_ref):
    matrix = matrix_at(pl.program_id(0), foreign, scalars)

    @pl.when(matrix != 3)
    def _():
        put_rows(scalars, matrix, x_ref[...], grad_ref[0], out_ref)

    @pl.when(matrix == 3)
    def _():
        put_rows(scalars, matrix, ctx_ref[...], grad_ref[0], out_ref)


def mixed_weight(scalars, x, context, grads, foreign, name):
    tokens, width = x.shape
    spec, shape = blocks_out(width)
    return call(
        functools.partial(mixed_weight_kernel, foreign),
        name,
        (2,),
        [full_spec(x.shape), full_spec(x.shape), pl.BlockSpec((1, tokens, width), lambda i, s: (matrix_at(i, foreign, s), 0, 0))],
        spec, shape, [],
        4 * tokens * width * width,
        8 * tokens * width + 4 * width * width,
        scalars, x, context, grads,
    )


def input_kernel(scalars, first_ref, grad_ref, wq_ref, wk_ref, wv_ref, out_ref):
    out_ref[...] = first_ref[...] + dots(grad_ref[0], wq_ref[...]) + dots(grad_ref[1], wk_ref[...]) + dots(grad_ref[2], wv_ref[...])


def input_back(scalars, first_sum, grads, weights):
    tokens, width = first_sum.shape
    rows = 256
    return call(
        input_kernel,
        "input_grad",
        (tokens // rows,),
        [rows_spec(rows, width), pl.BlockSpec((3, rows, width), lambda i, *_: (0, i, 0))] + [full_spec((width, width))] * 3,
        rows_spec(rows, width),
        shaped((tokens, width), jnp.float32),
        [],
        6 * tokens * width * width,
        14 * tokens * width + 6 * width * width,
        scalars, first_sum, grads, *weights,
    )


def local(
    inputs,
    lengths,
    positives,
    query_weight,
    query_bias,
    key_weight,
    value_weight,
    value_bias,
    output_weight,
    output_bias,
    first_gain,
    first_shift,
    up_weight,
    up_bias,
    down_weight_,
    down_bias,
    second_gain,
    second_shift,
):
    row_count, row_span, width = inputs.shape[1:]
    seg_count = lengths.shape[2]
    tokens = row_count * row_span
    hidden_width = up_weight.shape[1]
    sizes = (lax.axis_size("stream"), lax.axis_size("batch"))
    x = inputs.reshape(tokens, width)
    flat_lengths = lengths.reshape(row_count * seg_count)
    vec = jnp.concatenate(
        [query_bias, value_bias, output_bias, first_gain, first_shift, down_bias, second_gain, second_shift, up_bias]
    )
    vec = vec.astype(jnp.float32).reshape(-1, width)
    digits = jnp.stack([positives >> 6, positives & 63], axis=1).astype(jnp.bfloat16)
    digits = jnp.pad(digits, ((0, 0), (0, 126)))
    scalars = block_scalars(sizes)
    q, k, v, context, first_normed, hidden_low, aux = attend(
        flat_lengths, x, (query_weight, key_weight, value_weight, output_weight), vec, row_count
    )
    activation, slope, second_normed, second_factor, pooled, package = feed(
        flat_lengths, first_normed, hidden_low, up_weight, down_weight_, vec, digits, row_count
    )
    own, foreign = gather_embeddings(package, sizes)
    seg_length = lengths.reshape(row_count * seg_count, 1).astype(jnp.float32)
    contrast_terms, pooled_grad = contrast(own, foreign, pooled, seg_length, sizes)
    second_sum, branch_grad, second_totals = second_back(
        flat_lengths, pooled_grad, second_normed, second_factor, vec, row_count
    )
    down_send = down_weight(scalars, activation, branch_grad, 1, "down_weight_send")
    down_keep = down_weight(scalars, activation, branch_grad, 0, "down_weight_keep")
    down_share = reduce_blocks(down_send, down_keep, sizes)
    up_send, partial_grad, up_totals_send = up_back(
        scalars, branch_grad, slope, hidden_low, up_weight, down_weight_, second_sum, 1, "up_back_send"
    )
    up_keep, up_totals_keep, first_sum, attended_grad, first_totals = up_back(
        scalars, branch_grad, slope, hidden_low, up_weight, down_weight_, partial_grad, 0, "up_back_keep",
        (first_normed, aux, vec),
    )
    up_share = reduce_blocks(up_send, up_keep, sizes)
    grads, attend_totals = attend_back(flat_lengths, q, k, v, attended_grad, output_weight, aux, row_count)
    mixed_send = mixed_weight(scalars, x, context, grads, 1, "mixed_weight_send")
    mixed_keep = mixed_weight(scalars, x, context, grads, 0, "mixed_weight_keep")
    mixed_share = reduce_blocks(mixed_send, mixed_keep, sizes)
    input_grad = input_back(scalars, first_sum, grads, (query_weight, key_weight, value_weight))
    (down_total,) = spread(scalars, gather_blocks(down_share, sizes), "tall", "down_spread")
    (up_total,) = spread(scalars, gather_blocks(up_share, sizes), "wide", "up_spread")
    query_total, key_total, value_total, output_total = spread(
        scalars, gather_blocks(mixed_share, sizes), "separate", "mixed_spread"
    )
    up_totals = jnp.where(
        scalars[0] == 0,
        jnp.concatenate([up_totals_keep, up_totals_send])[:, 0],
        jnp.concatenate([up_totals_send, up_totals_keep])[:, 0],
    )
    vectors = jnp.concatenate([attend_totals[0:2], first_totals[0:3], second_totals[0:3], up_totals])
    summed = sum_vectors(vectors.reshape(-1), sizes).reshape(vectors.shape)
    return (
        contrast_terms.reshape(1, row_count * seg_count),
        input_grad.reshape(1, row_count, row_span, width),
        query_total,
        summed[0],
        key_total,
        value_total,
        summed[1],
        output_total,
        summed[2],
        summed[3],
        summed[4],
        up_total,
        summed[8:].reshape(hidden_width),
        down_total.reshape(hidden_width, width),
        summed[5],
        summed[6],
        summed[7],
    )


def solution(mesh):
    return jax.shard_map(
        local,
        mesh=mesh,
        in_specs=(
            P("stream", "batch", None, None),
            P("stream", "batch", None),
            P("batch"),
            P(),
            P(),
            P(),
            P(),
            P(),
            P(),
            P(),
            P(),
            P(),
            P(),
            P(),
            P(),
            P(),
            P(),
            P(),
        ),
        out_specs=(
            P("stream", "batch"),
            P("stream", "batch", None, None),
            P(),
            P(),
            P(),
            P(),
            P(),
            P(),
            P(),
            P(),
            P(),
            P(),
            P(),
            P(),
            P(),
            P(),
            P(),
        ),
        check_vma=False,
    )
```

```python
import functools

import jax
import jax.numpy as jnp
import numpy as np
from jax import lax
from jax.experimental import pallas as pl
from jax.experimental.pallas import tpu as pltpu
from jax.sharding import PartitionSpec as P

HEAD_DIM = 64
MIB = 2**20
TILE = 512
LABELS = 16
THIRDS = 3
BOTH = ("stream", "batch")


def link_dims(batch_size):
    bits = batch_size.bit_length() - 1
    main = [("stream", 1), ("batch", 2), ("batch", 1 << (bits - 2)), ("batch", 3 << (bits - 2))]
    rest = [("batch", 1 << j) for j in range(2, bits - 2)]
    return main, rest


def coordinate(dim, stream, batch, batch_size):
    bits = batch_size.bit_length() - 1
    if dim[0] == "stream":
        return stream
    mask = dim[1]
    top = (batch >> (bits - 1)) & 1
    if mask == 3 << (bits - 2):
        return top
    if mask == 1 << (bits - 2):
        return ((batch >> (bits - 2)) & 1) ^ top
    return (batch >> (mask.bit_length() - 1)) & 1


def flipped(dim, stream, batch):
    return (stream ^ 1, batch) if dim[0] == "stream" else (stream, batch ^ dim[1])


def exchange(array, even_dim, sizes, odd_dim=None):
    odd_dim = odd_dim or even_dim
    pairs = []
    for stream in range(sizes[0]):
        for batch in range(sizes[1]):
            other = flipped(odd_dim if batch & 1 else even_dim, stream, batch)
            pairs.append((stream * sizes[1] + batch, other[0] * sizes[1] + other[1]))
    return lax.ppermute(array, BOTH, pairs)


CORE = ("batch", 1)


def halving_orders(batch_size):
    (x, y, a, b), rest = link_dims(batch_size)
    return ((x, y, a, b), (y, a, x, b), (a, x, y, b)), rest


def gather_orders(batch_size):
    (x, y, a, b), rest = link_dims(batch_size)
    return tuple(rest) + (b, a, x, y), tuple(rest) + (b, x, y, a)


def labels_of(stream, batch, batch_size):
    labels = []
    for order in halving_orders(batch_size)[0]:
        label = 0
        for dim in order:
            label = label * 2 + coordinate(dim, stream, batch, batch_size)
        labels.append(label)
    return labels


def place_at(order_even, order_odd, place, numbers):
    stream, batch = numbers[0], numbers[1]
    core = batch & 1
    for step, (even_dim, odd_dim) in enumerate(zip(order_even, order_odd, strict=True)):
        bit = (place >> step) & 1
        even = (bit, 0) if even_dim[0] == "stream" else (0, bit * even_dim[1])
        odd = (bit, 0) if odd_dim[0] == "stream" else (0, bit * odd_dim[1])
        stream = stream ^ jnp.where(core == 0, even[0], odd[0])
        batch = batch ^ jnp.where(core == 0, even[1], odd[1])
    return stream, batch


def full_spec(shape):
    return pl.BlockSpec(shape, lambda *_: (0,) * len(shape))


def added(former, latter):
    return (former.astype(jnp.float32) + latter.astype(jnp.float32)).astype(jnp.bfloat16)


def split(value):
    half = value.shape[0] // 2
    return value[half:], value[:half]


def halve(values, step, sizes):
    orders, _ = halving_orders(sizes[1])
    parts = [split(value) for value in values]
    arrived = [exchange(parts[i][0], orders[i][step], sizes) for i in range(THIRDS)]
    return [part[1] for part in parts], arrived


def halve_and_gather(values, step, gathered, back, sizes, vector=None):
    orders, _ = halving_orders(sizes[1])
    parts = [split(value) for value in values]
    arrived, fresh = [None] * THIRDS, [None] * THIRDS
    for i in range(THIRDS):
        dim = orders[i][step]
        j = [order[back] for order in orders].index(dim)
        send, rows = parts[i][0], parts[i][0].shape[1]
        message = [send, gathered[j].reshape(-1, rows, gathered[j].shape[2])]
        if vector is not None and i == 0:
            block, own = coded(vector)
            message.append(block)
        reply = exchange(jnp.concatenate(message, axis=0), dim, sizes)
        if vector is not None and i == 0:
            vector = own + decoded(reply[-1])
            reply = reply[:-1]
        arrived[i] = reply[: send.shape[0]]
        fresh[j] = reply[send.shape[0] :].reshape(gathered[j].shape)
    return [part[1] for part in parts], arrived, fresh, vector


def thirds_of(share):
    rows = share.shape[1] // THIRDS
    return [share[:, i * rows : (i + 1) * rows] for i in range(THIRDS)]


def all_joined(former, latter):
    return [jnp.concatenate([former[i], latter[i]], axis=0) for i in range(THIRDS)]


def all_added(kept, arrived):
    return [added(former, latter) for former, latter in zip(kept, arrived, strict=True)]


def spread_kernel(kind, batch_size, numbers, *refs):
    sources, targets = refs[: 2 * THIRDS], refs[2 * THIRDS :]
    core = numbers[1] & 1
    labels = labels_of(numbers[0], numbers[1], batch_size)
    _, rows, third = sources[0].shape
    rows = rows // 2
    for matrix in range(4):

        def put(first, matrix=matrix):
            for part in range(THIRDS):
                for own in range(4):
                    value = sources[first + part][own ^ (labels[part] & 3), (matrix % 2) * rows : (matrix % 2 + 1) * rows]
                    value = value.astype(jnp.float32)
                    at, columns = slice(own * rows, (own + 1) * rows), slice(part * third, (part + 1) * third)
                    if kind == "tall":
                        targets[0][matrix, at, columns] = value
                    elif kind == "wide":
                        start = (matrix * THIRDS + part) * third
                        targets[0][at, start : start + third] = value
                    else:
                        targets[matrix][at, columns] = value

        @pl.when(core == matrix // 2)
        def _():
            put(0)

        @pl.when(core != matrix // 2)
        def _():
            put(THIRDS)


def spread(numbers, blocks, chunk, kind, name, sizes, **waits):
    third = blocks[0].shape[2]
    width = THIRDS * third
    rows = 2 * width // LABELS
    group = 2 * rows

    def source_spec(part):
        def at(i, numbers):
            return (i ^ (labels_of(numbers[0], numbers[1], sizes[1])[part] >> 2), chunk, 0)

        return pl.BlockSpec((4, rows, third), at)

    if kind == "tall":
        specs = [pl.BlockSpec((4, group, width), lambda i, *_: (0, i, 0))]
        shapes = [shaped((4, width, width), jnp.float32)]
    elif kind == "wide":
        specs = [pl.BlockSpec((group, 4 * width), lambda i, *_: (i, 0))]
        shapes = [shaped((width, 4 * width), jnp.float32)]
    else:
        specs = [pl.BlockSpec((group, width), lambda i, *_: (i, 0))] * 4
        shapes = [shaped((width, width), jnp.float32)] * 4
    return call(
        functools.partial(spread_kernel, kind, sizes[1]),
        name,
        (LABELS // 4,),
        [source_spec(part % THIRDS) for part in range(2 * THIRDS)],
        specs, shapes, [],
        0,
        24 * width * width,
        (numbers,), *blocks, **waits,
    )


def gather_embeddings(own, sizes):
    orders = gather_orders(sizes[1])
    value = own[None]
    for even_dim, odd_dim in zip(*orders, strict=True):
        value = jnp.concatenate([value, exchange(value, even_dim, sizes, odd_dim)], axis=0)
    return value, exchange(value, CORE, sizes)


BAND = 64
STEP = 128
WINDOW = STEP + 2 * BAND
QUERY_BIAS, VALUE_BIAS, OUTPUT_BIAS, FIRST_GAIN, FIRST_SHIFT, DOWN_BIAS, SECOND_GAIN, SECOND_SHIFT, UP_BIAS = range(9)


def dots(former, latter):
    return lax.dot_general(former, latter, (((1,), (1,)), ((), ())), preferred_element_type=jnp.float32)


def product(former, latter):
    return jnp.dot(former, latter, preferred_element_type=jnp.float32)


def transposed(former, latter):
    return lax.dot_general(former, latter, (((0,), (0,)), ((), ())), preferred_element_type=jnp.float32)


def low(values):
    return values.astype(jnp.bfloat16)


def call(kernel, name, grid, in_specs, out_specs, out_shape, scratch, flops, moved, scalars, *args, after=(), carry=(), limit=16):
    taken, given = len(scalars) + len(in_specs), len(out_specs)
    waits = len(after) + len(carry)

    def run(*refs):
        kernel(*refs[:taken], *refs[taken + waits : taken + waits + given], *refs[taken + waits + given + len(carry) :])

    anywhere = pl.BlockSpec(memory_space=pl.ANY)
    return pl.pallas_call(
        run,
        grid_spec=pltpu.PrefetchScalarGridSpec(
            num_scalar_prefetch=len(scalars),
            grid=grid,
            in_specs=list(in_specs) + [anywhere] * waits,
            out_specs=list(out_specs) + [anywhere] * len(carry),
            scratch_shapes=scratch,
        ),
        out_shape=list(out_shape) + [shaped(value.shape, value.dtype) for value in carry],
        input_output_aliases={taken + len(after) + i: given + i for i in range(len(carry))},
        compiler_params=pltpu.CompilerParams(vmem_limit_bytes=limit * MIB),
        cost_estimate=pl.CostEstimate(flops=flops, bytes_accessed=moved, transcendentals=0),
        name=name,
    )(*scalars, *args, *after, *carry)


def whole(kernel, name, scalars, args, outs, scratch, flops, after=(), carry=(), far=(), far_outs=(), limit=12):
    taken, given = len(scalars) + len(args), len(outs)
    waits = len(after) + len(carry)

    def run(*refs):
        kernel(*refs[:taken], *refs[taken + waits : taken + waits + given], *refs[taken + waits + given + len(carry) :])

    near, remote = pl.BlockSpec(memory_space=pltpu.VMEM), pl.BlockSpec(memory_space=pltpu.HBM)
    anywhere = pl.BlockSpec(memory_space=pl.ANY)
    moved = sum(a.size * a.dtype.itemsize for a in args) + sum(o.size * o.dtype.itemsize for o in outs)
    args = [pltpu.with_memory_space_constraint(a, pltpu.HBM) if i in far else a for i, a in enumerate(args)]
    out_shape = [pltpu.HBM(o.shape, o.dtype) if i in far_outs else o for i, o in enumerate(outs)]
    return pl.pallas_call(
        run,
        in_specs=[pl.BlockSpec(memory_space=pltpu.SMEM)] * len(scalars)
        + [remote if i in far else near for i in range(len(args))]
        + [anywhere] * waits,
        out_specs=[remote if i in far_outs else near for i in range(given)] + [anywhere] * len(carry),
        out_shape=out_shape + [shaped(value.shape, value.dtype) for value in carry],
        scratch_shapes=scratch,
        input_output_aliases={taken + len(after) + i: given + i for i in range(len(carry))},
        compiler_params=pltpu.CompilerParams(vmem_limit_bytes=limit * MIB),
        cost_estimate=pl.CostEstimate(flops=flops, bytes_accessed=moved, transcendentals=0),
        name=name,
    )(*scalars, *args, *after, *carry)


def shaped(shape, dtype):
    return jax.ShapeDtypeStruct(shape, dtype)


def rows_spec(rows, width):
    return pl.BlockSpec((rows, width), lambda i, *_: (i, 0))


def segment_of(lengths, row, count, shape, dim):
    place = lax.broadcasted_iota(jnp.int32, shape, dim)
    total, ids = 0, jnp.zeros(shape, jnp.int32)
    for j in range(count):
        total = total + lengths[row, j]
        ids = ids + (place >= total).astype(jnp.int32)
    return ids


def window_start(block, span):
    return min(max(block * STEP - BAND, 0), span - WINDOW)


def fill_bias(lengths, row, count, span, bias_ref, first=0):
    down = segment_of(lengths, row, count, (span, 128), 0)
    along = segment_of(lengths, row, count, (8, span), 1)
    for block in range(span // STEP):
        start = window_start(block, span)
        same = down[block * STEP : (block + 1) * STEP, 0:1] == along[0:1, start : start + WINDOW]
        bias_ref[first + block] = jnp.where(same, 0.0, -1e9)


def head_masks(scale):
    lane = lax.broadcasted_iota(jnp.int32, (1, 2 * HEAD_DIM), 1)
    first = low(jnp.where(lane < HEAD_DIM, scale, 0.0))
    second = low(jnp.where(lane < HEAD_DIM, 0.0, scale))
    return first, second


def stacked(values, masks):
    return jnp.concatenate([values * masks[0], values * masks[1]], axis=0)


def merged(values):
    lane = lax.broadcasted_iota(jnp.int32, (STEP, 2 * HEAD_DIM), 1)
    return jnp.where(lane < HEAD_DIM, values[:STEP], values[STEP:])


def biased(scores, bias):
    return (scores.reshape(2, STEP, WINDOW) + bias[None]).reshape(2 * STEP, WINDOW)


def normalised(values):
    centred = values - jnp.mean(values, axis=-1, keepdims=True)
    factor = lax.rsqrt(jnp.mean(centred * centred, axis=-1, keepdims=True) + 1e-12)
    return centred * factor, factor


def norm_back(gradient, normed, factor, gain):
    inner = gradient * gain
    centred = inner - jnp.mean(inner, axis=-1, keepdims=True)
    return factor * (centred - normed * jnp.mean(inner * normed, axis=-1, keepdims=True))


def contrast_kernel(scale, sizes, numbers, lengths, own_ref, foreign_ref, pooled_ref, terms_ref, grad_ref, all_ref, digits_ref, totals_ref):
    half, texts, wide = own_ref.shape
    width = pooled_ref.shape[1]
    total = all_ref.shape[1]
    stream, batch = numbers[0], numbers[1]
    orders = gather_orders(sizes[1])

    def place(source, from_stream, from_batch, i):
        at = pl.multiple_of(from_batch * texts, texts)
        other = from_stream ^ stream
        all_ref[other, pl.ds(at, texts)] = source[i, :, :width]

        @pl.when(other == 1)
        def _():
            digits_ref[pl.ds(at, texts)] = source[i, :, width:]

    def place_both(i, carry):
        place(own_ref, *place_at(*orders, i, (stream, batch)), i)
        place(foreign_ref, *place_at(*orders, i, (stream, batch ^ 1)), i)
        return carry

    lax.fori_loop(0, half, place_both, 0)

    tile = min(TILE, total)
    totals_ref[...] = jnp.zeros_like(totals_ref)
    for column in range(total // tile):
        latter = all_ref[1, column * tile : (column + 1) * tile]

        def add(i, carry, latter=latter, column=column):
            former = all_ref[0, pl.ds(pl.multiple_of(i * tile, tile), tile)]
            sums = jnp.sum(jnp.exp(dots(former, latter) / 0.05), axis=0, keepdims=True)
            totals_ref[:, column * tile : (column + 1) * tile] += sums
            return carry

        lax.fori_loop(0, total // tile, add, 0)
    mine = all_ref[0, pl.ds(pl.multiple_of(batch * texts, texts), texts)]
    partners = all_ref[1]
    own_digits = own_ref[0, :, width:]
    logits = dots(mine, partners) / 0.05
    exponent = jnp.exp(logits)
    row_total = jnp.sum(exponent, axis=1, keepdims=True)
    own_target = (64.0 * own_digits[:, 0:1].astype(jnp.float32) + own_digits[:, 1:2].astype(jnp.float32)).astype(jnp.int32)
    lane = lax.broadcasted_iota(jnp.int32, (8, 128), 1)
    pick = jnp.where(lane == 0, 64.0, jnp.where(lane == 1, 1.0, 0.0)).astype(jnp.bfloat16)
    all_target = dots(pick, digits_ref[...])[0:1].astype(jnp.int32)
    columns = lax.broadcasted_iota(jnp.int32, (texts, total), 1)
    rows = batch * texts + lax.broadcasted_iota(jnp.int32, (texts, total), 0)
    query_hit = (own_target == columns).astype(jnp.float32)
    doc_hit = (all_target == rows).astype(jnp.float32)
    target = jnp.where(stream == 0, query_hit, doc_hit)
    chosen = jnp.sum(logits * target, axis=1, keepdims=True)
    terms_ref[...] = jnp.broadcast_to(jnp.log(row_total) - chosen, terms_ref.shape)
    own_low = ((exponent / row_total - target) * scale).astype(jnp.bfloat16)
    cross_low = ((exponent / totals_ref[0:1, :] - target) * scale).astype(jnp.bfloat16)
    gradient = (
        jnp.dot(own_low, partners, preferred_element_type=jnp.float32)
        + jnp.dot(cross_low, partners, preferred_element_type=jnp.float32)
    ) / 0.05
    gradient = gradient.astype(jnp.bfloat16).astype(jnp.float32)
    pooled = pooled_ref[...]
    inverse_norm = lax.rsqrt(jnp.sum(pooled * pooled, axis=1, keepdims=True) + 1e-06)
    embedding = pooled * inverse_norm
    inner = jnp.sum(gradient * embedding, axis=1, keepdims=True)
    count = texts // lengths.shape[0]
    divisor = jnp.concatenate([length_column(lengths, row, count) for row in range(lengths.shape[0])], axis=0)
    grad_ref[...] = inverse_norm * (gradient - embedding * inner) / divisor


def contrast(numbers, lengths, own, foreign, pooled, sizes):
    _, texts, wide = own.shape
    width = pooled.shape[1]
    total = sizes[1] * texts
    terms, gradient = whole(
        functools.partial(contrast_kernel, 1.0 / (2.0 * total), sizes),
        "contrast",
        (numbers, lengths),
        (own, foreign, pooled),
        [shaped((texts, 128), jnp.float32), shaped(pooled.shape, jnp.float32)],
        [
            pltpu.VMEM((2, total, width), jnp.bfloat16),
            pltpu.VMEM((total, wide - width), jnp.bfloat16),
            pltpu.VMEM((8, total), jnp.float32),
        ],
        2 * total * total * width,
        limit=max(12, 8 + total * width // 2**16),
    )
    return terms[:, 0], gradient


def attend_kernel(count, lengths, x_in, wq_in, wk_in, wv_in, wo_in, *refs):
    vectors_in, refs = refs[:9], refs[9:]
    q_out, k_out, v_out, ctx_out, aux_out, vec_ref, normed_ref, hidden_ref = refs[:8]
    x_ref, w_ref, wide_ref, q_ref, k_ref, v_ref, ctx_ref, aux_ref, bias_ref, sems = refs[8:]
    tokens, width = x_ref.shape
    row_count = lengths.shape[0]
    span = tokens // row_count
    places, at = [], 0
    for vector in vectors_in:
        places.append(at)
        at += vector.shape[0]
    loads = [pltpu.make_async_copy(x_in, x_ref, sems.at[0]), pltpu.make_async_copy(wq_in, w_ref.at[0], sems.at[1])]
    small = [
        pltpu.make_async_copy(vector, wide_ref.at[pl.ds(place, vector.shape[0])], sems.at[5 + i])
        for i, (vector, place) in enumerate(zip(vectors_in, places, strict=True))
    ]
    loads += [pltpu.make_async_copy(w, w_ref.at[i], sems.at[1 + i]) for i, w in ((1, wk_in), (2, wv_in), (3, wo_in))]
    for copy in loads[:2] + small + loads[2:]:
        copy.start()
    for row in range(row_count):
        fill_bias(lengths, row, count, span, bias_ref, row * (span // STEP))
    for copy in small:
        copy.wait()
    flat = wide_ref[...].astype(jnp.float32)
    for row in range(vec_ref.shape[0]):
        vec_ref[row : row + 1] = flat[row * width : (row + 1) * width].reshape(1, width)
    loads[0].wait()
    stores = [
        pltpu.make_async_copy(ref, out, sems.at[14 + i])
        for i, (ref, out) in enumerate(
            ((q_ref, q_out), (k_ref, k_out), (v_ref, v_out), (ctx_ref, ctx_out), (aux_ref, aux_out))
        )
    ]
    for i, (ref, bias) in enumerate(((q_ref, QUERY_BIAS), (k_ref, None), (v_ref, VALUE_BIAS))):
        loads[1 + i].wait()
        for row in range(row_count):
            rows = slice(row * span, (row + 1) * span)
            values = product(x_ref[rows], w_ref[i])
            ref[rows] = low(values if bias is None else values + vec_ref[bias : bias + 1])
        stores[i].start()
    masks = head_masks(HEAD_DIM**-0.5)
    aux_ref[...] = jnp.zeros_like(aux_ref)
    pairs = width // (2 * HEAD_DIM)

    def heads(step, carry):
        row, pair = step // pairs, step % pairs
        at = pl.ds(pl.multiple_of(pair * 2 * HEAD_DIM, 2 * HEAD_DIM), 2 * HEAD_DIM)
        lane = lax.broadcasted_iota(jnp.int32, (STEP, 128), 1)
        for block in range(span // STEP):
            rows = pl.ds(pl.multiple_of(row * span + block * STEP, STEP), STEP)
            keys = pl.ds(pl.multiple_of(row * span + window_start(block, span), BAND), WINDOW)
            bias = bias_ref[row * (span // STEP) + block]
            scores = biased(dots(stacked(q_ref[rows, at], masks), k_ref[keys, at]), bias)
            highest = jnp.max(scores, axis=1, keepdims=True)
            exponent = jnp.exp(scores - highest)
            total = jnp.sum(exponent, axis=1, keepdims=True)
            attention = low(exponent * (1.0 / total))
            ctx_ref[rows, at] = low(merged(product(attention, v_ref[keys, at])))
            log_total = highest + jnp.log(total)
            kept = jnp.where(lane == 2 * pair, log_total[:STEP], aux_ref[rows])
            aux_ref[rows] = jnp.where(lane == 2 * pair + 1, log_total[STEP:], kept)
        return carry

    lax.fori_loop(0, row_count * pairs, heads, 0)
    stores[3].start()
    loads[4].wait()
    for row in range(row_count):
        rows = slice(row * span, (row + 1) * span)
        attended = product(ctx_ref[rows], w_ref[3]) + vec_ref[OUTPUT_BIAS : OUTPUT_BIAS + 1]
        normed, factor = normalised(x_ref[rows].astype(jnp.float32) + attended)
        normed_ref[rows] = normed
        hidden_ref[rows] = low(normed * vec_ref[FIRST_GAIN : FIRST_GAIN + 1] + vec_ref[FIRST_SHIFT : FIRST_SHIFT + 1])
        lane = lax.broadcasted_iota(jnp.int32, (span, 128), 1)
        aux_ref[rows] = jnp.where(lane == 127, factor, aux_ref[rows])
    stores[4].start()
    for copy in stores:
        copy.wait()


def attend(lengths, x, weights, vectors):
    tokens, width = x.shape
    row_count = lengths.shape[0]
    span = tokens // row_count
    vector_rows = sum(vector.shape[0] for vector in vectors) // width
    square = shaped((tokens, width), jnp.bfloat16)
    token_scratch = pltpu.VMEM((tokens, width), jnp.bfloat16)
    return whole(
        functools.partial(attend_kernel, lengths.shape[1]),
        "attend",
        (lengths,),
        (x, *weights, *vectors),
        [square] * 4
        + [
            shaped((tokens, 128), jnp.float32),
            shaped((vector_rows, width), jnp.float32),
            shaped((tokens, width), jnp.float32),
            square,
        ],
        [token_scratch, pltpu.VMEM((4, width, width), jnp.bfloat16), pltpu.VMEM((vector_rows * width,), jnp.bfloat16)]
        + [token_scratch] * 4
        + [pltpu.VMEM((tokens, 128), jnp.float32)]
        + [pltpu.VMEM((row_count * span // STEP, STEP, WINDOW), jnp.float32), pltpu.SemaphoreType.DMA((19,))],
        8 * tokens * width * width + 4 * tokens * WINDOW * width,
        far=range(5 + len(vectors)),
        far_outs=range(5),
        limit=24,
    )


def gelu_and_slope(values):
    size = jnp.abs(values)
    part = 1.0 / (1.0 + (0.3275911 * 0.5**0.5) * size)
    bell = jnp.exp(values * values * -0.5)
    series = part * (0.5 * 0.254829592 + part * (-0.5 * 0.284496736 + part * (0.5 * 1.421413741 + part * (-0.5 * 1.453152027 + part * (0.5 * 1.061405429)))))
    tail = series * bell
    share = jnp.where(values < 0.0, tail, 1.0 - tail)
    return values * share, share + values * bell * 0.3989422804014327


def two_parts(values):
    high = low(values)
    return high, low(values - high.astype(jnp.float32))


def membership(lengths, row, count, rows, offset):
    place = lax.broadcasted_iota(jnp.int32, (count, rows), 1) + offset
    text = lax.broadcasted_iota(jnp.int32, (count, rows), 0)
    total = 0
    inside = jnp.zeros((count, rows), jnp.float32)
    for j in range(count):
        start, total = total, total + lengths[row, j]
        inside = jnp.where((text == j) & (place >= start) & (place < total), 1.0, inside)
    return low(inside)


def length_column(lengths, row, count):
    text = lax.broadcasted_iota(jnp.int32, (count, 128), 0)
    column = jnp.zeros((count, 128), jnp.float32)
    for j in range(count):
        column = jnp.where(text == j, lengths[row, j].astype(jnp.float32), column)
    return column[:, 0:1]


def feed_kernel(count, lengths, positives, normed_ref, hidden_ref, up_ref, down_ref, vec_ref, act_out, slope_out, second_ref, factor_ref, pooled_ref, package_ref, act_ref, slope_ref, sems):
    tokens, width = normed_ref.shape
    row_count = lengths.shape[0]
    span = tokens // row_count
    rows = 256
    parts = span // rows
    pooled_ref[...] = jnp.zeros_like(pooled_ref)

    def copies(step, slot):
        here = pl.ds(pl.multiple_of(step * rows, rows), rows)
        return (
            pltpu.make_async_copy(act_ref.at[slot], act_out.at[here], sems.at[0, slot]),
            pltpu.make_async_copy(slope_ref.at[slot], slope_out.at[here], sems.at[1, slot]),
        )

    def block(step, carry):
        row, part = step // parts, step % parts
        here = pl.ds(pl.multiple_of(step * rows, rows), rows)
        slot = step % 2
        stores = copies(step, slot)

        @pl.when(step >= 2)
        def _():
            for copy in copies(step - 2, slot):
                copy.wait()

        hidden_low = hidden_ref[here]
        branch = jnp.zeros((rows, width), jnp.float32)
        for piece in range(up_ref.shape[1] // width):
            at = slice(piece * width, (piece + 1) * width)
            bias = vec_ref[UP_BIAS + piece : UP_BIAS + piece + 1]
            activation, slope = gelu_and_slope(product(hidden_low, up_ref[:, at]) + bias)
            activation = low(activation)
            act_ref[slot, :, at] = activation
            slope_ref[slot, :, at] = low(slope)
            branch = branch + product(activation, down_ref[at])
        for copy in stores:
            copy.start()
        hidden = normed_ref[here] * vec_ref[FIRST_GAIN : FIRST_GAIN + 1] + vec_ref[FIRST_SHIFT : FIRST_SHIFT + 1]
        normed, factor = normalised(hidden + branch + vec_ref[DOWN_BIAS : DOWN_BIAS + 1])
        second_ref[here] = normed
        factor_ref[here] = jnp.broadcast_to(factor, (rows, 128))
        high, rest = two_parts(normed * vec_ref[SECOND_GAIN : SECOND_GAIN + 1] + vec_ref[SECOND_SHIFT : SECOND_SHIFT + 1])
        inside = membership(lengths, row, count, rows, part * rows)
        texts = pl.ds(pl.multiple_of(row * count, count), count)
        pooled_ref[texts] += product(inside, high) + product(inside, rest)
        return carry

    lax.fori_loop(0, tokens // rows, block, 0)
    text = lax.broadcasted_iota(jnp.int32, (count, 128), 0)
    lane = lax.broadcasted_iota(jnp.int32, (count, 128), 1)
    for row in range(row_count):
        texts = slice(row * count, (row + 1) * count)
        pooled = pooled_ref[texts] / length_column(lengths, row, count)
        pooled_ref[texts] = pooled
        inverse_norm = lax.rsqrt(jnp.sum(pooled * pooled, axis=1, keepdims=True) + 1e-06)
        package_ref[texts, :width] = low(pooled * inverse_norm)
        digits = jnp.zeros((count, 128), jnp.int32)
        for j in range(count):
            own = positives[row * count + j]
            digits = jnp.where(text == j, jnp.where(lane == 0, own >> 6, own & 63), digits)
        package_ref[texts, width:] = low(jnp.where(lane < 2, digits, 0).astype(jnp.float32))
    steps = tokens // rows
    for step in range(steps - 2, steps):
        for copy in copies(step, step % 2):
            copy.wait()


def feed(lengths, positives, normed, hidden_low, up, down, vec):
    tokens, width = normed.shape
    texts, hidden = lengths.size, up.shape[1]
    return whole(
        functools.partial(feed_kernel, lengths.shape[1]),
        "feed",
        (lengths, positives),
        (normed, hidden_low, up, down, vec),
        [
            shaped((tokens, hidden), jnp.bfloat16),
            shaped((tokens, hidden), jnp.bfloat16),
            shaped((tokens, width), jnp.float32),
            shaped((tokens, 128), jnp.float32),
            shaped((texts, width), jnp.float32),
            shaped((texts, width + 128), jnp.bfloat16),
        ],
        [pltpu.VMEM((2, 256, hidden), jnp.bfloat16)] * 2 + [pltpu.SemaphoreType.DMA((2, 2))],
        4 * tokens * width * hidden,
        far_outs=(0, 1),
        limit=16,
    )


def sums_of(values):
    return jnp.sum(values, axis=0, keepdims=True)


def second_back_kernel(count, lengths, grad_ref, normed_ref, factor_ref, vec_ref, sum_ref, low_ref, totals_ref):
    tokens, width = normed_ref.shape
    row_count = lengths.shape[0]
    span = tokens // row_count
    totals_ref[...] = jnp.zeros_like(totals_ref)
    for row in range(row_count):
        rows = slice(row * span, (row + 1) * span)
        inside = membership(lengths, row, count, span, 0)
        high, rest = two_parts(grad_ref[row * count : (row + 1) * count])
        result_grad = transposed(inside, high) + transposed(inside, rest)
        normed = normed_ref[rows]
        second_sum = norm_back(result_grad, normed, factor_ref[rows, 0:1], vec_ref[SECOND_GAIN : SECOND_GAIN + 1])
        branch_grad = low(second_sum)
        sum_ref[rows] = second_sum
        low_ref[rows] = branch_grad
        totals_ref[0:1] += sums_of(branch_grad.astype(jnp.float32))
        totals_ref[1:2] += sums_of(result_grad * normed)
        totals_ref[2:3] += sums_of(result_grad)


def second_back(lengths, grad, normed, factor, vec):
    tokens, width = normed.shape
    return whole(
        functools.partial(second_back_kernel, lengths.shape[1]),
        "second_norm_back",
        (lengths,),
        (grad, normed, factor, vec),
        [shaped((tokens, width), jnp.float32), shaped((tokens, width), jnp.bfloat16), shaped((8, width), jnp.float32)],
        [],
        8 * tokens * width,
    )


def matrix_at(place, foreign, numbers):
    return 2 * ((numbers[1] & 1) ^ foreign) + place


def put_rows(numbers, sizes, sides, out_ref, place, group=8):
    labels = labels_of(numbers[0], numbers[1], sizes[1])
    rows, third = out_ref.shape[2] // 2, out_ref.shape[3]
    for first in range(0, LABELS, group):
        piece = low(sum(transposed(left(first * rows, group * rows), right) for left, right in sides))
        for own in range(group):
            for part in range(THIRDS):
                value = piece[own * rows : (own + 1) * rows, part * third : (part + 1) * third]
                out_ref[part, (first + own) ^ labels[part], place * rows : (place + 1) * rows] = value


def columns(ref):
    return lambda at, size: ref[:, at : at + size]


def blocks_out(width):
    return shaped((THIRDS, LABELS, 2 * width // LABELS, width // THIRDS), jnp.bfloat16)


def column_loads(source, target, foreign, numbers, sems):
    width = target.shape[2]
    copies = []
    for place in range(2):
        at = pl.ds(pl.multiple_of(matrix_at(place, foreign, numbers) * width, width), width)
        copies.append(pltpu.make_async_copy(source.at[:, at], target.at[place], sems.at[place]))
    return copies


def down_weight_kernel(foreign, sizes, numbers, act_in, grad_ref, out_ref, act_ref, sems):
    loads = column_loads(act_in, act_ref, foreign, numbers, sems)
    for copy in loads:
        copy.start()
    for place in range(2):
        loads[place].wait()
        put_rows(numbers, sizes, [(columns(act_ref.at[place]), grad_ref[...])], out_ref, place)


def down_weight(numbers, activation, grad, foreign, sizes, name, **waits):
    tokens, width = grad.shape
    return whole(
        functools.partial(down_weight_kernel, foreign, sizes),
        name,
        (numbers,), (activation, grad), [blocks_out(width)],
        [pltpu.VMEM((2, tokens, width), jnp.bfloat16), pltpu.SemaphoreType.DMA((2,))],
        4 * tokens * width * width,
        far=(0,),
        **waits,
    )


def up_back_kernel(foreign, sizes, numbers, grad_ref, slope_in, hidden_ref, up_ref, down_ref, before_ref, *refs):
    if foreign:
        out_ref, after_ref, totals_ref, pre_ref, slope_ref, sems = refs
    else:
        normed_ref, aux_ref, vec_ref, out_ref, totals_ref, first_ref, low_ref, sums_ref, after_ref, pre_ref, slope_ref, sems = refs
    width = grad_ref.shape[1]
    loads = column_loads(slope_in, slope_ref, foreign, numbers, sems)
    for copy in loads:
        copy.start()
    for place in range(2):
        at = pl.ds(pl.multiple_of(matrix_at(place, foreign, numbers) * width, width), width)
        active_grad = dots(grad_ref[...], down_ref[at])
        loads[place].wait()
        pre_grad = low(active_grad * slope_ref[place].astype(jnp.float32))
        pre_ref[...] = pre_grad
        totals_ref[place] = jnp.broadcast_to(sums_of(pre_grad.astype(jnp.float32)), totals_ref.shape[1:])
        before = before_ref if place == 0 else after_ref
        after_ref[...] = before[...] + dots(pre_ref[...], up_ref[:, at])
        put_rows(numbers, sizes, [(columns(hidden_ref), pre_ref[...])], out_ref, place)
    if foreign:
        return
    hidden_grad, normed = after_ref[...], normed_ref[...]
    first_sum = norm_back(hidden_grad, normed, aux_ref[:, 127:128], vec_ref[FIRST_GAIN : FIRST_GAIN + 1])
    attended_grad = low(first_sum)
    first_ref[...] = first_sum
    low_ref[...] = attended_grad
    sums_ref[...] = jnp.zeros_like(sums_ref)
    sums_ref[0:1] = sums_of(attended_grad.astype(jnp.float32))
    sums_ref[1:2] = sums_of(hidden_grad * normed)
    sums_ref[2:3] = sums_of(hidden_grad)


def up_back(numbers, grad, slope, hidden_low, up, down, before, foreign, sizes, name, rest=(), **waits):
    tokens, width = grad.shape
    wide = shaped((tokens, width), jnp.float32)
    totals = shaped((2, 8, width), jnp.float32)
    pre = [
        pltpu.VMEM((tokens, width), jnp.bfloat16),
        pltpu.VMEM((2, tokens, width), jnp.bfloat16),
        pltpu.SemaphoreType.DMA((2,)),
    ]
    if foreign:
        outs, scratch = [blocks_out(width), wide, totals], pre
    else:
        outs = [blocks_out(width), totals, wide, shaped((tokens, width), jnp.bfloat16), shaped((8, width), jnp.float32)]
        scratch = [pltpu.VMEM((tokens, width), jnp.float32)] + pre
    return whole(
        functools.partial(up_back_kernel, foreign, sizes),
        name,
        (numbers,), (grad, slope, hidden_low, up, down, before, *rest), outs, scratch,
        12 * tokens * width * width,
        far=(1,),
        limit=16,
        **waits,
    )


def attend_back_kernel(count, row, half, lengths, q_ref, k_ref, v_ref, grad_ref, wo_ref, aux_ref, *refs):
    out_ref, totals_ref, bias_ref, ctx_ref, dk_ref, dv_ref = refs[-6:]
    width = q_ref.shape[1]
    span = q_ref.shape[0] // lengths.shape[0]
    base = row * span
    grad = grad_ref[base : base + span]
    part = width // 2
    ctx_ref[...] = low(dots(grad, wo_ref[half * part : (half + 1) * part]))
    fill_bias(lengths, row, count, span, bias_ref)
    scale = HEAD_DIM**-0.5
    scaled, plain = head_masks(scale), head_masks(1.0)
    dk_ref[...] = jnp.zeros_like(dk_ref)
    dv_ref[...] = jnp.zeros_like(dv_ref)

    def heads(pair, carry):
        at = pl.ds(pl.multiple_of(pair * 2 * HEAD_DIM, 2 * HEAD_DIM), 2 * HEAD_DIM)
        own = pl.ds(pl.multiple_of(pair * 2 * HEAD_DIM - half * part, 2 * HEAD_DIM), 2 * HEAD_DIM)
        lane = lax.broadcasted_iota(jnp.int32, (STEP, 128), 1)
        for block in range(span // STEP):
            rows = pl.ds(block * STEP, STEP)
            keys = pl.ds(window_start(block, span), WINDOW)
            own_rows = pl.ds(base + block * STEP, STEP)
            own_keys = pl.ds(base + window_start(block, span), WINDOW)
            aux = aux_ref[own_rows]
            log_total = jnp.concatenate(
                [jnp.sum(jnp.where(lane == 2 * pair + half, aux, 0.0), axis=1, keepdims=True) for half in range(2)], axis=0
            )
            queries = stacked(q_ref[own_rows, at], scaled)
            context_grad = stacked(ctx_ref[rows, own], plain)
            key_rows, value_rows = k_ref[own_keys, at], v_ref[own_keys, at]
            attention = jnp.exp(biased(dots(queries, key_rows), bias_ref[block]) - log_total)
            prob_grad = dots(context_grad, value_rows)
            inner = jnp.sum(attention * prob_grad, axis=1, keepdims=True)
            score_grad = low(attention * (prob_grad - inner))
            out_ref[0, rows, at] = low(merged(product(score_grad, key_rows)) * scale)
            dk_ref[keys, own] += transposed(score_grad, queries)
            dv_ref[keys, own] += transposed(low(attention), context_grad)
        return carry

    pairs = part // (2 * HEAD_DIM)
    lax.fori_loop(half * pairs, (half + 1) * pairs, heads, 0)
    out_ref[1, :, half * part : (half + 1) * part] = low(dk_ref[...])
    out_ref[2, :, half * part : (half + 1) * part] = low(dv_ref[...])
    if half == 0:
        return
    out_ref[:, :, :part] = refs[0][:, :, :part]

    totals_ref[...] = jnp.zeros_like(totals_ref)
    totals_ref[0:1] = sums_of(out_ref[0].astype(jnp.float32))
    totals_ref[1:2] = sums_of(out_ref[2].astype(jnp.float32))


def attend_back(lengths, q, k, v, grad, wo, aux, row, half, before=None, **waits):
    tokens, width = q.shape
    span = tokens // lengths.shape[0]
    return whole(
        functools.partial(attend_back_kernel, lengths.shape[1], row, half),
        "attend_back",
        (lengths,),
        (q, k, v, grad, wo, aux) + (() if before is None else (before,)),
        [shaped((3, span, width), jnp.bfloat16), shaped((8, width), jnp.float32)],
        [
            pltpu.VMEM((span // STEP, STEP, WINDOW), jnp.float32),
            pltpu.VMEM((span, width // 2), jnp.bfloat16),
            pltpu.VMEM((span, width // 2), jnp.float32),
            pltpu.VMEM((span, width // 2), jnp.float32),
        ],
        span * width * width + 5 * span * WINDOW * width,
        **waits,
    )


def mixed_weight_kernel(foreign, sizes, numbers, x_ref, ctx_ref, grad_ref, one_ref, other_ref, out_ref):
    span = one_ref.shape[1]

    def put(left, matrix, place):
        if matrix == 3:
            put_rows(numbers, sizes, [(columns(ctx_ref), grad_ref[...])], out_ref, place)
            return
        first = lambda at, size: left[:span, at : at + size]
        second = lambda at, size: left[span:, at : at + size]
        put_rows(numbers, sizes, [(first, one_ref[matrix]), (second, other_ref[matrix])], out_ref, place)

    for pair in range(2):

        @pl.when(matrix_at(0, foreign, numbers) == 2 * pair)
        def _(pair=pair):
            put(x_ref, 2 * pair, 0)
            put(x_ref, 2 * pair + 1, 1)


def mixed_weight(numbers, x, context, grad, grads, foreign, sizes, name, **waits):
    tokens, width = x.shape
    return whole(
        functools.partial(mixed_weight_kernel, foreign, sizes),
        name,
        (numbers,), (x, context, grad, *grads), [blocks_out(width)], [],
        4 * tokens * width * width,
        **waits,
    )


def input_kernel(steps, first_ref, one_ref, other_ref, wq_ref, wk_ref, wv_ref, out_ref):
    def put(grad_ref):
        out_ref[...] = first_ref[...] + dots(grad_ref[0], wq_ref[...]) + dots(grad_ref[1], wk_ref[...]) + dots(grad_ref[2], wv_ref[...])

    @pl.when(pl.program_id(0) < steps)
    def _():
        put(one_ref)

    @pl.when(pl.program_id(0) >= steps)
    def _():
        put(other_ref)


def input_back(first_sum, grads, weights, **waits):
    tokens, width = first_sum.shape
    rows = 256
    steps = grads[0].shape[1] // rows
    one = pl.BlockSpec((3, rows, width), lambda i, *_: (0, jnp.minimum(i, steps - 1), 0))
    other = pl.BlockSpec((3, rows, width), lambda i, *_: (0, jnp.maximum(i - steps, 0), 0))
    return call(
        functools.partial(input_kernel, steps),
        "input_grad",
        (tokens // rows,),
        [rows_spec(rows, width), one, other] + [full_spec((width, width))] * 3,
        [rows_spec(rows, width)],
        [shaped((tokens, width), jnp.float32)],
        [],
        6 * tokens * width * width,
        14 * tokens * width + 6 * width * width,
        (), first_sum, *grads, *weights, **waits,
    )


VECTOR_ROWS = 48


def bundle_kernel(numbers, first_ref, second_ref, one_ref, other_ref, send_ref, keep_ref, target_ref):
    width = first_ref.shape[1]
    third = target_ref.shape[1]
    pieces = width // third
    target_ref[...] = jnp.zeros_like(target_ref)

    def put(row, values):
        for piece in range(pieces):
            target_ref[pl.ds(row * pieces + piece, 1)] = values[:, piece * third : (piece + 1) * third]

    for row in range(2):
        put(row, one_ref[row : row + 1] + other_ref[row : row + 1])
    for row in range(3):
        put(2 + row, first_ref[row : row + 1])
        put(5 + row, second_ref[row : row + 1])
    for place in range(2):
        put(8 + matrix_at(place, 0, numbers), keep_ref[place, 0:1])
        put(8 + matrix_at(place, 1, numbers), send_ref[place, 0:1])


def bundle(numbers, first, second, one, other, send, keep, **waits):
    third = first.shape[1] // THIRDS
    return whole(
        bundle_kernel, "vector_grads", (numbers,), (first, second, one, other, send, keep),
        [shaped((VECTOR_ROWS, third), jnp.float32)], [], 0, **waits,
    )


def unbundle_kernel(source_ref, *targets):
    third = source_ref.shape[1]
    row = 0
    for target in targets:
        for piece in range(target.shape[0] // third):
            target[piece * third : (piece + 1) * third] = source_ref[row : row + 1].reshape(third)
            row += 1


def unbundle(vector, sizes_out, **waits):
    return whole(
        unbundle_kernel, "unbundle", (), (vector,), [shaped((size,), jnp.float32) for size in sizes_out], [], 0, **waits
    )


def rounded(values):
    return lax.reduce_precision(values, exponent_bits=8, mantissa_bits=7)


def coded(values):
    high = rounded(values)
    rest = rounded(values - high)
    return jnp.concatenate([high, rest], axis=0).astype(jnp.bfloat16)[None], high + rest


def decoded(block):
    block = block.astype(jnp.float32)
    return block[:VECTOR_ROWS] + block[VECTOR_ROWS:]


def exchange_with(value, vector, dim, sizes):
    block, own = coded(vector)
    arrived = exchange(jnp.concatenate([value, block], axis=0), dim, sizes)
    return arrived[:-1], own + decoded(arrived[-1])


def local(
    inputs,
    lengths,
    positives,
    query_weight,
    query_bias,
    key_weight,
    value_weight,
    value_bias,
    output_weight,
    output_bias,
    first_gain,
    first_shift,
    up_weight,
    up_bias,
    down_weight_,
    down_bias,
    second_gain,
    second_shift,
):
    row_count, row_span, width = inputs.shape[1:]
    seg_count = lengths.shape[2]
    tokens = row_count * row_span
    hidden_width = up_weight.shape[1]
    sizes = (lax.axis_size("stream"), lax.axis_size("batch"))
    rest = halving_orders(sizes[1])[1]
    x = inputs.reshape(tokens, width)
    lengths = lengths.reshape(row_count, seg_count)
    numbers = jnp.stack([lax.axis_index("stream"), lax.axis_index("batch")]).astype(jnp.int32)
    vectors = (query_bias, value_bias, output_bias, first_gain, first_shift, down_bias, second_gain, second_shift, up_bias)
    q, k, v, context, aux, vec, first_normed, hidden_low = attend(
        lengths, x, (query_weight, key_weight, value_weight, output_weight), vectors
    )
    activation, slope, second_normed, second_factor, pooled, package = feed(
        lengths, positives, first_normed, hidden_low, up_weight, down_weight_, vec
    )
    own, foreign = gather_embeddings(package, sizes)
    contrast_terms, pooled_grad = contrast(numbers, lengths, own, foreign, pooled, sizes)
    second_sum, branch_grad, second_totals = second_back(
        lengths, pooled_grad, second_normed, second_factor, vec
    )
    down_send, second_totals = down_weight(
        numbers, activation, branch_grad, 1, sizes, "down_weight_send", carry=(second_totals,)
    )
    down_in = exchange(down_send, CORE, sizes)
    down_keep, second_totals = down_weight(
        numbers, activation, branch_grad, 0, sizes, "down_weight_keep", carry=(second_totals,)
    )
    up_send, partial_grad, up_totals_send = up_back(
        numbers, branch_grad, slope, hidden_low, up_weight, down_weight_, second_sum, 1, sizes, "up_back_send",
        after=(second_totals,),
    )
    up_in = exchange(up_send, CORE, sizes)
    up_keep, up_totals_keep, first_sum, attended_grad, first_totals = up_back(
        numbers, branch_grad, slope, hidden_low, up_weight, down_weight_, partial_grad, 0, sizes, "up_back_keep",
        (first_normed, aux, vec),
    )
    both = [
        jnp.concatenate([added(down_keep[i], down_in[i]), added(up_keep[i], up_in[i])], axis=1) for i in range(THIRDS)
    ]
    kept, arrived = halve(both, 0, sizes)
    back = functools.partial(attend_back, lengths, q, k, v, attended_grad, output_weight, aux)
    grads_one, totals_one, *kept = back(0, 0, carry=kept)
    grads_one, totals_one, *kept = back(0, 1, before=grads_one, carry=kept)
    kept, arrived = halve(all_added(kept, arrived), 1, sizes)
    grads_other, totals_other, *kept = back(1, 0, carry=kept)
    kept, arrived = halve(all_added(kept, arrived), 2, sizes)
    grads_other, totals_other, *kept = back(1, 1, before=grads_other, carry=kept)
    grads = (grads_one, grads_other)
    far = halving_orders(sizes[1])[0][0][3]
    send, keep = split(jnp.concatenate(all_added(kept, arrived), axis=1))
    arrived = exchange(send, far, sizes)
    mixed_send, keep = mixed_weight(
        numbers, x, context, attended_grad, grads, 1, sizes, "mixed_weight_send", carry=(keep,)
    )
    mixed_in = exchange(mixed_send, CORE, sizes)
    mixed_keep, keep = mixed_weight(
        numbers, x, context, attended_grad, grads, 0, sizes, "mixed_weight_keep", carry=(keep,)
    )
    share = added(keep, arrived)
    for dim in rest:
        share = added(share, exchange(share, dim, sizes))
    both_share = share
    both_far = exchange(both_share, far, sizes)
    (vector,) = bundle(
        numbers, first_totals, second_totals, totals_one, totals_other, up_totals_send, up_totals_keep
    )
    vector = vector + exchange(vector, CORE, sizes)
    orders, _ = halving_orders(sizes[1])
    values = [added(mixed_keep[i], mixed_in[i]) for i in range(THIRDS)]
    parts = [split(value) for value in values]
    arrived, vector = exchange_with(parts[0][0], vector, orders[0][0], sizes)
    arrived = [arrived] + [exchange(parts[i][0], orders[i][0], sizes) for i in (1, 2)]
    input_grad, *kept = input_back(
        first_sum, grads, (query_weight, key_weight, value_weight), carry=[part[1] for part in parts]
    )
    values = all_added(kept, arrived)
    both = thirds_of(jnp.concatenate([both_share, both_far], axis=0))
    for step in (1, 2):
        kept, arrived, fresh, vector = halve_and_gather(values, step, both, THIRDS - step, sizes, vector)
        values, both = all_added(kept, arrived), all_joined(both, fresh)
    send, keep = split(jnp.concatenate(values, axis=1))
    block, own = coded(vector)
    arrived = exchange(jnp.concatenate([send[0], block[0]], axis=0), far, sizes)
    fresh = [exchange(both[i], orders[i][0], sizes) for i in range(THIRDS)]
    share = added(keep, arrived[None, : send.shape[1]])
    vector = own + decoded(arrived[send.shape[1] :])
    for dim in rest:
        share = added(share, exchange(share, dim, sizes))
        vector = vector + exchange(vector, dim, sizes)
    values = thirds_of(jnp.concatenate([share, exchange(share, far, sizes)], axis=0))
    both = all_joined(both, fresh)
    both = both + [exchange(value, CORE, sizes) for value in both]
    for step in (2, 1, 0):
        arrived = [exchange(values[i], orders[i][step], sizes) for i in range(THIRDS)]
        if step == 2:
            *summed, values[0] = unbundle(vector, [width] * 8 + [hidden_width], carry=(values[0],))
        if step == 1:
            down_total, *values = spread(numbers, both, 0, "tall", "down_spread", sizes, carry=values)
        if step == 0:
            up_total, *values = spread(numbers, both, 1, "wide", "up_spread", sizes, carry=values)
        values = all_joined(values, arrived)
    blocks = values + [exchange(value, CORE, sizes) for value in values]
    query_total, key_total, value_total, output_total = spread(
        numbers, blocks, 0, "separate", "mixed_spread", sizes
    )
    return (
        contrast_terms.reshape(1, row_count * seg_count),
        input_grad.reshape(1, row_count, row_span, width),
        query_total,
        summed[0],
        key_total,
        value_total,
        summed[1],
        output_total,
        summed[2],
        summed[3],
        summed[4],
        up_total,
        summed[8],
        down_total.reshape(hidden_width, width),
        summed[5],
        summed[6],
        summed[7],
    )


def solution(mesh):
    return jax.shard_map(
        local,
        mesh=mesh,
        in_specs=(
            P("stream", "batch", None, None),
            P("stream", "batch", None),
            P("batch"),
            P(),
            P(),
            P(),
            P(),
            P(),
            P(),
            P(),
            P(),
            P(),
            P(),
            P(),
            P(),
            P(),
            P(),
            P(),
        ),
        out_specs=(
            P("stream", "batch"),
            P("stream", "batch", None, None),
            P(),
            P(),
            P(),
            P(),
            P(),
            P(),
            P(),
            P(),
            P(),
            P(),
            P(),
            P(),
            P(),
            P(),
            P(),
        ),
        check_vma=False,
    )
```

```python
import functools

import jax
import jax.numpy as jnp
import numpy as np
from jax import lax
from jax.experimental import pallas as pl
from jax.experimental.pallas import tpu as pltpu
from jax.sharding import PartitionSpec as P

HEAD_DIM = 64
MIB = 2**20
FOLD_LIMIT = 16
TILE = 512
LABELS = 16
THIRDS = 3
BOTH = ("stream", "batch")


def link_dims(batch_size):
    bits = batch_size.bit_length() - 1
    main = [("stream", 1), ("batch", 2), ("batch", 1 << (bits - 2)), ("batch", 3 << (bits - 2))]
    rest = [("batch", 1 << j) for j in range(2, bits - 2)]
    return main, rest


def coordinate(dim, stream, batch, batch_size):
    bits = batch_size.bit_length() - 1
    if dim[0] == "stream":
        return stream
    mask = dim[1]
    top = (batch >> (bits - 1)) & 1
    if mask == 3 << (bits - 2):
        return top
    if mask == 1 << (bits - 2):
        return ((batch >> (bits - 2)) & 1) ^ top
    return (batch >> (mask.bit_length() - 1)) & 1


def flipped(dim, stream, batch):
    return (stream ^ 1, batch) if dim[0] == "stream" else (stream, batch ^ dim[1])


def exchange(array, even_dim, sizes, odd_dim=None):
    odd_dim = odd_dim or even_dim
    pairs = []
    for stream in range(sizes[0]):
        for batch in range(sizes[1]):
            other = flipped(odd_dim if batch & 1 else even_dim, stream, batch)
            pairs.append((stream * sizes[1] + batch, other[0] * sizes[1] + other[1]))
    return lax.ppermute(array, BOTH, pairs)


CORE = ("batch", 1)


def halving_orders(batch_size):
    (x, y, a, b), rest = link_dims(batch_size)
    return ((x, y, a, b), (y, a, x, b), (a, x, y, b)), rest


def gather_orders(batch_size):
    (x, y, a, b), rest = link_dims(batch_size)
    return tuple(rest) + (b, a, x, y), tuple(rest) + (b, x, y, a)


def labels_of(stream, batch, batch_size):
    labels = []
    for order in halving_orders(batch_size)[0]:
        label = 0
        for dim in order:
            label = label * 2 + coordinate(dim, stream, batch, batch_size)
        labels.append(label)
    return labels


def place_at(order_even, order_odd, place, numbers):
    stream, batch = numbers[0], numbers[1]
    core = batch & 1
    for step, (even_dim, odd_dim) in enumerate(zip(order_even, order_odd, strict=True)):
        bit = (place >> step) & 1
        even = (bit, 0) if even_dim[0] == "stream" else (0, bit * even_dim[1])
        odd = (bit, 0) if odd_dim[0] == "stream" else (0, bit * odd_dim[1])
        stream = stream ^ jnp.where(core == 0, even[0], odd[0])
        batch = batch ^ jnp.where(core == 0, even[1], odd[1])
    return stream, batch


def full_spec(shape):
    return pl.BlockSpec(shape, lambda *_: (0,) * len(shape))


def added(former, latter):
    return (former.astype(jnp.float32) + latter.astype(jnp.float32)).astype(jnp.bfloat16)


def split(value):
    half = value.shape[0] // 2
    return value[half:], value[:half]


def fold_kernel(plan, *refs):
    count = len(refs) - len(plan)
    for terms, target in zip(plan, refs[count:], strict=True):
        for place, size, coded, sources in terms:
            if coded:
                values = sum(decoded(refs[number][start]) for number, start in sources)
                target[place] = encoded(values)
            elif len(sources) == 1:
                number, start = sources[0]
                target[place : place + size] = refs[number][start : start + size]
            else:
                values = sum(refs[number][start : start + size].astype(jnp.float32) for number, start in sources)
                target[place : place + size] = low(values)


def fold(outs, order, name):
    arrays, plan, shapes = [], [], []
    for out in outs:
        place, terms = 0, []
        for size, *sources in out:
            numbered = []
            for array, start in sources:
                found = [n for n, other in enumerate(arrays) if other is array]
                if not found:
                    arrays.append(array)
                numbered.append((found[0] if found else len(arrays) - 1, start))
            terms.append((place, max(size, 1), size == 0, tuple(numbered)))
            place += max(size, 1)
        plan.append(tuple(terms))
        shapes.append(shaped((place,) + arrays[0].shape[1:], jnp.bfloat16))
    return whole(functools.partial(fold_kernel, plan), name, (), arrays, shapes, [], 0, carry=(order,), limit=FOLD_LIMIT)


def exchange_each(values, step, sizes):
    orders, _ = halving_orders(sizes[1])
    return [exchange(values[i], orders[i][step], sizes) for i in range(THIRDS)]


def spread_kernel(kind, batch_size, numbers, *refs):
    sources, targets = refs[: 2 * THIRDS], refs[2 * THIRDS :]
    core = numbers[1] & 1
    labels = labels_of(numbers[0], numbers[1], batch_size)
    _, rows, third = sources[0].shape
    rows = rows // 2
    for matrix in range(4):

        def put(first, matrix=matrix):
            for part in range(THIRDS):
                for own in range(4):
                    value = sources[first + part][own ^ (labels[part] & 3), (matrix % 2) * rows : (matrix % 2 + 1) * rows]
                    value = value.astype(jnp.float32)
                    at, columns = slice(own * rows, (own + 1) * rows), slice(part * third, (part + 1) * third)
                    if kind == "tall":
                        targets[0][matrix, at, columns] = value
                    elif kind == "wide":
                        start = (matrix * THIRDS + part) * third
                        targets[0][at, start : start + third] = value
                    else:
                        targets[matrix][at, columns] = value

        @pl.when(core == matrix // 2)
        def _():
            put(0)

        @pl.when(core != matrix // 2)
        def _():
            put(THIRDS)


def spread(numbers, blocks, chunk, kind, name, sizes, **waits):
    third = blocks[0].shape[2]
    width = THIRDS * third
    rows = 2 * width // LABELS
    group = 2 * rows

    def source_spec(part):
        def at(i, numbers):
            return ((i ^ (labels_of(numbers[0], numbers[1], sizes[1])[part] >> 2)) + chunk * (LABELS // 4), 0, 0)

        return pl.BlockSpec((4, rows, third), at)

    if kind == "tall":
        specs = [pl.BlockSpec((4, group, width), lambda i, *_: (0, i, 0))]
        shapes = [shaped((4, width, width), jnp.float32)]
    elif kind == "wide":
        specs = [pl.BlockSpec((group, 4 * width), lambda i, *_: (i, 0))]
        shapes = [shaped((width, 4 * width), jnp.float32)]
    else:
        specs = [pl.BlockSpec((group, width), lambda i, *_: (i, 0))] * 4
        shapes = [shaped((width, width), jnp.float32)] * 4
    return call(
        functools.partial(spread_kernel, kind, sizes[1]),
        name,
        (LABELS // 4,),
        [source_spec(part % THIRDS) for part in range(2 * THIRDS)],
        specs, shapes, [],
        0,
        24 * width * width,
        (numbers,), *blocks, **waits,
    )


def gather_embeddings(own, sizes):
    orders = gather_orders(sizes[1])
    value = own[None]
    for even_dim, odd_dim in zip(*orders, strict=True):
        value = jnp.concatenate([value, exchange(value, even_dim, sizes, odd_dim)], axis=0)
    return value, exchange(value, CORE, sizes)


BAND = 64
STEP = 128
WINDOW = STEP + 2 * BAND
QUERY_BIAS, VALUE_BIAS, OUTPUT_BIAS, FIRST_GAIN, FIRST_SHIFT, DOWN_BIAS, SECOND_GAIN, SECOND_SHIFT, UP_BIAS = range(9)


def dots(former, latter):
    return lax.dot_general(former, latter, (((1,), (1,)), ((), ())), preferred_element_type=jnp.float32)


def product(former, latter):
    return jnp.dot(former, latter, preferred_element_type=jnp.float32)


def transposed(former, latter):
    return lax.dot_general(former, latter, (((0,), (0,)), ((), ())), preferred_element_type=jnp.float32)


def low(values):
    return values.astype(jnp.bfloat16)


def call(kernel, name, grid, in_specs, out_specs, out_shape, scratch, flops, moved, scalars, *args, after=(), carry=(), limit=16):
    taken, given = len(scalars) + len(in_specs), len(out_specs)
    waits = len(after) + len(carry)

    def run(*refs):
        kernel(*refs[:taken], *refs[taken + waits : taken + waits + given], *refs[taken + waits + given + len(carry) :])

    anywhere = pl.BlockSpec(memory_space=pl.ANY)
    return pl.pallas_call(
        run,
        grid_spec=pltpu.PrefetchScalarGridSpec(
            num_scalar_prefetch=len(scalars),
            grid=grid,
            in_specs=list(in_specs) + [anywhere] * waits,
            out_specs=list(out_specs) + [anywhere] * len(carry),
            scratch_shapes=scratch,
        ),
        out_shape=list(out_shape) + [shaped(value.shape, value.dtype) for value in carry],
        input_output_aliases={taken + len(after) + i: given + i for i in range(len(carry))},
        compiler_params=pltpu.CompilerParams(vmem_limit_bytes=limit * MIB),
        cost_estimate=pl.CostEstimate(flops=flops, bytes_accessed=moved, transcendentals=0),
        name=name,
    )(*scalars, *args, *after, *carry)


def whole(kernel, name, scalars, args, outs, scratch, flops, after=(), carry=(), far=(), far_outs=(), limit=12):
    taken, given = len(scalars) + len(args), len(outs)
    waits = len(after) + len(carry)

    def run(*refs):
        kernel(*refs[:taken], *refs[taken + waits : taken + waits + given], *refs[taken + waits + given + len(carry) :])

    near, remote = pl.BlockSpec(memory_space=pltpu.VMEM), pl.BlockSpec(memory_space=pltpu.HBM)
    anywhere = pl.BlockSpec(memory_space=pl.ANY)
    moved = sum(a.size * a.dtype.itemsize for a in args) + sum(o.size * o.dtype.itemsize for o in outs)
    args = [pltpu.with_memory_space_constraint(a, pltpu.HBM) if i in far else a for i, a in enumerate(args)]
    out_shape = [pltpu.HBM(o.shape, o.dtype) if i in far_outs else o for i, o in enumerate(outs)]
    return pl.pallas_call(
        run,
        in_specs=[pl.BlockSpec(memory_space=pltpu.SMEM)] * len(scalars)
        + [remote if i in far else near for i in range(len(args))]
        + [anywhere] * waits,
        out_specs=[remote if i in far_outs else near for i in range(given)] + [anywhere] * len(carry),
        out_shape=out_shape + [shaped(value.shape, value.dtype) for value in carry],
        scratch_shapes=scratch,
        input_output_aliases={taken + len(after) + i: given + i for i in range(len(carry))},
        compiler_params=pltpu.CompilerParams(vmem_limit_bytes=limit * MIB),
        cost_estimate=pl.CostEstimate(flops=flops, bytes_accessed=moved, transcendentals=0),
        name=name,
    )(*scalars, *args, *after, *carry)


def shaped(shape, dtype):
    return jax.ShapeDtypeStruct(shape, dtype)


def rows_spec(rows, width):
    return pl.BlockSpec((rows, width), lambda i, *_: (i, 0))


def segment_of(lengths, row, count, shape, dim):
    place = lax.broadcasted_iota(jnp.int32, shape, dim)
    total, ids = 0, jnp.zeros(shape, jnp.int32)
    for j in range(count):
        total = total + lengths[row, j]
        ids = ids + (place >= total).astype(jnp.int32)
    return ids


def window_start(block, span):
    return min(max(block * STEP - BAND, 0), span - WINDOW)


def fill_bias(lengths, row, count, span, bias_ref, first=0):
    down = segment_of(lengths, row, count, (span, 128), 0)
    along = segment_of(lengths, row, count, (8, span), 1)
    for block in range(span // STEP):
        start = window_start(block, span)
        same = down[block * STEP : (block + 1) * STEP, 0:1] == along[0:1, start : start + WINDOW]
        bias_ref[first + block] = jnp.where(same, 0.0, -1e9)


def head_masks(scale):
    lane = lax.broadcasted_iota(jnp.int32, (1, 2 * HEAD_DIM), 1)
    first = low(jnp.where(lane < HEAD_DIM, scale, 0.0))
    second = low(jnp.where(lane < HEAD_DIM, 0.0, scale))
    return first, second


def stacked(values, masks):
    return jnp.concatenate([values * masks[0], values * masks[1]], axis=0)


def merged(values):
    lane = lax.broadcasted_iota(jnp.int32, (STEP, 2 * HEAD_DIM), 1)
    return jnp.where(lane < HEAD_DIM, values[:STEP], values[STEP:])


def biased(scores, bias):
    return (scores.reshape(2, STEP, WINDOW) + bias[None]).reshape(2 * STEP, WINDOW)


def normalised(values):
    centred = values - jnp.mean(values, axis=-1, keepdims=True)
    factor = lax.rsqrt(jnp.mean(centred * centred, axis=-1, keepdims=True) + 1e-12)
    return centred * factor, factor


def norm_back(gradient, normed, factor, gain):
    inner = gradient * gain
    centred = inner - jnp.mean(inner, axis=-1, keepdims=True)
    return factor * (centred - normed * jnp.mean(inner * normed, axis=-1, keepdims=True))


def contrast_kernel(scale, sizes, numbers, lengths, own_ref, foreign_ref, pooled_ref, terms_ref, grad_ref, all_ref, digits_ref, totals_ref):
    half, texts, wide = own_ref.shape
    width = pooled_ref.shape[1]
    total = all_ref.shape[1]
    stream, batch = numbers[0], numbers[1]
    orders = gather_orders(sizes[1])

    def place(source, from_stream, from_batch, i):
        at = pl.multiple_of(from_batch * texts, texts)
        other = from_stream ^ stream
        all_ref[other, pl.ds(at, texts)] = source[i, :, :width]

        @pl.when(other == 1)
        def _():
            digits_ref[pl.ds(at, texts)] = source[i, :, width:]

    def place_both(i, carry):
        place(own_ref, *place_at(*orders, i, (stream, batch)), i)
        place(foreign_ref, *place_at(*orders, i, (stream, batch ^ 1)), i)
        return carry

    lax.fori_loop(0, half, place_both, 0)

    tile = min(TILE, total)
    totals_ref[...] = jnp.zeros_like(totals_ref)
    for column in range(total // tile):
        latter = all_ref[1, column * tile : (column + 1) * tile]

        def add(i, carry, latter=latter, column=column):
            former = all_ref[0, pl.ds(pl.multiple_of(i * tile, tile), tile)]
            sums = jnp.sum(jnp.exp(dots(former, latter) / 0.05), axis=0, keepdims=True)
            totals_ref[:, column * tile : (column + 1) * tile] += sums
            return carry

        lax.fori_loop(0, total // tile, add, 0)
    mine = all_ref[0, pl.ds(pl.multiple_of(batch * texts, texts), texts)]
    partners = all_ref[1]
    own_digits = own_ref[0, :, width:]
    logits = dots(mine, partners) / 0.05
    exponent = jnp.exp(logits)
    row_total = jnp.sum(exponent, axis=1, keepdims=True)
    own_target = (64.0 * own_digits[:, 0:1].astype(jnp.float32) + own_digits[:, 1:2].astype(jnp.float32)).astype(jnp.int32)
    lane = lax.broadcasted_iota(jnp.int32, (8, 128), 1)
    pick = jnp.where(lane == 0, 64.0, jnp.where(lane == 1, 1.0, 0.0)).astype(jnp.bfloat16)
    all_target = dots(pick, digits_ref[...])[0:1].astype(jnp.int32)
    columns = lax.broadcasted_iota(jnp.int32, (texts, total), 1)
    rows = batch * texts + lax.broadcasted_iota(jnp.int32, (texts, total), 0)
    query_hit = (own_target == columns).astype(jnp.float32)
    doc_hit = (all_target == rows).astype(jnp.float32)
    target = jnp.where(stream == 0, query_hit, doc_hit)
    chosen = jnp.sum(logits * target, axis=1, keepdims=True)
    terms_ref[...] = jnp.broadcast_to(jnp.log(row_total) - chosen, terms_ref.shape)
    own_low = ((exponent / row_total - target) * scale).astype(jnp.bfloat16)
    cross_low = ((exponent / totals_ref[0:1, :] - target) * scale).astype(jnp.bfloat16)
    gradient = (
        jnp.dot(own_low, partners, preferred_element_type=jnp.float32)
        + jnp.dot(cross_low, partners, preferred_element_type=jnp.float32)
    ) / 0.05
    gradient = gradient.astype(jnp.bfloat16).astype(jnp.float32)
    pooled = pooled_ref[...]
    inverse_norm = lax.rsqrt(jnp.sum(pooled * pooled, axis=1, keepdims=True) + 1e-06)
    embedding = pooled * inverse_norm
    inner = jnp.sum(gradient * embedding, axis=1, keepdims=True)
    count = texts // lengths.shape[0]
    divisor = jnp.concatenate([length_column(lengths, row, count) for row in range(lengths.shape[0])], axis=0)
    grad_ref[...] = inverse_norm * (gradient - embedding * inner) / divisor


def contrast(numbers, lengths, own, foreign, pooled, sizes):
    _, texts, wide = own.shape
    width = pooled.shape[1]
    total = sizes[1] * texts
    terms, gradient = whole(
        functools.partial(contrast_kernel, 1.0 / (2.0 * total), sizes),
        "contrast",
        (numbers, lengths),
        (own, foreign, pooled),
        [shaped((texts, 128), jnp.float32), shaped(pooled.shape, jnp.float32)],
        [
            pltpu.VMEM((2, total, width), jnp.bfloat16),
            pltpu.VMEM((total, wide - width), jnp.bfloat16),
            pltpu.VMEM((8, total), jnp.float32),
        ],
        2 * total * total * width,
        limit=max(12, 8 + total * width // 2**16),
    )
    return terms[:, 0], gradient


def attend_kernel(count, lengths, x_in, wq_in, wk_in, wv_in, wo_in, *refs):
    vectors_in, refs = refs[:9], refs[9:]
    q_out, k_out, v_out, ctx_out, aux_out, vec_ref, normed_ref, hidden_ref = refs[:8]
    x_ref, w_ref, wide_ref, q_ref, k_ref, v_ref, ctx_ref, aux_ref, bias_ref, sems = refs[8:]
    tokens, width = x_ref.shape
    row_count = lengths.shape[0]
    span = tokens // row_count
    places, at = [], 0
    for vector in vectors_in:
        places.append(at)
        at += vector.shape[0]
    loads = [pltpu.make_async_copy(x_in, x_ref, sems.at[0]), pltpu.make_async_copy(wq_in, w_ref.at[0], sems.at[1])]
    small = [
        pltpu.make_async_copy(vector, wide_ref.at[pl.ds(place, vector.shape[0])], sems.at[5 + i])
        for i, (vector, place) in enumerate(zip(vectors_in, places, strict=True))
    ]
    loads += [pltpu.make_async_copy(w, w_ref.at[i], sems.at[1 + i]) for i, w in ((1, wk_in), (2, wv_in), (3, wo_in))]
    for copy in loads[:2] + small + loads[2:]:
        copy.start()
    for row in range(row_count):
        fill_bias(lengths, row, count, span, bias_ref, row * (span // STEP))
    for copy in small:
        copy.wait()
    flat = wide_ref[...].astype(jnp.float32)
    for row in range(vec_ref.shape[0]):
        vec_ref[row : row + 1] = flat[row * width : (row + 1) * width].reshape(1, width)
    loads[0].wait()
    stores = [
        pltpu.make_async_copy(ref, out, sems.at[14 + i])
        for i, (ref, out) in enumerate(
            ((q_ref, q_out), (k_ref, k_out), (v_ref, v_out), (ctx_ref, ctx_out), (aux_ref, aux_out))
        )
    ]
    for i, (ref, bias) in enumerate(((q_ref, QUERY_BIAS), (k_ref, None), (v_ref, VALUE_BIAS))):
        loads[1 + i].wait()
        for row in range(row_count):
            rows = slice(row * span, (row + 1) * span)
            values = product(x_ref[rows], w_ref[i])
            ref[rows] = low(values if bias is None else values + vec_ref[bias : bias + 1])
        stores[i].start()
    masks = head_masks(HEAD_DIM**-0.5)
    aux_ref[...] = jnp.zeros_like(aux_ref)
    pairs = width // (2 * HEAD_DIM)

    def heads(step, carry):
        row, pair = step // pairs, step % pairs
        at = pl.ds(pl.multiple_of(pair * 2 * HEAD_DIM, 2 * HEAD_DIM), 2 * HEAD_DIM)
        lane = lax.broadcasted_iota(jnp.int32, (STEP, 128), 1)
        blocks = range(span // STEP)
        rows = [pl.ds(pl.multiple_of(row * span + block * STEP, STEP), STEP) for block in blocks]
        keys = [pl.ds(pl.multiple_of(row * span + window_start(block, span), BAND), WINDOW) for block in blocks]
        scores = [dots(stacked(q_ref[rows[b], at], masks), k_ref[keys[b], at]) for b in blocks]
        scores = [biased(scores[b], bias_ref[row * (span // STEP) + b]) for b in blocks]
        highest = [jnp.max(value, axis=1, keepdims=True) for value in scores]
        exponent = [jnp.exp(scores[b] - highest[b]) for b in blocks]
        total = [jnp.sum(value, axis=1, keepdims=True) for value in exponent]
        attention = [low(exponent[b] * (1.0 / total[b])) for b in blocks]
        for b in blocks:
            ctx_ref[rows[b], at] = low(merged(product(attention[b], v_ref[keys[b], at])))
        for b in blocks:
            log_total = highest[b] + jnp.log(total[b])
            kept = jnp.where(lane == 2 * pair, log_total[:STEP], aux_ref[rows[b]])
            aux_ref[rows[b]] = jnp.where(lane == 2 * pair + 1, log_total[STEP:], kept)
        return carry

    lax.fori_loop(0, row_count * pairs, heads, 0)
    stores[3].start()
    loads[4].wait()
    for row in range(row_count):
        rows = slice(row * span, (row + 1) * span)
        attended = product(ctx_ref[rows], w_ref[3]) + vec_ref[OUTPUT_BIAS : OUTPUT_BIAS + 1]
        normed, factor = normalised(x_ref[rows].astype(jnp.float32) + attended)
        normed_ref[rows] = normed
        hidden_ref[rows] = low(normed * vec_ref[FIRST_GAIN : FIRST_GAIN + 1] + vec_ref[FIRST_SHIFT : FIRST_SHIFT + 1])
        lane = lax.broadcasted_iota(jnp.int32, (span, 128), 1)
        aux_ref[rows] = jnp.where(lane == 127, factor, aux_ref[rows])
    stores[4].start()
    for copy in stores:
        copy.wait()


def attend(lengths, x, weights, vectors):
    tokens, width = x.shape
    row_count = lengths.shape[0]
    span = tokens // row_count
    vector_rows = sum(vector.shape[0] for vector in vectors) // width
    square = shaped((tokens, width), jnp.bfloat16)
    token_scratch = pltpu.VMEM((tokens, width), jnp.bfloat16)
    return whole(
        functools.partial(attend_kernel, lengths.shape[1]),
        "attend",
        (lengths,),
        (x, *weights, *vectors),
        [square] * 4
        + [
            shaped((tokens, 128), jnp.float32),
            shaped((vector_rows, width), jnp.float32),
            shaped((tokens, width), jnp.float32),
            square,
        ],
        [token_scratch, pltpu.VMEM((4, width, width), jnp.bfloat16), pltpu.VMEM((vector_rows * width,), jnp.bfloat16)]
        + [token_scratch] * 4
        + [pltpu.VMEM((tokens, 128), jnp.float32)]
        + [pltpu.VMEM((row_count * span // STEP, STEP, WINDOW), jnp.float32), pltpu.SemaphoreType.DMA((19,))],
        8 * tokens * width * width + 4 * tokens * WINDOW * width,
        far=range(5 + len(vectors)),
        far_outs=range(5),
        limit=24,
    )


def gelu_and_slope(values):
    size = jnp.abs(values)
    part = 1.0 / (1.0 + (0.3275911 * 0.5**0.5) * size)
    bell = jnp.exp(values * values * -0.5)
    series = part * (0.5 * 0.254829592 + part * (-0.5 * 0.284496736 + part * (0.5 * 1.421413741 + part * (-0.5 * 1.453152027 + part * (0.5 * 1.061405429)))))
    tail = series * bell
    share = jnp.where(values < 0.0, tail, 1.0 - tail)
    return values * share, share + values * bell * 0.3989422804014327


def two_parts(values):
    high = low(values)
    return high, low(values - high.astype(jnp.float32))


def membership(lengths, row, count, rows, offset):
    place = lax.broadcasted_iota(jnp.int32, (count, rows), 1) + offset
    text = lax.broadcasted_iota(jnp.int32, (count, rows), 0)
    total = 0
    inside = jnp.zeros((count, rows), jnp.float32)
    for j in range(count):
        start, total = total, total + lengths[row, j]
        inside = jnp.where((text == j) & (place >= start) & (place < total), 1.0, inside)
    return low(inside)


def length_column(lengths, row, count):
    text = lax.broadcasted_iota(jnp.int32, (count, 128), 0)
    column = jnp.zeros((count, 128), jnp.float32)
    for j in range(count):
        column = jnp.where(text == j, lengths[row, j].astype(jnp.float32), column)
    return column[:, 0:1]


def feed_kernel(count, lengths, positives, normed_ref, hidden_ref, up_ref, down_ref, vec_ref, act_out, slope_out, second_ref, factor_ref, pooled_ref, package_ref, act_ref, slope_ref, sems):
    tokens, width = normed_ref.shape
    row_count = lengths.shape[0]
    span = tokens // row_count
    rows = 256
    parts = span // rows
    pooled_ref[...] = jnp.zeros_like(pooled_ref)

    def copies(step, slot):
        here = pl.ds(pl.multiple_of(step * rows, rows), rows)
        return (
            pltpu.make_async_copy(act_ref.at[slot], act_out.at[here], sems.at[0, slot]),
            pltpu.make_async_copy(slope_ref.at[slot], slope_out.at[here], sems.at[1, slot]),
        )

    def block(step, carry):
        row, part = step // parts, step % parts
        here = pl.ds(pl.multiple_of(step * rows, rows), rows)
        slot = step % 2
        stores = copies(step, slot)

        @pl.when(step >= 2)
        def _():
            for copy in copies(step - 2, slot):
                copy.wait()

        hidden_low = hidden_ref[here]
        branch = jnp.zeros((rows, width), jnp.float32)
        pieces = up_ref.shape[1] // width
        spots = [slice(piece * width, (piece + 1) * width) for piece in range(pieces)]
        later = product(hidden_low, up_ref[:, spots[0]])
        done = None
        for piece, at in enumerate(spots):
            values = later + vec_ref[UP_BIAS + piece : UP_BIAS + piece + 1]
            if piece + 1 < pieces:
                later = product(hidden_low, up_ref[:, spots[piece + 1]])
            if done is not None:
                branch = branch + product(done, down_ref[spots[piece - 1]])
            activation, slope = gelu_and_slope(values)
            done = low(activation)
            act_ref[slot, :, at] = done
            slope_ref[slot, :, at] = low(slope)
        branch = branch + product(done, down_ref[spots[-1]])
        for copy in stores:
            copy.start()
        hidden = normed_ref[here] * vec_ref[FIRST_GAIN : FIRST_GAIN + 1] + vec_ref[FIRST_SHIFT : FIRST_SHIFT + 1]
        normed, factor = normalised(hidden + branch + vec_ref[DOWN_BIAS : DOWN_BIAS + 1])
        second_ref[here] = normed
        factor_ref[here] = jnp.broadcast_to(factor, (rows, 128))
        high, rest = two_parts(normed * vec_ref[SECOND_GAIN : SECOND_GAIN + 1] + vec_ref[SECOND_SHIFT : SECOND_SHIFT + 1])
        inside = membership(lengths, row, count, rows, part * rows)
        texts = pl.ds(pl.multiple_of(row * count, count), count)
        pooled_ref[texts] += product(inside, high) + product(inside, rest)
        return carry

    lax.fori_loop(0, tokens // rows, block, 0)
    text = lax.broadcasted_iota(jnp.int32, (count, 128), 0)
    lane = lax.broadcasted_iota(jnp.int32, (count, 128), 1)
    for row in range(row_count):
        texts = slice(row * count, (row + 1) * count)
        pooled = pooled_ref[texts] / length_column(lengths, row, count)
        pooled_ref[texts] = pooled
        inverse_norm = lax.rsqrt(jnp.sum(pooled * pooled, axis=1, keepdims=True) + 1e-06)
        package_ref[texts, :width] = low(pooled * inverse_norm)
        digits = jnp.zeros((count, 128), jnp.int32)
        for j in range(count):
            own = positives[row * count + j]
            digits = jnp.where(text == j, jnp.where(lane == 0, own >> 6, own & 63), digits)
        package_ref[texts, width:] = low(jnp.where(lane < 2, digits, 0).astype(jnp.float32))
    steps = tokens // rows
    for step in range(steps - 2, steps):
        for copy in copies(step, step % 2):
            copy.wait()


def feed(lengths, positives, normed, hidden_low, up, down, vec):
    tokens, width = normed.shape
    texts, hidden = lengths.size, up.shape[1]
    return whole(
        functools.partial(feed_kernel, lengths.shape[1]),
        "feed",
        (lengths, positives),
        (normed, hidden_low, up, down, vec),
        [
            shaped((tokens, hidden), jnp.bfloat16),
            shaped((tokens, hidden), jnp.bfloat16),
            shaped((tokens, width), jnp.float32),
            shaped((tokens, 128), jnp.float32),
            shaped((texts, width), jnp.float32),
            shaped((texts, width + 128), jnp.bfloat16),
        ],
        [pltpu.VMEM((2, 256, hidden), jnp.bfloat16)] * 2 + [pltpu.SemaphoreType.DMA((2, 2))],
        4 * tokens * width * hidden,
        far_outs=(0, 1),
        limit=16,
    )


def sums_of(values):
    return jnp.sum(values, axis=0, keepdims=True)


def second_back_kernel(count, lengths, grad_ref, normed_ref, factor_ref, vec_ref, sum_ref, low_ref, totals_ref):
    tokens, width = normed_ref.shape
    row_count = lengths.shape[0]
    span = tokens // row_count
    totals_ref[...] = jnp.zeros_like(totals_ref)
    for row in range(row_count):
        rows = slice(row * span, (row + 1) * span)
        inside = membership(lengths, row, count, span, 0)
        high, rest = two_parts(grad_ref[row * count : (row + 1) * count])
        result_grad = transposed(inside, high) + transposed(inside, rest)
        normed = normed_ref[rows]
        second_sum = norm_back(result_grad, normed, factor_ref[rows, 0:1], vec_ref[SECOND_GAIN : SECOND_GAIN + 1])
        branch_grad = low(second_sum)
        sum_ref[rows] = second_sum
        low_ref[rows] = branch_grad
        totals_ref[0:1] += sums_of(branch_grad.astype(jnp.float32))
        totals_ref[1:2] += sums_of(result_grad * normed)
        totals_ref[2:3] += sums_of(result_grad)


def second_back(lengths, grad, normed, factor, vec):
    tokens, width = normed.shape
    return whole(
        functools.partial(second_back_kernel, lengths.shape[1]),
        "second_norm_back",
        (lengths,),
        (grad, normed, factor, vec),
        [shaped((tokens, width), jnp.float32), shaped((tokens, width), jnp.bfloat16), shaped((8, width), jnp.float32)],
        [],
        8 * tokens * width,
    )


def matrix_at(place, foreign, numbers):
    return 2 * ((numbers[1] & 1) ^ foreign) + place


def put_rows(numbers, sizes, sides, out_ref, place, group=8):
    labels = labels_of(numbers[0], numbers[1], sizes[1])
    rows, third = out_ref.shape[2] // 2, out_ref.shape[3]
    for first in range(0, LABELS, group):
        piece = low(sum(transposed(left(first * rows, group * rows), right) for left, right in sides))
        for own in range(group):
            for part in range(THIRDS):
                value = piece[own * rows : (own + 1) * rows, part * third : (part + 1) * third]
                out_ref[part, (first + own) ^ labels[part], place * rows : (place + 1) * rows] = value


def columns(ref):
    return lambda at, size: ref[:, at : at + size]


def blocks_out(width):
    return shaped((THIRDS, LABELS, 2 * width // LABELS, width // THIRDS), jnp.bfloat16)


def column_loads(source, target, foreign, numbers, sems):
    width = target.shape[2]
    copies = []
    for place in range(2):
        at = pl.ds(pl.multiple_of(matrix_at(place, foreign, numbers) * width, width), width)
        copies.append(pltpu.make_async_copy(source.at[:, at], target.at[place], sems.at[place]))
    return copies


def down_weight_kernel(foreign, sizes, numbers, act_in, grad_ref, out_ref, act_ref, sems):
    loads = column_loads(act_in, act_ref, foreign, numbers, sems)
    for copy in loads:
        copy.start()
    for place in range(2):
        loads[place].wait()
        put_rows(numbers, sizes, [(columns(act_ref.at[place]), grad_ref[...])], out_ref, place)


def down_weight(numbers, activation, grad, foreign, sizes, name, **waits):
    tokens, width = grad.shape
    return whole(
        functools.partial(down_weight_kernel, foreign, sizes),
        name,
        (numbers,), (activation, grad), [blocks_out(width)],
        [pltpu.VMEM((2, tokens, width), jnp.bfloat16), pltpu.SemaphoreType.DMA((2,))],
        4 * tokens * width * width,
        far=(0,),
        **waits,
    )


def up_back_kernel(foreign, sizes, numbers, grad_ref, slope_in, hidden_ref, up_ref, down_ref, before_ref, *refs):
    if foreign:
        out_ref, after_ref, totals_ref, pre_ref, slope_ref, sems = refs
    else:
        normed_ref, aux_ref, vec_ref, out_ref, totals_ref, first_ref, low_ref, sums_ref, after_ref, pre_ref, slope_ref, sems = refs
    width = grad_ref.shape[1]
    loads = column_loads(slope_in, slope_ref, foreign, numbers, sems)
    for copy in loads:
        copy.start()
    for place in range(2):
        at = pl.ds(pl.multiple_of(matrix_at(place, foreign, numbers) * width, width), width)
        active_grad = dots(grad_ref[...], down_ref[at])
        loads[place].wait()
        pre_grad = low(active_grad * slope_ref[place].astype(jnp.float32))
        pre_ref[...] = pre_grad
        totals_ref[place] = jnp.broadcast_to(sums_of(pre_grad.astype(jnp.float32)), totals_ref.shape[1:])
        before = before_ref if place == 0 else after_ref
        after_ref[...] = before[...] + dots(pre_ref[...], up_ref[:, at])
        put_rows(numbers, sizes, [(columns(hidden_ref), pre_ref[...])], out_ref, place)
    if foreign:
        return
    hidden_grad, normed = after_ref[...], normed_ref[...]
    first_sum = norm_back(hidden_grad, normed, aux_ref[:, 127:128], vec_ref[FIRST_GAIN : FIRST_GAIN + 1])
    attended_grad = low(first_sum)
    first_ref[...] = first_sum
    low_ref[...] = attended_grad
    sums_ref[...] = jnp.zeros_like(sums_ref)
    sums_ref[0:1] = sums_of(attended_grad.astype(jnp.float32))
    sums_ref[1:2] = sums_of(hidden_grad * normed)
    sums_ref[2:3] = sums_of(hidden_grad)


def up_back(numbers, grad, slope, hidden_low, up, down, before, foreign, sizes, name, rest=(), **waits):
    tokens, width = grad.shape
    wide = shaped((tokens, width), jnp.float32)
    totals = shaped((2, 8, width), jnp.float32)
    pre = [
        pltpu.VMEM((tokens, width), jnp.bfloat16),
        pltpu.VMEM((2, tokens, width), jnp.bfloat16),
        pltpu.SemaphoreType.DMA((2,)),
    ]
    if foreign:
        outs, scratch = [blocks_out(width), wide, totals], pre
    else:
        outs = [blocks_out(width), totals, wide, shaped((tokens, width), jnp.bfloat16), shaped((8, width), jnp.float32)]
        scratch = [pltpu.VMEM((tokens, width), jnp.float32)] + pre
    return whole(
        functools.partial(up_back_kernel, foreign, sizes),
        name,
        (numbers,), (grad, slope, hidden_low, up, down, before, *rest), outs, scratch,
        12 * tokens * width * width,
        far=(1,),
        limit=16,
        **waits,
    )


def attend_back_kernel(count, row, half, lengths, q_ref, k_ref, v_ref, grad_ref, wo_ref, aux_ref, *refs):
    out_ref, totals_ref, bias_ref, ctx_ref, dk_ref, dv_ref = refs[-6:]
    width = q_ref.shape[1]
    span = q_ref.shape[0] // lengths.shape[0]
    base = row * span
    grad = grad_ref[base : base + span]
    part = width // 2
    ctx_ref[...] = low(dots(grad, wo_ref[half * part : (half + 1) * part]))
    fill_bias(lengths, row, count, span, bias_ref)
    scale = HEAD_DIM**-0.5
    scaled, plain = head_masks(scale), head_masks(1.0)
    dk_ref[...] = jnp.zeros_like(dk_ref)
    dv_ref[...] = jnp.zeros_like(dv_ref)

    def heads(pair, carry):
        at = pl.ds(pl.multiple_of(pair * 2 * HEAD_DIM, 2 * HEAD_DIM), 2 * HEAD_DIM)
        own = pl.ds(pl.multiple_of(pair * 2 * HEAD_DIM - half * part, 2 * HEAD_DIM), 2 * HEAD_DIM)
        lane = lax.broadcasted_iota(jnp.int32, (STEP, 128), 1)
        blocks = range(span // STEP)
        rows = [pl.ds(block * STEP, STEP) for block in blocks]
        keys = [pl.ds(window_start(block, span), WINDOW) for block in blocks]
        own_rows = [pl.ds(base + block * STEP, STEP) for block in blocks]
        own_keys = [pl.ds(base + window_start(block, span), WINDOW) for block in blocks]
        queries = [stacked(q_ref[own_rows[b], at], scaled) for b in blocks]
        context_grad = [stacked(ctx_ref[rows[b], own], plain) for b in blocks]
        scores = [dots(queries[b], k_ref[own_keys[b], at]) for b in blocks]
        prob_grad = [dots(context_grad[b], v_ref[own_keys[b], at]) for b in blocks]
        log_total = [
            jnp.concatenate(
                [
                    jnp.sum(jnp.where(lane == 2 * pair + side, aux_ref[own_rows[b]], 0.0), axis=1, keepdims=True)
                    for side in range(2)
                ],
                axis=0,
            )
            for b in blocks
        ]
        attention = [jnp.exp(biased(scores[b], bias_ref[b]) - log_total[b]) for b in blocks]
        inner = [jnp.sum(attention[b] * prob_grad[b], axis=1, keepdims=True) for b in blocks]
        score_grad = [low(attention[b] * (prob_grad[b] - inner[b])) for b in blocks]
        for b in blocks:
            out_ref[0, rows[b], at] = low(merged(product(score_grad[b], k_ref[own_keys[b], at])) * scale)
        for b in blocks:
            dk_ref[keys[b], own] += transposed(score_grad[b], queries[b])
        for b in blocks:
            dv_ref[keys[b], own] += transposed(low(attention[b]), context_grad[b])
        return carry

    pairs = part // (2 * HEAD_DIM)
    lax.fori_loop(half * pairs, (half + 1) * pairs, heads, 0)
    out_ref[1, :, half * part : (half + 1) * part] = low(dk_ref[...])
    out_ref[2, :, half * part : (half + 1) * part] = low(dv_ref[...])
    if half == 0:
        return
    out_ref[:, :, :part] = refs[0][:, :, :part]

    totals_ref[...] = jnp.zeros_like(totals_ref)
    totals_ref[0:1] = sums_of(out_ref[0].astype(jnp.float32))
    totals_ref[1:2] = sums_of(out_ref[2].astype(jnp.float32))


def attend_back(lengths, q, k, v, grad, wo, aux, row, half, before=None, **waits):
    tokens, width = q.shape
    span = tokens // lengths.shape[0]
    return whole(
        functools.partial(attend_back_kernel, lengths.shape[1], row, half),
        "attend_back",
        (lengths,),
        (q, k, v, grad, wo, aux) + (() if before is None else (before,)),
        [shaped((3, span, width), jnp.bfloat16), shaped((8, width), jnp.float32)],
        [
            pltpu.VMEM((span // STEP, STEP, WINDOW), jnp.float32),
            pltpu.VMEM((span, width // 2), jnp.bfloat16),
            pltpu.VMEM((span, width // 2), jnp.float32),
            pltpu.VMEM((span, width // 2), jnp.float32),
        ],
        span * width * width + 5 * span * WINDOW * width,
        **waits,
    )


def mixed_weight_kernel(foreign, sizes, numbers, x_ref, ctx_ref, grad_ref, one_ref, other_ref, out_ref):
    span = one_ref.shape[1]

    def put(left, matrix, place):
        if matrix == 3:
            put_rows(numbers, sizes, [(columns(ctx_ref), grad_ref[...])], out_ref, place)
            return
        first = lambda at, size: left[:span, at : at + size]
        second = lambda at, size: left[span:, at : at + size]
        put_rows(numbers, sizes, [(first, one_ref[matrix]), (second, other_ref[matrix])], out_ref, place)

    for pair in range(2):

        @pl.when(matrix_at(0, foreign, numbers) == 2 * pair)
        def _(pair=pair):
            put(x_ref, 2 * pair, 0)
            put(x_ref, 2 * pair + 1, 1)


def mixed_weight(numbers, x, context, grad, grads, foreign, sizes, name, **waits):
    tokens, width = x.shape
    return whole(
        functools.partial(mixed_weight_kernel, foreign, sizes),
        name,
        (numbers,), (x, context, grad, *grads), [blocks_out(width)], [],
        4 * tokens * width * width,
        **waits,
    )


def input_kernel(steps, first_ref, one_ref, other_ref, wq_ref, wk_ref, wv_ref, out_ref):
    def put(grad_ref):
        out_ref[...] = first_ref[...] + dots(grad_ref[0], wq_ref[...]) + dots(grad_ref[1], wk_ref[...]) + dots(grad_ref[2], wv_ref[...])

    @pl.when(pl.program_id(0) < steps)
    def _():
        put(one_ref)

    @pl.when(pl.program_id(0) >= steps)
    def _():
        put(other_ref)


def input_back(first_sum, grads, weights, **waits):
    tokens, width = first_sum.shape
    rows = 256
    steps = grads[0].shape[1] // rows
    one = pl.BlockSpec((3, rows, width), lambda i, *_: (0, jnp.minimum(i, steps - 1), 0))
    other = pl.BlockSpec((3, rows, width), lambda i, *_: (0, jnp.maximum(i - steps, 0), 0))
    return call(
        functools.partial(input_kernel, steps),
        "input_grad",
        (tokens // rows,),
        [rows_spec(rows, width), one, other] + [full_spec((width, width))] * 3,
        [rows_spec(rows, width)],
        [shaped((tokens, width), jnp.float32)],
        [],
        6 * tokens * width * width,
        14 * tokens * width + 6 * width * width,
        (), first_sum, *grads, *weights, **waits,
    )


VECTOR_ROWS = 48


def encoded(values):
    high, rest = two_parts(values)
    return jnp.concatenate([high, rest], axis=0)


def decoded(block):
    block = block.astype(jnp.float32)
    return block[:VECTOR_ROWS] + block[VECTOR_ROWS:]


def bundle_kernel(numbers, first_ref, second_ref, one_ref, other_ref, send_ref, keep_ref, coded_ref, target_ref):
    width = first_ref.shape[1]
    third = target_ref.shape[1]
    pieces = width // third
    target_ref[...] = jnp.zeros_like(target_ref)

    def put(row, values):
        for piece in range(pieces):
            target_ref[pl.ds(row * pieces + piece, 1)] = values[:, piece * third : (piece + 1) * third]

    for row in range(2):
        put(row, one_ref[row : row + 1] + other_ref[row : row + 1])
    for row in range(3):
        put(2 + row, first_ref[row : row + 1])
        put(5 + row, second_ref[row : row + 1])
    for place in range(2):
        put(8 + matrix_at(place, 0, numbers), keep_ref[place, 0:1])
        put(8 + matrix_at(place, 1, numbers), send_ref[place, 0:1])
    coded_ref[0] = encoded(target_ref[...])


def bundle(numbers, first, second, one, other, send, keep, **waits):
    third = first.shape[1] // THIRDS
    return whole(
        bundle_kernel, "vector_grads", (numbers,), (first, second, one, other, send, keep),
        [shaped((1, 2 * VECTOR_ROWS, third), jnp.bfloat16)], [pltpu.VMEM((VECTOR_ROWS, third), jnp.float32)], 0, **waits,
    )


def unbundle_kernel(source_ref, *targets):
    third = source_ref.shape[2]
    values = decoded(source_ref[0])
    row = 0
    for target in targets:
        for piece in range(target.shape[0] // third):
            target[piece * third : (piece + 1) * third] = values[row : row + 1].reshape(third)
            row += 1


def unbundle(block, sizes_out, **waits):
    return whole(
        unbundle_kernel, "unbundle", (), (block,), [shaped((size,), jnp.float32) for size in sizes_out], [], 0, **waits
    )


def local(
    inputs,
    lengths,
    positives,
    query_weight,
    query_bias,
    key_weight,
    value_weight,
    value_bias,
    output_weight,
    output_bias,
    first_gain,
    first_shift,
    up_weight,
    up_bias,
    down_weight_,
    down_bias,
    second_gain,
    second_shift,
):
    row_count, row_span, width = inputs.shape[1:]
    seg_count = lengths.shape[2]
    tokens = row_count * row_span
    hidden_width = up_weight.shape[1]
    sizes = (lax.axis_size("stream"), lax.axis_size("batch"))
    rest = halving_orders(sizes[1])[1]
    x = inputs.reshape(tokens, width)
    lengths = lengths.reshape(row_count, seg_count)
    numbers = jnp.stack([lax.axis_index("stream"), lax.axis_index("batch")]).astype(jnp.int32)
    vectors = (query_bias, value_bias, output_bias, first_gain, first_shift, down_bias, second_gain, second_shift, up_bias)
    q, k, v, context, aux, vec, first_normed, hidden_low = attend(
        lengths, x, (query_weight, key_weight, value_weight, output_weight), vectors
    )
    activation, slope, second_normed, second_factor, pooled, package = feed(
        lengths, positives, first_normed, hidden_low, up_weight, down_weight_, vec
    )
    own, foreign = gather_embeddings(package, sizes)
    contrast_terms, pooled_grad = contrast(numbers, lengths, own, foreign, pooled, sizes)
    second_sum, branch_grad, second_totals = second_back(
        lengths, pooled_grad, second_normed, second_factor, vec
    )
    orders, rest = halving_orders(sizes[1])
    far = orders[0][3]
    parts = range(THIRDS)
    half = LABELS // 2

    def flat(value):
        return value.reshape((-1,) + value.shape[2:])

    order = second_totals
    down_send, order = down_weight(numbers, activation, branch_grad, 1, sizes, "down_weight_send", carry=(order,))
    down_in = exchange(down_send, CORE, sizes)
    down_keep, order = down_weight(numbers, activation, branch_grad, 0, sizes, "down_weight_keep", carry=(order,))
    up_send, partial_grad, up_totals_send, order = up_back(
        numbers, branch_grad, slope, hidden_low, up_weight, down_weight_, second_sum, 1, sizes, "up_back_send",
        carry=(order,),
    )
    up_in = exchange(up_send, CORE, sizes)
    up_keep, up_totals_keep, first_sum, attended_grad, first_totals, order = up_back(
        numbers, branch_grad, slope, hidden_low, up_weight, down_weight_, partial_grad, 0, sizes, "up_back_keep",
        (first_normed, aux, vec), carry=(order,),
    )
    pairs = [(flat(down_keep), flat(down_in)), (flat(up_keep), flat(up_in))]

    def taken(i, start, size):
        return [(size, (keep, i * LABELS + start), (arrived, i * LABELS + start)) for keep, arrived in pairs]

    *made, order = fold([taken(i, half, half) for i in parts] + [taken(i, 0, half) for i in parts], order, "both_0")
    both, kept = made[:THIRDS], made[THIRDS:]
    arrived = exchange_each(both, 0, sizes)
    back = functools.partial(attend_back, lengths, q, k, v, attended_grad, output_weight, aux)
    grads_one, totals_one, order = back(0, 0, carry=(order,))
    grads_one, totals_one, order = back(0, 1, before=grads_one, carry=(order,))

    def halved(kept, arrived, size, chunks):
        sums = lambda i, start: [
            (size, (kept[i], 2 * size * c + start), (arrived[i], 2 * size * c + start)) for c in range(chunks)
        ]
        return [sums(i, size) for i in parts], [sums(i, 0) for i in parts]

    sends, keeps = halved(kept, arrived, half // 2, 2)
    *made, order = fold(sends + keeps, order, "both_1")
    both, kept = made[:THIRDS], made[THIRDS:]
    arrived = exchange_each(both, 1, sizes)
    grads_other, totals_other, order = back(1, 0, carry=(order,))
    sends, keeps = halved(kept, arrived, half // 4, 2)
    *made, order = fold(sends + keeps, order, "both_2")
    both, kept = made[:THIRDS], made[THIRDS:]
    arrived = exchange_each(both, 2, sizes)
    grads_other, totals_other, order = back(1, 1, before=grads_other, carry=(order,))
    grads = (grads_one, grads_other)
    sends, keeps = halved(kept, arrived, 1, 2)
    both, kept, order = fold([sum(sends, []), sum(keeps, [])], order, "both_3")
    arrived = exchange(both, far, sizes)
    mixed_send, order = mixed_weight(
        numbers, x, context, attended_grad, grads, 1, sizes, "mixed_weight_send", carry=(order,)
    )
    mixed_in = exchange(mixed_send, CORE, sizes)
    vector, order = bundle(
        numbers, first_totals, second_totals, totals_one, totals_other, up_totals_send, up_totals_keep, carry=(order,)
    )
    vector_in = exchange(vector, CORE, sizes)
    mixed_keep, order = mixed_weight(
        numbers, x, context, attended_grad, grads, 0, sizes, "mixed_weight_keep", carry=(order,)
    )
    pairs = [(flat(mixed_keep), flat(mixed_in))]
    sends = [taken(i, half, half) for i in parts]
    sends[0] = sends[0] + [(0, (vector, 0), (vector_in, 0))]
    *made, order = fold(sends + [taken(i, 0, half) for i in parts], order, "mixed_0")
    mixed, mixed_kept = made[:THIRDS], made[THIRDS:]
    mixed_in = exchange_each(mixed, 0, sizes)
    both, order = fold([[(2 * THIRDS, (kept, 0), (arrived, 0))]], order, "both_4")
    for dim in rest:
        both, order = fold([[(2 * THIRDS, (both, 0), (exchange(both, dim, sizes), 0))]], order, "both_rest")
    arrived = exchange(both, far, sizes)
    input_grad, order = input_back(first_sum, grads, (query_weight, key_weight, value_weight), carry=(order,))

    def mixed_step(mixed, mixed_kept, mixed_in, size):
        sends, keeps = halved(mixed_kept, mixed_in, size, 1)
        sends[0] = sends[0] + [(0, (mixed[0], 2 * size), (mixed_in[0], 2 * size))]
        return sends, keeps

    def joined(former, latter, size, chunks):
        return [
            sum([[(size, (former[i], size * c)), (size, (latter[i], size * c))] for c in range(chunks)], [])
            for i in parts
        ]

    sends, keeps = mixed_step(mixed, mixed_kept, mixed_in, half // 2)
    *made, order = fold(sends + keeps, order, "mixed_1")
    mixed, mixed_kept = made[:THIRDS], made[THIRDS:]
    mixed_in = exchange_each(mixed, 1, sizes)
    sends = [
        [(1, (source, 2 * i + c)) for c in range(2) for source in (both, arrived)] for i in parts
    ]
    *both, order = fold(sends, order, "both_5")
    arrived = exchange_each(both, 2, sizes)
    sends, keeps = mixed_step(mixed, mixed_kept, mixed_in, half // 4)
    *made, order = fold(sends + keeps, order, "mixed_2")
    mixed, mixed_kept = made[:THIRDS], made[THIRDS:]
    mixed_in = exchange_each(mixed, 2, sizes)
    *both, order = fold(joined(both, arrived, 2, 2), order, "both_6")
    arrived = exchange_each(both, 1, sizes)
    sends, keeps = mixed_step(mixed, mixed_kept, mixed_in, 1)
    mixed, mixed_kept, order = fold([sends[1] + sends[2] + sends[0], keeps[1] + keeps[2] + keeps[0]], order, "mixed_3")
    mixed_in = exchange(mixed, far, sizes)
    *both, order = fold(joined(both, arrived, 4, 2), order, "both_7")
    arrived = exchange_each(both, 0, sizes)
    share, vector, order = fold(
        [[(THIRDS, (mixed_kept, 0), (mixed_in, 0))], [(0, (mixed, THIRDS), (mixed_in, THIRDS))]], order, "mixed_4"
    )
    for dim in rest:
        share_in, vector_in = exchange(share, dim, sizes), exchange(vector, dim, sizes)
        share, vector, order = fold(
            [[(THIRDS, (share, 0), (share_in, 0))], [(0, (vector, 0), (vector_in, 0))]], order, "mixed_rest"
        )
    mixed_in = exchange(share, far, sizes)
    *summed, order = unbundle(vector, [width] * 8 + [hidden_width], carry=(order,))
    turned = [(i + 2) % THIRDS for i in parts]
    *mixed, order = fold(
        [[(1, (source, turned[i])) for source in (share, mixed_in)] for i in parts], order, "mixed_5"
    )
    mixed_in = exchange_each(mixed, 2, sizes)
    *both, order = fold(joined(both, arrived, 8, 2), order, "both_8")
    both = both + [exchange(value, CORE, sizes) for value in both]
    *mixed, order = fold(joined(mixed, mixed_in, 2, 1), order, "mixed_6")
    mixed_in = exchange_each(mixed, 1, sizes)
    down_total, order = spread(numbers, both, 0, "tall", "down_spread", sizes, carry=(order,))
    *mixed, order = fold(joined(mixed, mixed_in, 4, 1), order, "mixed_7")
    mixed_in = exchange_each(mixed, 0, sizes)
    up_total, order = spread(numbers, both, 1, "wide", "up_spread", sizes, carry=(order,))
    *mixed, order = fold(joined(mixed, mixed_in, 8, 1), order, "mixed_8")
    blocks = mixed + [exchange(value, CORE, sizes) for value in mixed]
    query_total, key_total, value_total, output_total = spread(
        numbers, blocks, 0, "separate", "mixed_spread", sizes, after=(order,)
    )
    return (
        contrast_terms.reshape(1, row_count * seg_count),
        input_grad.reshape(1, row_count, row_span, width),
        query_total,
        summed[0],
        key_total,
        value_total,
        summed[1],
        output_total,
        summed[2],
        summed[3],
        summed[4],
        up_total,
        summed[8],
        down_total.reshape(hidden_width, width),
        summed[5],
        summed[6],
        summed[7],
    )


def solution(mesh):
    return jax.shard_map(
        local,
        mesh=mesh,
        in_specs=(
            P("stream", "batch", None, None),
            P("stream", "batch", None),
            P("batch"),
            P(),
            P(),
            P(),
            P(),
            P(),
            P(),
            P(),
            P(),
            P(),
            P(),
            P(),
            P(),
            P(),
            P(),
            P(),
        ),
        out_specs=(
            P("stream", "batch"),
            P("stream", "batch", None, None),
            P(),
            P(),
            P(),
            P(),
            P(),
            P(),
            P(),
            P(),
            P(),
            P(),
            P(),
            P(),
            P(),
            P(),
            P(),
        ),
        check_vma=False,
    )
```

```python
import functools

import jax
import jax.numpy as jnp
import numpy as np
from jax import lax
from jax.experimental import pallas as pl
from jax.experimental.pallas import tpu as pltpu
from jax.sharding import PartitionSpec as P

HEAD_DIM = 64
MIB = 2**20
FOLD_LIMIT = 16
TILE = 512
LABELS = 16
THIRDS = 3
BOTH = ("stream", "batch")


def link_dims(batch_size):
    bits = batch_size.bit_length() - 1
    main = [("stream", 1), ("batch", 2), ("batch", 1 << (bits - 2)), ("batch", 3 << (bits - 2))]
    rest = [("batch", 1 << j) for j in range(2, bits - 2)]
    return main, rest


def coordinate(dim, stream, batch, batch_size):
    bits = batch_size.bit_length() - 1
    if dim[0] == "stream":
        return stream
    mask = dim[1]
    top = (batch >> (bits - 1)) & 1
    if mask == 3 << (bits - 2):
        return top
    if mask == 1 << (bits - 2):
        return ((batch >> (bits - 2)) & 1) ^ top
    return (batch >> (mask.bit_length() - 1)) & 1


def flipped(dim, stream, batch):
    return (stream ^ 1, batch) if dim[0] == "stream" else (stream, batch ^ dim[1])


def exchange(array, even_dim, sizes, odd_dim=None):
    odd_dim = odd_dim or even_dim
    pairs = []
    for stream in range(sizes[0]):
        for batch in range(sizes[1]):
            other = flipped(odd_dim if batch & 1 else even_dim, stream, batch)
            pairs.append((stream * sizes[1] + batch, other[0] * sizes[1] + other[1]))
    return lax.ppermute(array, BOTH, pairs)


CORE = ("batch", 1)


def halving_orders(batch_size):
    (x, y, a, b), rest = link_dims(batch_size)
    return ((x, y, a, b), (y, a, x, b), (a, x, y, b)), rest


def gather_orders(batch_size):
    (x, y, a, b), rest = link_dims(batch_size)
    return tuple(rest) + (b, a, x, y), tuple(rest) + (b, x, y, a)


def labels_of(stream, batch, batch_size):
    labels = []
    for order in halving_orders(batch_size)[0]:
        label = 0
        for dim in order:
            label = label * 2 + coordinate(dim, stream, batch, batch_size)
        labels.append(label)
    return labels


def place_at(order_even, order_odd, place, numbers):
    stream, batch = numbers[0], numbers[1]
    core = batch & 1
    for step, (even_dim, odd_dim) in enumerate(zip(order_even, order_odd, strict=True)):
        bit = (place >> step) & 1
        even = (bit, 0) if even_dim[0] == "stream" else (0, bit * even_dim[1])
        odd = (bit, 0) if odd_dim[0] == "stream" else (0, bit * odd_dim[1])
        stream = stream ^ jnp.where(core == 0, even[0], odd[0])
        batch = batch ^ jnp.where(core == 0, even[1], odd[1])
    return stream, batch


def full_spec(shape):
    return pl.BlockSpec(shape, lambda *_: (0,) * len(shape))


def added(former, latter):
    return (former.astype(jnp.float32) + latter.astype(jnp.float32)).astype(jnp.bfloat16)


def split(value):
    half = value.shape[0] // 2
    return value[half:], value[:half]


def fold_kernel(plan, *refs):
    count = len(refs) - len(plan)
    for terms, target in zip(plan, refs[count:], strict=True):
        for place, size, coded, sources in terms:
            if coded:
                values = sum(decoded(refs[number][start]) for number, start in sources)
                target[place] = encoded(values)
            elif len(sources) == 1:
                number, start = sources[0]
                target[place : place + size] = refs[number][start : start + size]
            else:
                values = sum(refs[number][start : start + size].astype(jnp.float32) for number, start in sources)
                target[place : place + size] = low(values)


def fold(outs, order, name):
    arrays, plan, shapes = [], [], []
    for out in outs:
        place, terms = 0, []
        for size, *sources in out:
            numbered = []
            for array, start in sources:
                found = [n for n, other in enumerate(arrays) if other is array]
                if not found:
                    arrays.append(array)
                numbered.append((found[0] if found else len(arrays) - 1, start))
            terms.append((place, max(size, 1), size == 0, tuple(numbered)))
            place += max(size, 1)
        plan.append(tuple(terms))
        shapes.append(shaped((place,) + arrays[0].shape[1:], jnp.bfloat16))
    return whole(functools.partial(fold_kernel, plan), name, (), arrays, shapes, [], 0, carry=(order,), limit=FOLD_LIMIT)


def exchange_each(values, step, sizes):
    orders, _ = halving_orders(sizes[1])
    return [exchange(values[i], orders[i][step], sizes) for i in range(THIRDS)]


def spread_kernel(kind, batch_size, numbers, *refs):
    sources, targets = refs[: 2 * THIRDS], refs[2 * THIRDS :]
    core = numbers[1] & 1
    labels = labels_of(numbers[0], numbers[1], batch_size)
    _, rows, third = sources[0].shape
    rows = rows // 2
    for matrix in range(4):

        def put(first, matrix=matrix):
            for part in range(THIRDS):
                for own in range(4):
                    value = sources[first + part][own ^ (labels[part] & 3), (matrix % 2) * rows : (matrix % 2 + 1) * rows]
                    value = value.astype(jnp.float32)
                    at, columns = slice(own * rows, (own + 1) * rows), slice(part * third, (part + 1) * third)
                    if kind == "tall":
                        targets[0][matrix, at, columns] = value
                    elif kind == "wide":
                        start = (matrix * THIRDS + part) * third
                        targets[0][at, start : start + third] = value
                    else:
                        targets[matrix][at, columns] = value

        @pl.when(core == matrix // 2)
        def _():
            put(0)

        @pl.when(core != matrix // 2)
        def _():
            put(THIRDS)


def spread(numbers, blocks, kind, name, sizes, **waits):
    third = blocks[0].shape[2]
    width = THIRDS * third
    rows = 2 * width // LABELS
    group = 2 * rows

    groups = LABELS // 4

    def source_spec(part):
        def at(i, numbers):
            return ((i ^ (labels_of(numbers[0], numbers[1], sizes[1])[part] >> 2)) + part * groups, 0, 0)

        return pl.BlockSpec((4, rows, third), at)

    if kind == "tall":
        specs = [pl.BlockSpec((4, group, width), lambda i, *_: (0, i, 0))]
        shapes = [shaped((4, width, width), jnp.float32)]
    elif kind == "wide":
        specs = [pl.BlockSpec((group, 4 * width), lambda i, *_: (i, 0))]
        shapes = [shaped((width, 4 * width), jnp.float32)]
    else:
        specs = [pl.BlockSpec((group, width), lambda i, *_: (i, 0))] * 4
        shapes = [shaped((width, width), jnp.float32)] * 4
    return call(
        functools.partial(spread_kernel, kind, sizes[1]),
        name,
        (LABELS // 4,),
        [source_spec(part % THIRDS) for part in range(2 * THIRDS)],
        specs, shapes, [],
        0,
        24 * width * width,
        (numbers,), *[blocks[0]] * THIRDS, *[blocks[1]] * THIRDS, **waits,
    )


def gather_embeddings(own, sizes):
    orders = gather_orders(sizes[1])
    value = own[None]
    for even_dim, odd_dim in zip(*orders, strict=True):
        value = jnp.concatenate([value, exchange(value, even_dim, sizes, odd_dim)], axis=0)
    return value, exchange(value, CORE, sizes)


BAND = 64
STEP = 128
WINDOW = STEP + 2 * BAND
QUERY_BIAS, VALUE_BIAS, OUTPUT_BIAS, FIRST_GAIN, FIRST_SHIFT, DOWN_BIAS, SECOND_GAIN, SECOND_SHIFT, UP_BIAS = range(9)


def dots(former, latter):
    return lax.dot_general(former, latter, (((1,), (1,)), ((), ())), preferred_element_type=jnp.float32)


def product(former, latter):
    return jnp.dot(former, latter, preferred_element_type=jnp.float32)


def transposed(former, latter):
    return lax.dot_general(former, latter, (((0,), (0,)), ((), ())), preferred_element_type=jnp.float32)


def low(values):
    return values.astype(jnp.bfloat16)


def call(kernel, name, grid, in_specs, out_specs, out_shape, scratch, flops, moved, scalars, *args, after=(), carry=(), limit=16):
    taken, given = len(scalars) + len(in_specs), len(out_specs)
    waits = len(after) + len(carry)

    def run(*refs):
        kernel(*refs[:taken], *refs[taken + waits : taken + waits + given], *refs[taken + waits + given + len(carry) :])

    anywhere = pl.BlockSpec(memory_space=pl.ANY)
    return pl.pallas_call(
        run,
        grid_spec=pltpu.PrefetchScalarGridSpec(
            num_scalar_prefetch=len(scalars),
            grid=grid,
            in_specs=list(in_specs) + [anywhere] * waits,
            out_specs=list(out_specs) + [anywhere] * len(carry),
            scratch_shapes=scratch,
        ),
        out_shape=list(out_shape) + [shaped(value.shape, value.dtype) for value in carry],
        input_output_aliases={taken + len(after) + i: given + i for i in range(len(carry))},
        compiler_params=pltpu.CompilerParams(vmem_limit_bytes=limit * MIB),
        cost_estimate=pl.CostEstimate(flops=flops, bytes_accessed=moved, transcendentals=0),
        name=name,
    )(*scalars, *args, *after, *carry)


def whole(kernel, name, scalars, args, outs, scratch, flops, after=(), carry=(), far=(), far_outs=(), limit=12):
    taken, given = len(scalars) + len(args), len(outs)
    waits = len(after) + len(carry)

    def run(*refs):
        kernel(*refs[:taken], *refs[taken + waits : taken + waits + given], *refs[taken + waits + given + len(carry) :])

    near, remote = pl.BlockSpec(memory_space=pltpu.VMEM), pl.BlockSpec(memory_space=pltpu.HBM)
    anywhere = pl.BlockSpec(memory_space=pl.ANY)
    moved = sum(a.size * a.dtype.itemsize for a in args) + sum(o.size * o.dtype.itemsize for o in outs)
    args = [pltpu.with_memory_space_constraint(a, pltpu.HBM) if i in far else a for i, a in enumerate(args)]
    out_shape = [pltpu.HBM(o.shape, o.dtype) if i in far_outs else o for i, o in enumerate(outs)]
    return pl.pallas_call(
        run,
        in_specs=[pl.BlockSpec(memory_space=pltpu.SMEM)] * len(scalars)
        + [remote if i in far else near for i in range(len(args))]
        + [anywhere] * waits,
        out_specs=[remote if i in far_outs else near for i in range(given)] + [anywhere] * len(carry),
        out_shape=out_shape + [shaped(value.shape, value.dtype) for value in carry],
        scratch_shapes=scratch,
        input_output_aliases={taken + len(after) + i: given + i for i in range(len(carry))},
        compiler_params=pltpu.CompilerParams(vmem_limit_bytes=limit * MIB),
        cost_estimate=pl.CostEstimate(flops=flops, bytes_accessed=moved, transcendentals=0),
        name=name,
    )(*scalars, *args, *after, *carry)


def shaped(shape, dtype):
    return jax.ShapeDtypeStruct(shape, dtype)


def rows_spec(rows, width):
    return pl.BlockSpec((rows, width), lambda i, *_: (i, 0))


def segment_of(lengths, row, count, shape, dim):
    place = lax.broadcasted_iota(jnp.int32, shape, dim)
    total, ids = 0, jnp.zeros(shape, jnp.int32)
    for j in range(count):
        total = total + lengths[row, j]
        ids = ids + (place >= total).astype(jnp.int32)
    return ids


def window_start(block, span):
    return min(max(block * STEP - BAND, 0), span - WINDOW)


def fill_bias(lengths, row, count, span, bias_ref, first=0):
    down = segment_of(lengths, row, count, (span, 128), 0)
    along = segment_of(lengths, row, count, (8, span), 1)
    for block in range(span // STEP):
        start = window_start(block, span)
        same = down[block * STEP : (block + 1) * STEP, 0:1] == along[0:1, start : start + WINDOW]
        bias_ref[first + block] = jnp.where(same, 0.0, -1e9)


def head_masks(scale):
    lane = lax.broadcasted_iota(jnp.int32, (1, 2 * HEAD_DIM), 1)
    first = low(jnp.where(lane < HEAD_DIM, scale, 0.0))
    second = low(jnp.where(lane < HEAD_DIM, 0.0, scale))
    return first, second


def stacked(values, masks):
    return jnp.concatenate([values * masks[0], values * masks[1]], axis=0)


def merged(values):
    lane = lax.broadcasted_iota(jnp.int32, (STEP, 2 * HEAD_DIM), 1)
    return jnp.where(lane < HEAD_DIM, values[:STEP], values[STEP:])


def biased(scores, bias):
    return (scores.reshape(2, STEP, WINDOW) + bias[None]).reshape(2 * STEP, WINDOW)


def normalised(values):
    centred = values - jnp.mean(values, axis=-1, keepdims=True)
    factor = lax.rsqrt(jnp.mean(centred * centred, axis=-1, keepdims=True) + 1e-12)
    return centred * factor, factor


def norm_back(gradient, normed, factor, gain):
    inner = gradient * gain
    centred = inner - jnp.mean(inner, axis=-1, keepdims=True)
    return factor * (centred - normed * jnp.mean(inner * normed, axis=-1, keepdims=True))


def contrast_kernel(scale, sizes, numbers, lengths, own_ref, foreign_ref, pooled_ref, terms_ref, grad_ref, all_ref, digits_ref, totals_ref):
    half, texts, wide = own_ref.shape
    width = pooled_ref.shape[1]
    total = all_ref.shape[1]
    stream, batch = numbers[0], numbers[1]
    orders = gather_orders(sizes[1])

    def place(source, from_stream, from_batch, i):
        at = pl.multiple_of(from_batch * texts, texts)
        other = from_stream ^ stream
        all_ref[other, pl.ds(at, texts)] = source[i, :, :width]

        @pl.when(other == 1)
        def _():
            digits_ref[pl.ds(at, texts)] = source[i, :, width:]

    def place_both(i, carry):
        place(own_ref, *place_at(*orders, i, (stream, batch)), i)
        place(foreign_ref, *place_at(*orders, i, (stream, batch ^ 1)), i)
        return carry

    lax.fori_loop(0, half, place_both, 0)

    tile = min(TILE, total)
    totals_ref[...] = jnp.zeros_like(totals_ref)
    for column in range(total // tile):
        latter = all_ref[1, column * tile : (column + 1) * tile]

        def add(i, carry, latter=latter, column=column):
            former = all_ref[0, pl.ds(pl.multiple_of(i * tile, tile), tile)]
            sums = jnp.sum(jnp.exp(dots(former, latter) / 0.05), axis=0, keepdims=True)
            totals_ref[:, column * tile : (column + 1) * tile] += sums
            return carry

        lax.fori_loop(0, total // tile, add, 0)
    mine = all_ref[0, pl.ds(pl.multiple_of(batch * texts, texts), texts)]
    partners = all_ref[1]
    own_digits = own_ref[0, :, width:]
    logits = dots(mine, partners) / 0.05
    exponent = jnp.exp(logits)
    row_total = jnp.sum(exponent, axis=1, keepdims=True)
    own_target = (64.0 * own_digits[:, 0:1].astype(jnp.float32) + own_digits[:, 1:2].astype(jnp.float32)).astype(jnp.int32)
    lane = lax.broadcasted_iota(jnp.int32, (8, 128), 1)
    pick = jnp.where(lane == 0, 64.0, jnp.where(lane == 1, 1.0, 0.0)).astype(jnp.bfloat16)
    all_target = dots(pick, digits_ref[...])[0:1].astype(jnp.int32)
    columns = lax.broadcasted_iota(jnp.int32, (texts, total), 1)
    rows = batch * texts + lax.broadcasted_iota(jnp.int32, (texts, total), 0)
    query_hit = (own_target == columns).astype(jnp.float32)
    doc_hit = (all_target == rows).astype(jnp.float32)
    target = jnp.where(stream == 0, query_hit, doc_hit)
    chosen = jnp.sum(logits * target, axis=1, keepdims=True)
    terms_ref[...] = jnp.broadcast_to(jnp.log(row_total) - chosen, terms_ref.shape)
    own_low = ((exponent / row_total - target) * scale).astype(jnp.bfloat16)
    cross_low = ((exponent / totals_ref[0:1, :] - target) * scale).astype(jnp.bfloat16)
    gradient = (
        jnp.dot(own_low, partners, preferred_element_type=jnp.float32)
        + jnp.dot(cross_low, partners, preferred_element_type=jnp.float32)
    ) / 0.05
    gradient = gradient.astype(jnp.bfloat16).astype(jnp.float32)
    pooled = pooled_ref[...]
    inverse_norm = lax.rsqrt(jnp.sum(pooled * pooled, axis=1, keepdims=True) + 1e-06)
    embedding = pooled * inverse_norm
    inner = jnp.sum(gradient * embedding, axis=1, keepdims=True)
    count = texts // lengths.shape[0]
    divisor = jnp.concatenate([length_column(lengths, row, count) for row in range(lengths.shape[0])], axis=0)
    grad_ref[...] = inverse_norm * (gradient - embedding * inner) / divisor


def contrast(numbers, lengths, own, foreign, pooled, sizes):
    _, texts, wide = own.shape
    width = pooled.shape[1]
    total = sizes[1] * texts
    terms, gradient = whole(
        functools.partial(contrast_kernel, 1.0 / (2.0 * total), sizes),
        "contrast",
        (numbers, lengths),
        (own, foreign, pooled),
        [shaped((texts, 128), jnp.float32), shaped(pooled.shape, jnp.float32)],
        [
            pltpu.VMEM((2, total, width), jnp.bfloat16),
            pltpu.VMEM((total, wide - width), jnp.bfloat16),
            pltpu.VMEM((8, total), jnp.float32),
        ],
        2 * total * total * width,
        limit=max(12, 8 + total * width // 2**16),
    )
    return terms[:, 0], gradient


def attend_kernel(count, lengths, x_in, wq_in, wk_in, wv_in, wo_in, *refs):
    vectors_in, refs = refs[:9], refs[9:]
    q_out, k_out, v_out, ctx_out, aux_out, vec_ref, normed_ref, hidden_ref = refs[:8]
    x_ref, w_ref, wide_ref, q_ref, k_ref, v_ref, ctx_ref, aux_ref, bias_ref, sems = refs[8:]
    tokens, width = x_ref.shape
    row_count = lengths.shape[0]
    span = tokens // row_count
    places, at = [], 0
    for vector in vectors_in:
        places.append(at)
        at += vector.shape[0]
    loads = [pltpu.make_async_copy(x_in, x_ref, sems.at[0]), pltpu.make_async_copy(wq_in, w_ref.at[0], sems.at[1])]
    small = [
        pltpu.make_async_copy(vector, wide_ref.at[pl.ds(place, vector.shape[0])], sems.at[5 + i])
        for i, (vector, place) in enumerate(zip(vectors_in, places, strict=True))
    ]
    loads += [pltpu.make_async_copy(w, w_ref.at[i], sems.at[1 + i]) for i, w in ((1, wk_in), (2, wv_in), (3, wo_in))]
    for copy in loads[:2] + small + loads[2:]:
        copy.start()
    for row in range(row_count):
        fill_bias(lengths, row, count, span, bias_ref, row * (span // STEP))
    for copy in small:
        copy.wait()
    flat = wide_ref[...].astype(jnp.float32)
    for row in range(vec_ref.shape[0]):
        vec_ref[row : row + 1] = flat[row * width : (row + 1) * width].reshape(1, width)
    loads[0].wait()
    stores = [
        pltpu.make_async_copy(ref, out, sems.at[14 + i])
        for i, (ref, out) in enumerate(
            ((q_ref, q_out), (k_ref, k_out), (v_ref, v_out), (ctx_ref, ctx_out), (aux_ref, aux_out))
        )
    ]
    for i, (ref, bias) in enumerate(((q_ref, QUERY_BIAS), (k_ref, None), (v_ref, VALUE_BIAS))):
        loads[1 + i].wait()
        for row in range(row_count):
            rows = slice(row * span, (row + 1) * span)
            values = product(x_ref[rows], w_ref[i])
            ref[rows] = low(values if bias is None else values + vec_ref[bias : bias + 1])
        stores[i].start()
    masks = head_masks(HEAD_DIM**-0.5)
    aux_ref[...] = jnp.zeros_like(aux_ref)
    pairs = width // (2 * HEAD_DIM)

    def heads(step, carry):
        row, pair = step // pairs, step % pairs
        at = pl.ds(pl.multiple_of(pair * 2 * HEAD_DIM, 2 * HEAD_DIM), 2 * HEAD_DIM)
        lane = lax.broadcasted_iota(jnp.int32, (STEP, 128), 1)
        blocks = range(span // STEP)
        rows = [pl.ds(pl.multiple_of(row * span + block * STEP, STEP), STEP) for block in blocks]
        keys = [pl.ds(pl.multiple_of(row * span + window_start(block, span), BAND), WINDOW) for block in blocks]
        scores = [dots(stacked(q_ref[rows[b], at], masks), k_ref[keys[b], at]) for b in blocks]
        scores = [biased(scores[b], bias_ref[row * (span // STEP) + b]) for b in blocks]
        highest = [jnp.max(value, axis=1, keepdims=True) for value in scores]
        exponent = [jnp.exp(scores[b] - highest[b]) for b in blocks]
        total = [jnp.sum(value, axis=1, keepdims=True) for value in exponent]
        attention = [low(exponent[b] * (1.0 / total[b])) for b in blocks]
        for b in blocks:
            ctx_ref[rows[b], at] = low(merged(product(attention[b], v_ref[keys[b], at])))
        for b in blocks:
            log_total = highest[b] + jnp.log(total[b])
            kept = jnp.where(lane == 2 * pair, log_total[:STEP], aux_ref[rows[b]])
            aux_ref[rows[b]] = jnp.where(lane == 2 * pair + 1, log_total[STEP:], kept)
        return carry

    lax.fori_loop(0, row_count * pairs, heads, 0)
    stores[3].start()
    loads[4].wait()
    for row in range(row_count):
        rows = slice(row * span, (row + 1) * span)
        attended = product(ctx_ref[rows], w_ref[3]) + vec_ref[OUTPUT_BIAS : OUTPUT_BIAS + 1]
        normed, factor = normalised(x_ref[rows].astype(jnp.float32) + attended)
        normed_ref[rows] = normed
        hidden_ref[rows] = low(normed * vec_ref[FIRST_GAIN : FIRST_GAIN + 1] + vec_ref[FIRST_SHIFT : FIRST_SHIFT + 1])
        lane = lax.broadcasted_iota(jnp.int32, (span, 128), 1)
        aux_ref[rows] = jnp.where(lane == 127, factor, aux_ref[rows])
    stores[4].start()
    for copy in stores:
        copy.wait()


def attend(lengths, x, weights, vectors):
    tokens, width = x.shape
    row_count = lengths.shape[0]
    span = tokens // row_count
    vector_rows = sum(vector.shape[0] for vector in vectors) // width
    square = shaped((tokens, width), jnp.bfloat16)
    token_scratch = pltpu.VMEM((tokens, width), jnp.bfloat16)
    return whole(
        functools.partial(attend_kernel, lengths.shape[1]),
        "attend",
        (lengths,),
        (x, *weights, *vectors),
        [square] * 4
        + [
            shaped((tokens, 128), jnp.float32),
            shaped((vector_rows, width), jnp.float32),
            shaped((tokens, width), jnp.float32),
            square,
        ],
        [token_scratch, pltpu.VMEM((4, width, width), jnp.bfloat16), pltpu.VMEM((vector_rows * width,), jnp.bfloat16)]
        + [token_scratch] * 4
        + [pltpu.VMEM((tokens, 128), jnp.float32)]
        + [pltpu.VMEM((row_count * span // STEP, STEP, WINDOW), jnp.float32), pltpu.SemaphoreType.DMA((19,))],
        8 * tokens * width * width + 4 * tokens * WINDOW * width,
        far=range(5 + len(vectors)),
        far_outs=range(5),
        limit=24,
    )


def gelu_and_slope(values):
    size = jnp.abs(values)
    part = 1.0 / (1.0 + (0.3275911 * 0.5**0.5) * size)
    bell = jnp.exp(values * values * -0.5)
    series = part * (0.5 * 0.254829592 + part * (-0.5 * 0.284496736 + part * (0.5 * 1.421413741 + part * (-0.5 * 1.453152027 + part * (0.5 * 1.061405429)))))
    tail = series * bell
    share = jnp.where(values < 0.0, tail, 1.0 - tail)
    return values * share, share + values * bell * 0.3989422804014327


def two_parts(values):
    high = low(values)
    return high, low(values - high.astype(jnp.float32))


def membership(lengths, row, count, rows, offset):
    place = lax.broadcasted_iota(jnp.int32, (count, rows), 1) + offset
    text = lax.broadcasted_iota(jnp.int32, (count, rows), 0)
    total = 0
    inside = jnp.zeros((count, rows), jnp.float32)
    for j in range(count):
        start, total = total, total + lengths[row, j]
        inside = jnp.where((text == j) & (place >= start) & (place < total), 1.0, inside)
    return low(inside)


def length_column(lengths, row, count):
    text = lax.broadcasted_iota(jnp.int32, (count, 128), 0)
    column = jnp.zeros((count, 128), jnp.float32)
    for j in range(count):
        column = jnp.where(text == j, lengths[row, j].astype(jnp.float32), column)
    return column[:, 0:1]


def feed_kernel(count, lengths, positives, normed_ref, hidden_ref, up_ref, down_ref, vec_ref, act_out, slope_out, second_ref, factor_ref, pooled_ref, package_ref, act_ref, slope_ref, sems):
    tokens, width = normed_ref.shape
    row_count = lengths.shape[0]
    span = tokens // row_count
    rows = 256
    parts = span // rows
    pooled_ref[...] = jnp.zeros_like(pooled_ref)

    def copies(step, slot):
        here = pl.ds(pl.multiple_of(step * rows, rows), rows)
        return (
            pltpu.make_async_copy(act_ref.at[slot], act_out.at[here], sems.at[0, slot]),
            pltpu.make_async_copy(slope_ref.at[slot], slope_out.at[here], sems.at[1, slot]),
        )

    def block(step, carry):
        row, part = step // parts, step % parts
        here = pl.ds(pl.multiple_of(step * rows, rows), rows)
        slot = step % 2
        stores = copies(step, slot)

        @pl.when(step >= 2)
        def _():
            for copy in copies(step - 2, slot):
                copy.wait()

        hidden_low = hidden_ref[here]
        branch = jnp.zeros((rows, width), jnp.float32)
        pieces = up_ref.shape[1] // width
        spots = [slice(piece * width, (piece + 1) * width) for piece in range(pieces)]
        later = product(hidden_low, up_ref[:, spots[0]])
        done = None
        for piece, at in enumerate(spots):
            values = later + vec_ref[UP_BIAS + piece : UP_BIAS + piece + 1]
            if piece + 1 < pieces:
                later = product(hidden_low, up_ref[:, spots[piece + 1]])
            if done is not None:
                branch = branch + product(done, down_ref[spots[piece - 1]])
            activation, slope = gelu_and_slope(values)
            done = low(activation)
            act_ref[slot, :, at] = done
            slope_ref[slot, :, at] = low(slope)
        branch = branch + product(done, down_ref[spots[-1]])
        for copy in stores:
            copy.start()
        hidden = normed_ref[here] * vec_ref[FIRST_GAIN : FIRST_GAIN + 1] + vec_ref[FIRST_SHIFT : FIRST_SHIFT + 1]
        normed, factor = normalised(hidden + branch + vec_ref[DOWN_BIAS : DOWN_BIAS + 1])
        second_ref[here] = normed
        factor_ref[here] = jnp.broadcast_to(factor, (rows, 128))
        high, rest = two_parts(normed * vec_ref[SECOND_GAIN : SECOND_GAIN + 1] + vec_ref[SECOND_SHIFT : SECOND_SHIFT + 1])
        inside = membership(lengths, row, count, rows, part * rows)
        texts = pl.ds(pl.multiple_of(row * count, count), count)
        pooled_ref[texts] += product(inside, high) + product(inside, rest)
        return carry

    lax.fori_loop(0, tokens // rows, block, 0)
    text = lax.broadcasted_iota(jnp.int32, (count, 128), 0)
    lane = lax.broadcasted_iota(jnp.int32, (count, 128), 1)
    for row in range(row_count):
        texts = slice(row * count, (row + 1) * count)
        pooled = pooled_ref[texts] / length_column(lengths, row, count)
        pooled_ref[texts] = pooled
        inverse_norm = lax.rsqrt(jnp.sum(pooled * pooled, axis=1, keepdims=True) + 1e-06)
        package_ref[texts, :width] = low(pooled * inverse_norm)
        digits = jnp.zeros((count, 128), jnp.int32)
        for j in range(count):
            own = positives[row * count + j]
            digits = jnp.where(text == j, jnp.where(lane == 0, own >> 6, own & 63), digits)
        package_ref[texts, width:] = low(jnp.where(lane < 2, digits, 0).astype(jnp.float32))
    steps = tokens // rows
    for step in range(steps - 2, steps):
        for copy in copies(step, step % 2):
            copy.wait()


def feed(lengths, positives, normed, hidden_low, up, down, vec):
    tokens, width = normed.shape
    texts, hidden = lengths.size, up.shape[1]
    return whole(
        functools.partial(feed_kernel, lengths.shape[1]),
        "feed",
        (lengths, positives),
        (normed, hidden_low, up, down, vec),
        [
            shaped((tokens, hidden), jnp.bfloat16),
            shaped((tokens, hidden), jnp.bfloat16),
            shaped((tokens, width), jnp.float32),
            shaped((tokens, 128), jnp.float32),
            shaped((texts, width), jnp.float32),
            shaped((texts, width + 128), jnp.bfloat16),
        ],
        [pltpu.VMEM((2, 256, hidden), jnp.bfloat16)] * 2 + [pltpu.SemaphoreType.DMA((2, 2))],
        4 * tokens * width * hidden,
        far_outs=(0, 1),
        limit=16,
    )


def sums_of(values):
    return jnp.sum(values, axis=0, keepdims=True)


def second_back_kernel(count, lengths, grad_ref, normed_ref, factor_ref, vec_ref, sum_ref, low_ref, totals_ref):
    tokens, width = normed_ref.shape
    row_count = lengths.shape[0]
    span = tokens // row_count
    totals_ref[...] = jnp.zeros_like(totals_ref)
    for row in range(row_count):
        rows = slice(row * span, (row + 1) * span)
        inside = membership(lengths, row, count, span, 0)
        high, rest = two_parts(grad_ref[row * count : (row + 1) * count])
        result_grad = transposed(inside, high) + transposed(inside, rest)
        normed = normed_ref[rows]
        second_sum = norm_back(result_grad, normed, factor_ref[rows, 0:1], vec_ref[SECOND_GAIN : SECOND_GAIN + 1])
        branch_grad = low(second_sum)
        sum_ref[rows] = second_sum
        low_ref[rows] = branch_grad
        totals_ref[0:1] += sums_of(branch_grad.astype(jnp.float32))
        totals_ref[1:2] += sums_of(result_grad * normed)
        totals_ref[2:3] += sums_of(result_grad)


def second_back(lengths, grad, normed, factor, vec):
    tokens, width = normed.shape
    return whole(
        functools.partial(second_back_kernel, lengths.shape[1]),
        "second_norm_back",
        (lengths,),
        (grad, normed, factor, vec),
        [shaped((tokens, width), jnp.float32), shaped((tokens, width), jnp.bfloat16), shaped((8, width), jnp.float32)],
        [],
        8 * tokens * width,
    )


def matrix_at(place, foreign, numbers):
    return 2 * ((numbers[1] & 1) ^ foreign) + place


def put_rows(numbers, sizes, sides, out_ref, place, group=8):
    labels = labels_of(numbers[0], numbers[1], sizes[1])
    rows, third = out_ref.shape[2] // 2, out_ref.shape[3]
    for first in range(0, LABELS, group):
        piece = low(sum(transposed(left(first * rows, group * rows), right) for left, right in sides))
        for own in range(group):
            for part in range(THIRDS):
                value = piece[own * rows : (own + 1) * rows, part * third : (part + 1) * third]
                out_ref[part, (first + own) ^ labels[part], place * rows : (place + 1) * rows] = value


def columns(ref):
    return lambda at, size: ref[:, at : at + size]


def blocks_out(width):
    return shaped((THIRDS, LABELS, 2 * width // LABELS, width // THIRDS), jnp.bfloat16)


def column_loads(source, target, foreign, numbers, sems):
    width = target.shape[2]
    copies = []
    for place in range(2):
        at = pl.ds(pl.multiple_of(matrix_at(place, foreign, numbers) * width, width), width)
        copies.append(pltpu.make_async_copy(source.at[:, at], target.at[place], sems.at[place]))
    return copies


def down_weight_kernel(foreign, sizes, numbers, act_in, grad_ref, out_ref, act_ref, sems):
    loads = column_loads(act_in, act_ref, foreign, numbers, sems)
    for copy in loads:
        copy.start()
    for place in range(2):
        loads[place].wait()
        put_rows(numbers, sizes, [(columns(act_ref.at[place]), grad_ref[...])], out_ref, place)


def down_weight(numbers, activation, grad, foreign, sizes, name, **waits):
    tokens, width = grad.shape
    return whole(
        functools.partial(down_weight_kernel, foreign, sizes),
        name,
        (numbers,), (activation, grad), [blocks_out(width)],
        [pltpu.VMEM((2, tokens, width), jnp.bfloat16), pltpu.SemaphoreType.DMA((2,))],
        4 * tokens * width * width,
        far=(0,),
        **waits,
    )


def up_back_kernel(foreign, sizes, numbers, grad_ref, slope_in, hidden_ref, up_ref, down_ref, before_ref, *refs):
    if foreign:
        out_ref, after_ref, totals_ref, pre_ref, slope_ref, sems = refs
    else:
        normed_ref, aux_ref, vec_ref, out_ref, totals_ref, first_ref, low_ref, sums_ref, pre_ref, slope_ref, sems = refs
        after_ref = first_ref
    width = grad_ref.shape[1]
    loads = column_loads(slope_in, slope_ref, foreign, numbers, sems)
    for copy in loads:
        copy.start()
    for place in range(2):
        at = pl.ds(pl.multiple_of(matrix_at(place, foreign, numbers) * width, width), width)
        active_grad = dots(grad_ref[...], down_ref[at])
        loads[place].wait()
        pre_grad = low(active_grad * slope_ref[place].astype(jnp.float32))
        pre_ref[...] = pre_grad
        totals_ref[place] = jnp.broadcast_to(sums_of(pre_grad.astype(jnp.float32)), totals_ref.shape[1:])
        before = before_ref if place == 0 else after_ref
        after_ref[...] = before[...] + dots(pre_ref[...], up_ref[:, at])
        put_rows(numbers, sizes, [(columns(hidden_ref), pre_ref[...])], out_ref, place)
    if foreign:
        return
    hidden_grad, normed = after_ref[...], normed_ref[...]
    first_sum = norm_back(hidden_grad, normed, aux_ref[:, 127:128], vec_ref[FIRST_GAIN : FIRST_GAIN + 1])
    attended_grad = low(first_sum)
    first_ref[...] = first_sum
    low_ref[...] = attended_grad
    sums_ref[...] = jnp.zeros_like(sums_ref)
    sums_ref[0:1] = sums_of(attended_grad.astype(jnp.float32))
    sums_ref[1:2] = sums_of(hidden_grad * normed)
    sums_ref[2:3] = sums_of(hidden_grad)


def up_back(numbers, grad, slope, hidden_low, up, down, before, foreign, sizes, name, rest=(), **waits):
    tokens, width = grad.shape
    wide = shaped((tokens, width), jnp.float32)
    totals = shaped((2, 8, width), jnp.float32)
    pre = [
        pltpu.VMEM((tokens, width), jnp.bfloat16),
        pltpu.VMEM((2, tokens, width), jnp.bfloat16),
        pltpu.SemaphoreType.DMA((2,)),
    ]
    if foreign:
        outs, scratch = [blocks_out(width), wide, totals], pre
    else:
        outs = [blocks_out(width), totals, wide, shaped((tokens, width), jnp.bfloat16), shaped((8, width), jnp.float32)]
        scratch = pre
    return whole(
        functools.partial(up_back_kernel, foreign, sizes),
        name,
        (numbers,), (grad, slope, hidden_low, up, down, before, *rest), outs, scratch,
        12 * tokens * width * width,
        far=(1,),
        limit=12,
        **waits,
    )


def attend_back_kernel(count, row, half, lengths, q_ref, k_ref, v_ref, grad_ref, wo_ref, aux_ref, *refs):
    out_ref, totals_ref, bias_ref, ctx_ref, dk_ref, dv_ref = refs[-6:]
    width = q_ref.shape[1]
    span = q_ref.shape[0] // lengths.shape[0]
    base = row * span
    grad = grad_ref[base : base + span]
    part = width // 2
    ctx_ref[...] = low(dots(grad, wo_ref[half * part : (half + 1) * part]))
    fill_bias(lengths, row, count, span, bias_ref)
    scale = HEAD_DIM**-0.5
    scaled, plain = head_masks(scale), head_masks(1.0)
    dk_ref[...] = jnp.zeros_like(dk_ref)
    dv_ref[...] = jnp.zeros_like(dv_ref)

    def heads(pair, carry):
        at = pl.ds(pl.multiple_of(pair * 2 * HEAD_DIM, 2 * HEAD_DIM), 2 * HEAD_DIM)
        own = pl.ds(pl.multiple_of(pair * 2 * HEAD_DIM - half * part, 2 * HEAD_DIM), 2 * HEAD_DIM)
        lane = lax.broadcasted_iota(jnp.int32, (STEP, 128), 1)
        blocks = range(span // STEP)
        rows = [pl.ds(block * STEP, STEP) for block in blocks]
        keys = [pl.ds(window_start(block, span), WINDOW) for block in blocks]
        own_rows = [pl.ds(base + block * STEP, STEP) for block in blocks]
        own_keys = [pl.ds(base + window_start(block, span), WINDOW) for block in blocks]
        queries = [stacked(q_ref[own_rows[b], at], scaled) for b in blocks]
        context_grad = [stacked(ctx_ref[rows[b], own], plain) for b in blocks]
        scores = [dots(queries[b], k_ref[own_keys[b], at]) for b in blocks]
        prob_grad = [dots(context_grad[b], v_ref[own_keys[b], at]) for b in blocks]
        log_total = [
            jnp.concatenate(
                [
                    jnp.sum(jnp.where(lane == 2 * pair + side, aux_ref[own_rows[b]], 0.0), axis=1, keepdims=True)
                    for side in range(2)
                ],
                axis=0,
            )
            for b in blocks
        ]
        attention = [jnp.exp(biased(scores[b], bias_ref[b]) - log_total[b]) for b in blocks]
        inner = [jnp.sum(attention[b] * prob_grad[b], axis=1, keepdims=True) for b in blocks]
        score_grad = [low(attention[b] * (prob_grad[b] - inner[b])) for b in blocks]
        for b in blocks:
            out_ref[0, rows[b], at] = low(merged(product(score_grad[b], k_ref[own_keys[b], at])) * scale)
        for b in blocks:
            dk_ref[keys[b], own] += transposed(score_grad[b], queries[b])
        for b in blocks:
            dv_ref[keys[b], own] += transposed(low(attention[b]), context_grad[b])
        return carry

    pairs = part // (2 * HEAD_DIM)
    lax.fori_loop(half * pairs, (half + 1) * pairs, heads, 0)
    out_ref[1, :, half * part : (half + 1) * part] = low(dk_ref[...])
    out_ref[2, :, half * part : (half + 1) * part] = low(dv_ref[...])
    if half == 0:
        return
    out_ref[:, :, :part] = refs[0][:, :, :part]

    totals_ref[...] = jnp.zeros_like(totals_ref)
    totals_ref[0:1] = sums_of(out_ref[0].astype(jnp.float32))
    totals_ref[1:2] = sums_of(out_ref[2].astype(jnp.float32))


def attend_back(lengths, q, k, v, grad, wo, aux, row, half, before=None, **waits):
    tokens, width = q.shape
    span = tokens // lengths.shape[0]
    return whole(
        functools.partial(attend_back_kernel, lengths.shape[1], row, half),
        "attend_back",
        (lengths,),
        (q, k, v, grad, wo, aux) + (() if before is None else (before,)),
        [shaped((3, span, width), jnp.bfloat16), shaped((8, width), jnp.float32)],
        [
            pltpu.VMEM((span // STEP, STEP, WINDOW), jnp.float32),
            pltpu.VMEM((span, width // 2), jnp.bfloat16),
            pltpu.VMEM((span, width // 2), jnp.float32),
            pltpu.VMEM((span, width // 2), jnp.float32),
        ],
        span * width * width + 5 * span * WINDOW * width,
        **waits,
    )


def mixed_weight_kernel(foreign, sizes, numbers, x_ref, ctx_ref, grad_ref, one_ref, other_ref, out_ref):
    span = one_ref.shape[1]

    def put(left, matrix, place):
        if matrix == 3:
            put_rows(numbers, sizes, [(columns(ctx_ref), grad_ref[...])], out_ref, place)
            return
        first = lambda at, size: left[:span, at : at + size]
        second = lambda at, size: left[span:, at : at + size]
        put_rows(numbers, sizes, [(first, one_ref[matrix]), (second, other_ref[matrix])], out_ref, place)

    for pair in range(2):

        @pl.when(matrix_at(0, foreign, numbers) == 2 * pair)
        def _(pair=pair):
            put(x_ref, 2 * pair, 0)
            put(x_ref, 2 * pair + 1, 1)


def mixed_weight(numbers, x, context, grad, grads, foreign, sizes, name, **waits):
    tokens, width = x.shape
    return whole(
        functools.partial(mixed_weight_kernel, foreign, sizes),
        name,
        (numbers,), (x, context, grad, *grads), [blocks_out(width)], [],
        4 * tokens * width * width,
        **waits,
    )


def input_kernel(steps, first_ref, one_ref, other_ref, wq_ref, wk_ref, wv_ref, out_ref):
    def put(grad_ref):
        out_ref[...] = first_ref[...] + dots(grad_ref[0], wq_ref[...]) + dots(grad_ref[1], wk_ref[...]) + dots(grad_ref[2], wv_ref[...])

    @pl.when(pl.program_id(0) < steps)
    def _():
        put(one_ref)

    @pl.when(pl.program_id(0) >= steps)
    def _():
        put(other_ref)


def input_back(first_sum, grads, weights, **waits):
    tokens, width = first_sum.shape
    rows = 256
    steps = grads[0].shape[1] // rows
    one = pl.BlockSpec((3, rows, width), lambda i, *_: (0, jnp.minimum(i, steps - 1), 0))
    other = pl.BlockSpec((3, rows, width), lambda i, *_: (0, jnp.maximum(i - steps, 0), 0))
    return call(
        functools.partial(input_kernel, steps),
        "input_grad",
        (tokens // rows,),
        [rows_spec(rows, width), one, other] + [full_spec((width, width))] * 3,
        [rows_spec(rows, width)],
        [shaped((tokens, width), jnp.float32)],
        [],
        6 * tokens * width * width,
        14 * tokens * width + 6 * width * width,
        (), first_sum, *grads, *weights, **waits,
    )


VECTOR_ROWS = 48


def encoded(values):
    high, rest = two_parts(values)
    return jnp.concatenate([high, rest], axis=0)


def decoded(block):
    block = block.astype(jnp.float32)
    return block[:VECTOR_ROWS] + block[VECTOR_ROWS:]


def bundle_kernel(numbers, first_ref, second_ref, one_ref, other_ref, send_ref, keep_ref, coded_ref, target_ref):
    width = first_ref.shape[1]
    third = target_ref.shape[1]
    pieces = width // third
    target_ref[...] = jnp.zeros_like(target_ref)

    def put(row, values):
        for piece in range(pieces):
            target_ref[pl.ds(row * pieces + piece, 1)] = values[:, piece * third : (piece + 1) * third]

    for row in range(2):
        put(row, one_ref[row : row + 1] + other_ref[row : row + 1])
    for row in range(3):
        put(2 + row, first_ref[row : row + 1])
        put(5 + row, second_ref[row : row + 1])
    for place in range(2):
        put(8 + matrix_at(place, 0, numbers), keep_ref[place, 0:1])
        put(8 + matrix_at(place, 1, numbers), send_ref[place, 0:1])
    coded_ref[0] = encoded(target_ref[...])


def bundle(numbers, first, second, one, other, send, keep, **waits):
    third = first.shape[1] // THIRDS
    return whole(
        bundle_kernel, "vector_grads", (numbers,), (first, second, one, other, send, keep),
        [shaped((1, 2 * VECTOR_ROWS, third), jnp.bfloat16)], [pltpu.VMEM((VECTOR_ROWS, third), jnp.float32)], 0, **waits,
    )


def unbundle_kernel(source_ref, *targets):
    third = source_ref.shape[2]
    values = decoded(source_ref[0])
    row = 0
    for target in targets:
        for piece in range(target.shape[0] // third):
            target[piece * third : (piece + 1) * third] = values[row : row + 1].reshape(third)
            row += 1


def unbundle(block, sizes_out, **waits):
    return whole(
        unbundle_kernel, "unbundle", (), (block,), [shaped((size,), jnp.float32) for size in sizes_out], [], 0, **waits
    )


def local(
    inputs,
    lengths,
    positives,
    query_weight,
    query_bias,
    key_weight,
    value_weight,
    value_bias,
    output_weight,
    output_bias,
    first_gain,
    first_shift,
    up_weight,
    up_bias,
    down_weight_,
    down_bias,
    second_gain,
    second_shift,
):
    row_count, row_span, width = inputs.shape[1:]
    seg_count = lengths.shape[2]
    tokens = row_count * row_span
    hidden_width = up_weight.shape[1]
    sizes = (lax.axis_size("stream"), lax.axis_size("batch"))
    rest = halving_orders(sizes[1])[1]
    x = inputs.reshape(tokens, width)
    lengths = lengths.reshape(row_count, seg_count)
    numbers = jnp.stack([lax.axis_index("stream"), lax.axis_index("batch")]).astype(jnp.int32)
    vectors = (query_bias, value_bias, output_bias, first_gain, first_shift, down_bias, second_gain, second_shift, up_bias)
    q, k, v, context, aux, vec, first_normed, hidden_low = attend(
        lengths, x, (query_weight, key_weight, value_weight, output_weight), vectors
    )
    activation, slope, second_normed, second_factor, pooled, package = feed(
        lengths, positives, first_normed, hidden_low, up_weight, down_weight_, vec
    )
    own, foreign = gather_embeddings(package, sizes)
    contrast_terms, pooled_grad = contrast(numbers, lengths, own, foreign, pooled, sizes)
    second_sum, branch_grad, second_totals = second_back(
        lengths, pooled_grad, second_normed, second_factor, vec
    )
    orders, rest = halving_orders(sizes[1])
    far = orders[0][3]
    parts = range(THIRDS)
    half = LABELS // 2

    def flat(value):
        return value.reshape((-1,) + value.shape[2:])

    def same_link(i, step, other):
        return [order[other] for order in orders].index(orders[i][step])

    def chip_sums(keep, arrived, start):
        return [[(half, (keep, i * LABELS + start), (arrived, i * LABELS + start))] for i in parts]

    def sums(kept, kept_at, arrived, arrived_at, size):
        send = (size, (kept, kept_at + size), (arrived, arrived_at + size))
        return [send], [(size, (kept, kept_at), (arrived, arrived_at))]

    def all_sums(kept, arrived, size):
        both = [sums(kept[i], 0, arrived[i], 0, size) for i in parts]
        return [one[0] for one in both], [one[1] for one in both]

    def joined(former, former_at, latter, latter_at, size):
        return [(size, (former, former_at)), (size, (latter, latter_at))]

    def for_rest(outs, order, name):
        for dim in rest:
            arrived = [exchange(array, dim, sizes) for array, _ in outs]
            *arrays, order = fold(
                [
                    [(size, (array, start), (other, start)) for size, start in terms]
                    for (array, terms), other in zip(outs, arrived, strict=True)
                ],
                order, name,
            )
            outs = [(array, terms) for array, (_, terms) in zip(arrays, outs, strict=True)]
        return [array for array, _ in outs], order

    order = second_totals
    down_send, order = down_weight(numbers, activation, branch_grad, 1, sizes, "down_weight_send", carry=(order,))
    down_in = exchange(down_send, CORE, sizes)
    down_keep, order = down_weight(numbers, activation, branch_grad, 0, sizes, "down_weight_keep", carry=(order,))
    keep, arrived = flat(down_keep), flat(down_in)
    *made, order = fold(chip_sums(keep, arrived, half) + chip_sums(keep, arrived, 0), order, "down_0")
    down_kept = made[THIRDS:]
    down_in = exchange_each(made[:THIRDS], 0, sizes)
    up_send, partial_grad, up_totals_send, order = up_back(
        numbers, branch_grad, slope, hidden_low, up_weight, down_weight_, second_sum, 1, sizes, "up_back_send",
        carry=(order,),
    )
    sends, keeps = all_sums(down_kept, down_in, 4)
    up_send = flat(up_send)
    *made, up_send, order = fold(sends + keeps + [[(THIRDS * LABELS, (up_send, 0))]], order, "down_1")
    up_in = exchange(up_send, CORE, sizes)
    down_kept = made[THIRDS:]
    down_in = exchange_each(made[:THIRDS], 1, sizes)
    up_keep, up_totals_keep, first_sum, attended_grad, first_totals, order = up_back(
        numbers, branch_grad, slope, hidden_low, up_weight, down_weight_, partial_grad, 0, sizes, "up_back_keep",
        (first_normed, aux, vec), carry=(order,),
    )
    keep, arrived = flat(up_keep), up_in
    pair = [same_link(i, 0, 2) for i in parts]
    down_sends, down_keeps = all_sums(down_kept, down_in, 2)
    sends = chip_sums(keep, arrived, half)
    *made, order = fold(
        [sends[i] + down_sends[pair[i]] for i in parts]
        + chip_sums(keep, arrived, 0)
        + [down_keeps[pair[i]] for i in parts],
        order, "up_0",
    )
    up_kept, down_kept = made[THIRDS : 2 * THIRDS], made[2 * THIRDS :]
    up_in = exchange_each(made[:THIRDS], 0, sizes)
    back = functools.partial(attend_back, lengths, q, k, v, attended_grad, output_weight, aux)
    grads_one, totals_one, order = back(0, 0, carry=(order,))
    grads_one, totals_one, order = back(0, 1, before=grads_one, carry=(order,))
    sends, keeps = all_sums(up_kept, up_in, 4)
    far_sums = [sums(down_kept[pair.index(i)], 0, up_in[pair.index(i)], half, 1) for i in parts]
    *made, down_far, down_kept, order = fold(
        sends + keeps + [sum([one[0] for one in far_sums], []), sum([one[1] for one in far_sums], [])], order, "up_1"
    )
    up_kept = made[THIRDS:]
    up_in = exchange_each(made[:THIRDS], 1, sizes)
    down_in = exchange(down_far, far, sizes)
    grads_other, totals_other, order = back(1, 0, carry=(order,))
    sends, keeps = all_sums(up_kept, up_in, 2)
    *made, down, order = fold(sends + keeps + [[(THIRDS, (down_kept, 0), (down_in, 0))]], order, "up_2")
    up_kept = made[THIRDS:]
    up_in = exchange_each(made[:THIRDS], 2, sizes)
    (down,), order = for_rest([(down, [(THIRDS, 0)])], order, "down_rest")
    down_in = exchange(down, far, sizes)
    grads_other, totals_other, order = back(1, 1, before=grads_other, carry=(order,))
    grads = (grads_one, grads_other)
    sends, keeps = all_sums(up_kept, up_in, 1)
    up_far, up_kept, *down, order = fold(
        [sum(sends, []), sum(keeps, [])] + [joined(down, i, down_in, i, 1) for i in parts], order, "up_3"
    )
    up_in = exchange(up_far, far, sizes)
    down_in = exchange_each(down, 2, sizes)
    mixed_send, order = mixed_weight(
        numbers, x, context, attended_grad, grads, 1, sizes, "mixed_weight_send", carry=(order,)
    )
    mixed_in = exchange(mixed_send, CORE, sizes)
    vector, order = bundle(
        numbers, first_totals, second_totals, totals_one, totals_other, up_totals_send, up_totals_keep, carry=(order,)
    )
    vector_in = exchange(vector, CORE, sizes)
    mixed_keep, order = mixed_weight(
        numbers, x, context, attended_grad, grads, 0, sizes, "mixed_weight_keep", carry=(order,)
    )
    keep, arrived = flat(mixed_keep), flat(mixed_in)
    code = [[(0, (vector, 0), (vector_in, 0))], [], []]
    pair = [same_link(i, 0, 1) for i in parts]
    sends = chip_sums(keep, arrived, half)
    *made, up, order = fold(
        [sends[i] + code[i] + joined(down[pair[i]], 0, down_in[pair[i]], 0, 2) for i in parts]
        + chip_sums(keep, arrived, 0)
        + [[(THIRDS, (up_kept, 0), (up_in, 0))]],
        order, "mixed_0",
    )
    mixed, mixed_kept = made[:THIRDS], made[THIRDS:]
    mixed_in = exchange_each(mixed, 0, sizes)
    (up,), order = for_rest([(up, [(THIRDS, 0)])], order, "up_rest")
    up_in = exchange(up, far, sizes)
    input_grad, order = input_back(first_sum, grads, (query_weight, key_weight, value_weight), carry=(order,))
    sends, keeps = all_sums(mixed_kept, mixed_in, 4)
    code = [[(0, (mixed[0], half), (mixed_in[0], half))], [], []]
    skip = [half + 1, half, half]
    down = [joined(mixed[i], skip[i], mixed_in[i], skip[i], 4) for i in (pair.index(j) for j in parts)]
    pair = [same_link(i, 1, 2) for i in parts]
    other = [same_link(i, 1, 0) for i in parts]
    *made, order = fold(
        [sends[i] + code[i] + joined(up, pair[i], up_in, pair[i], 1) + down[other[i]] for i in parts] + keeps,
        order, "mixed_1",
    )
    mixed, mixed_kept = made[:THIRDS], made[THIRDS:]
    mixed_in = exchange_each(mixed, 1, sizes)
    at = [(other.index(j), 7 if other.index(j) == 0 else 6) for j in parts]
    down, down_in = [(mixed[i], start) for i, start in at], [(mixed_in[i], start) for i, start in at]
    sends, keeps = all_sums(mixed_kept, mixed_in, 2)
    code = [[(0, (mixed[0], 4), (mixed_in[0], 4))], [], []]
    skip = [5, 4, 4]
    up = [joined(mixed[i], skip[i], mixed_in[i], skip[i], 2) for i in (pair.index(j) for j in parts)]
    pair = [same_link(i, 2, 1) for i in parts]
    *made, order = fold([sends[i] + code[i] + up[pair[i]] for i in parts] + keeps, order, "mixed_2")
    mixed, mixed_kept = made[:THIRDS], made[THIRDS:]
    mixed_in = exchange_each(mixed, 2, sizes)
    down, order = fold([sum([[(half, down[i]), (half, down_in[i])] for i in parts], [])], order, "down_2")
    down = [down, exchange(down, CORE, sizes)]
    code = [(0, (mixed[0], 2), (mixed_in[0], 2))]
    skip = [3, 2, 2]
    up = [joined(mixed[i], skip[i], mixed_in[i], skip[i], 4) for i in (pair.index(j) for j in parts)]
    whole_sums = sum([[(2, (mixed_kept[i], 0), (mixed_in[i], 0))] for i in parts], [])
    mixed, *up, order = fold([whole_sums + code] + up, order, "mixed_3")
    mixed_in = exchange(mixed, far, sizes)
    up_in = exchange_each(up, 0, sizes)
    down_total, order = spread(numbers, down, "tall", "down_spread", sizes, carry=(order,))
    crossed = [[(1, (mixed, 2 * i), (mixed_in, 2 * i + 1)), (1, (mixed, 2 * i + 1), (mixed_in, 2 * i))] for i in parts]
    *mixed, vector, order = fold(crossed + [[(0, (mixed, 2 * THIRDS), (mixed_in, 2 * THIRDS))]], order, "mixed_4")
    (*mixed, vector), order = for_rest(
        [(value, [(2, 0)]) for value in mixed] + [(vector, [(0, 0)])], order, "mixed_rest"
    )
    mixed_in = exchange_each(mixed, 2, sizes)
    *summed, order = unbundle(vector, [width] * 8 + [hidden_width], carry=(order,))
    up, order = fold([sum([joined(up[i], 0, up_in[i], 0, half) for i in parts], [])], order, "up_4")
    up = [up, exchange(up, CORE, sizes)]
    *mixed, order = fold([joined(mixed[i], 0, mixed_in[i], 0, 2) for i in parts], order, "mixed_5")
    mixed_in = exchange_each(mixed, 1, sizes)
    *mixed, order = fold([joined(mixed[i], 0, mixed_in[i], 0, 4) for i in parts], order, "mixed_6")
    mixed_in = exchange_each(mixed, 0, sizes)
    up_total, order = spread(numbers, up, "wide", "up_spread", sizes, carry=(order,))
    mixed, order = fold([sum([joined(mixed[i], 0, mixed_in[i], 0, half) for i in parts], [])], order, "mixed_7")
    blocks = [mixed, exchange(mixed, CORE, sizes)]
    query_total, key_total, value_total, output_total = spread(
        numbers, blocks, "separate", "mixed_spread", sizes, after=(order,)
    )
    return (
        contrast_terms.reshape(1, row_count * seg_count),
        input_grad.reshape(1, row_count, row_span, width),
        query_total,
        summed[0],
        key_total,
        value_total,
        summed[1],
        output_total,
        summed[2],
        summed[3],
        summed[4],
        up_total,
        summed[8],
        down_total.reshape(hidden_width, width),
        summed[5],
        summed[6],
        summed[7],
    )


def solution(mesh):
    return jax.shard_map(
        local,
        mesh=mesh,
        in_specs=(
            P("stream", "batch", None, None),
            P("stream", "batch", None),
            P("batch"),
            P(),
            P(),
            P(),
            P(),
            P(),
            P(),
            P(),
            P(),
            P(),
            P(),
            P(),
            P(),
            P(),
            P(),
            P(),
        ),
        out_specs=(
            P("stream", "batch"),
            P("stream", "batch", None, None),
            P(),
            P(),
            P(),
            P(),
            P(),
            P(),
            P(),
            P(),
            P(),
            P(),
            P(),
            P(),
            P(),
            P(),
            P(),
        ),
        check_vma=False,
    )
```

```python
import functools

import jax
import jax.numpy as jnp
import numpy as np
from jax import lax
from jax.experimental import pallas as pl
from jax.experimental.pallas import tpu as pltpu
from jax.sharding import PartitionSpec as P

HEAD_DIM = 64
MIB = 2**20
FOLD_LIMIT = 16
TILE = 512
LABELS = 16
THIRDS = 3
BOTH = ("stream", "batch")


def link_dims(batch_size):
    bits = batch_size.bit_length() - 1
    main = [("stream", 1), ("batch", 2), ("batch", 1 << (bits - 2)), ("batch", 3 << (bits - 2))]
    rest = [("batch", 1 << j) for j in range(2, bits - 2)]
    return main, rest


def coordinate(dim, stream, batch, batch_size):
    bits = batch_size.bit_length() - 1
    if dim[0] == "stream":
        return stream
    mask = dim[1]
    top = (batch >> (bits - 1)) & 1
    if mask == 3 << (bits - 2):
        return top
    if mask == 1 << (bits - 2):
        return ((batch >> (bits - 2)) & 1) ^ top
    return (batch >> (mask.bit_length() - 1)) & 1


def flipped(dim, stream, batch):
    return (stream ^ 1, batch) if dim[0] == "stream" else (stream, batch ^ dim[1])


def exchange(array, even_dim, sizes, odd_dim=None):
    odd_dim = odd_dim or even_dim
    pairs = []
    for stream in range(sizes[0]):
        for batch in range(sizes[1]):
            other = flipped(odd_dim if batch & 1 else even_dim, stream, batch)
            pairs.append((stream * sizes[1] + batch, other[0] * sizes[1] + other[1]))
    return lax.ppermute(array, BOTH, pairs)


CORE = ("batch", 1)


def halving_orders(batch_size):
    (x, y, a, b), rest = link_dims(batch_size)
    return ((x, y, a, b), (y, a, x, b), (a, x, y, b)), rest


def gather_orders(batch_size):
    (x, y, a, b), rest = link_dims(batch_size)
    return tuple(rest) + (b, a, x, y), tuple(rest) + (b, x, y, a)


def labels_of(stream, batch, batch_size):
    labels = []
    for order in halving_orders(batch_size)[0]:
        label = 0
        for dim in order:
            label = label * 2 + coordinate(dim, stream, batch, batch_size)
        labels.append(label)
    return labels


def place_at(order_even, order_odd, place, numbers):
    stream, batch = numbers[0], numbers[1]
    core = batch & 1
    for step, (even_dim, odd_dim) in enumerate(zip(order_even, order_odd, strict=True)):
        bit = (place >> step) & 1
        even = (bit, 0) if even_dim[0] == "stream" else (0, bit * even_dim[1])
        odd = (bit, 0) if odd_dim[0] == "stream" else (0, bit * odd_dim[1])
        stream = stream ^ jnp.where(core == 0, even[0], odd[0])
        batch = batch ^ jnp.where(core == 0, even[1], odd[1])
    return stream, batch


def full_spec(shape):
    return pl.BlockSpec(shape, lambda *_: (0,) * len(shape))


def added(former, latter):
    return (former.astype(jnp.float32) + latter.astype(jnp.float32)).astype(jnp.bfloat16)


def split(value):
    half = value.shape[0] // 2
    return value[half:], value[:half]


def fold_kernel(plan, *refs):
    count = len(refs) - len(plan)
    for terms, target in zip(plan, refs[count:], strict=True):
        for place, size, coded, sources in terms:
            if coded:
                values = sum(decoded(refs[number][start]) for number, start in sources)
                target[place] = encoded(values)
            elif len(sources) == 1:
                number, start = sources[0]
                target[place : place + size] = refs[number][start : start + size]
            else:
                values = sum(refs[number][start : start + size].astype(jnp.float32) for number, start in sources)
                target[place : place + size] = low(values)


def fold(outs, order, name):
    arrays, plan, shapes = [], [], []
    for out in outs:
        place, terms = 0, []
        for size, *sources in out:
            numbered = []
            for array, start in sources:
                found = [n for n, other in enumerate(arrays) if other is array]
                if not found:
                    arrays.append(array)
                numbered.append((found[0] if found else len(arrays) - 1, start))
            terms.append((place, max(size, 1), size == 0, tuple(numbered)))
            place += max(size, 1)
        plan.append(tuple(terms))
        shapes.append(shaped((place,) + arrays[0].shape[1:], jnp.bfloat16))
    return whole(functools.partial(fold_kernel, plan), name, (), arrays, shapes, [], 0, carry=(order,), limit=FOLD_LIMIT)


def exchange_each(values, step, sizes):
    orders, _ = halving_orders(sizes[1])
    return [exchange(values[i], orders[i][step], sizes) for i in range(THIRDS)]


def spread_kernel(kind, batch_size, numbers, *refs):
    sources, targets = refs[: 2 * THIRDS], refs[2 * THIRDS :]
    core = numbers[1] & 1
    labels = labels_of(numbers[0], numbers[1], batch_size)
    _, rows, third = sources[0].shape
    rows = rows // 2
    for matrix in range(4):

        def put(first, matrix=matrix):
            for part in range(THIRDS):
                for own in range(4):
                    value = sources[first + part][own ^ (labels[part] & 3), (matrix % 2) * rows : (matrix % 2 + 1) * rows]
                    value = value.astype(jnp.float32)
                    at, columns = slice(own * rows, (own + 1) * rows), slice(part * third, (part + 1) * third)
                    if kind == "tall":
                        targets[0][matrix, at, columns] = value
                    elif kind == "wide":
                        start = (matrix * THIRDS + part) * third
                        targets[0][at, start : start + third] = value
                    else:
                        targets[matrix][at, columns] = value

        @pl.when(core == matrix // 2)
        def _():
            put(0)

        @pl.when(core != matrix // 2)
        def _():
            put(THIRDS)


def spread(numbers, blocks, kind, name, sizes, **waits):
    third = blocks[0].shape[2]
    width = THIRDS * third
    rows = 2 * width // LABELS
    group = 2 * rows

    groups = LABELS // 4

    def source_spec(part):
        def at(i, numbers):
            return ((i ^ (labels_of(numbers[0], numbers[1], sizes[1])[part] >> 2)) + part * groups, 0, 0)

        return pl.BlockSpec((4, rows, third), at)

    if kind == "tall":
        specs = [pl.BlockSpec((4, group, width), lambda i, *_: (0, i, 0))]
        shapes = [shaped((4, width, width), jnp.float32)]
    elif kind == "wide":
        specs = [pl.BlockSpec((group, 4 * width), lambda i, *_: (i, 0))]
        shapes = [shaped((width, 4 * width), jnp.float32)]
    else:
        specs = [pl.BlockSpec((group, width), lambda i, *_: (i, 0))] * 4
        shapes = [shaped((width, width), jnp.float32)] * 4
    return call(
        functools.partial(spread_kernel, kind, sizes[1]),
        name,
        (LABELS // 4,),
        [source_spec(part % THIRDS) for part in range(2 * THIRDS)],
        specs, shapes, [],
        0,
        24 * width * width,
        (numbers,), *[blocks[0]] * THIRDS, *[blocks[1]] * THIRDS, **waits,
    )


def gather_embeddings(own, sizes):
    orders = gather_orders(sizes[1])
    value = own[None]
    for even_dim, odd_dim in zip(*orders, strict=True):
        value = jnp.concatenate([value, exchange(value, even_dim, sizes, odd_dim)], axis=0)
    return value, exchange(value, CORE, sizes)


BAND = 64
STEP = 128
WINDOW = STEP + 2 * BAND
QUERY_BIAS, VALUE_BIAS, OUTPUT_BIAS, FIRST_GAIN, FIRST_SHIFT, DOWN_BIAS, SECOND_GAIN, SECOND_SHIFT, UP_BIAS = range(9)


def dots(former, latter):
    return lax.dot_general(former, latter, (((1,), (1,)), ((), ())), preferred_element_type=jnp.float32)


def product(former, latter):
    return jnp.dot(former, latter, preferred_element_type=jnp.float32)


def transposed(former, latter):
    return lax.dot_general(former, latter, (((0,), (0,)), ((), ())), preferred_element_type=jnp.float32)


def low(values):
    return values.astype(jnp.bfloat16)


def call(kernel, name, grid, in_specs, out_specs, out_shape, scratch, flops, moved, scalars, *args, after=(), carry=(), limit=16):
    taken, given = len(scalars) + len(in_specs), len(out_specs)
    waits = len(after) + len(carry)

    def run(*refs):
        kernel(*refs[:taken], *refs[taken + waits : taken + waits + given], *refs[taken + waits + given + len(carry) :])

    anywhere = pl.BlockSpec(memory_space=pl.ANY)
    return pl.pallas_call(
        run,
        grid_spec=pltpu.PrefetchScalarGridSpec(
            num_scalar_prefetch=len(scalars),
            grid=grid,
            in_specs=list(in_specs) + [anywhere] * waits,
            out_specs=list(out_specs) + [anywhere] * len(carry),
            scratch_shapes=scratch,
        ),
        out_shape=list(out_shape) + [shaped(value.shape, value.dtype) for value in carry],
        input_output_aliases={taken + len(after) + i: given + i for i in range(len(carry))},
        compiler_params=pltpu.CompilerParams(vmem_limit_bytes=limit * MIB),
        cost_estimate=pl.CostEstimate(flops=flops, bytes_accessed=moved, transcendentals=0),
        name=name,
    )(*scalars, *args, *after, *carry)


def whole(kernel, name, scalars, args, outs, scratch, flops, after=(), carry=(), far=(), far_outs=(), limit=12):
    taken, given = len(scalars) + len(args), len(outs)
    waits = len(after) + len(carry)

    def run(*refs):
        kernel(*refs[:taken], *refs[taken + waits : taken + waits + given], *refs[taken + waits + given + len(carry) :])

    near, remote = pl.BlockSpec(memory_space=pltpu.VMEM), pl.BlockSpec(memory_space=pltpu.HBM)
    anywhere = pl.BlockSpec(memory_space=pl.ANY)
    moved = sum(a.size * a.dtype.itemsize for a in args) + sum(o.size * o.dtype.itemsize for o in outs)
    args = [pltpu.with_memory_space_constraint(a, pltpu.HBM) if i in far else a for i, a in enumerate(args)]
    out_shape = [pltpu.HBM(o.shape, o.dtype) if i in far_outs else o for i, o in enumerate(outs)]
    return pl.pallas_call(
        run,
        in_specs=[pl.BlockSpec(memory_space=pltpu.SMEM)] * len(scalars)
        + [remote if i in far else near for i in range(len(args))]
        + [anywhere] * waits,
        out_specs=[remote if i in far_outs else near for i in range(given)] + [anywhere] * len(carry),
        out_shape=out_shape + [shaped(value.shape, value.dtype) for value in carry],
        scratch_shapes=scratch,
        input_output_aliases={taken + len(after) + i: given + i for i in range(len(carry))},
        compiler_params=pltpu.CompilerParams(vmem_limit_bytes=limit * MIB),
        cost_estimate=pl.CostEstimate(flops=flops, bytes_accessed=moved, transcendentals=0),
        name=name,
    )(*scalars, *args, *after, *carry)


def shaped(shape, dtype):
    return jax.ShapeDtypeStruct(shape, dtype)


def rows_spec(rows, width):
    return pl.BlockSpec((rows, width), lambda i, *_: (i, 0))


def segment_of(lengths, row, count, shape, dim):
    place = lax.broadcasted_iota(jnp.int32, shape, dim)
    total, ids = 0, jnp.zeros(shape, jnp.int32)
    for j in range(count):
        total = total + lengths[row, j]
        ids = ids + (place >= total).astype(jnp.int32)
    return ids


def window_start(block, span):
    return min(max(block * STEP - BAND, 0), span - WINDOW)


def fill_bias(lengths, row, count, span, bias_ref, first=0):
    down = segment_of(lengths, row, count, (span, 128), 0)
    along = segment_of(lengths, row, count, (8, span), 1)
    for block in range(span // STEP):
        start = window_start(block, span)
        same = down[block * STEP : (block + 1) * STEP, 0:1] == along[0:1, start : start + WINDOW]
        bias_ref[first + block] = jnp.where(same, 0.0, -1e9)


def head_masks(scale):
    lane = lax.broadcasted_iota(jnp.int32, (1, 2 * HEAD_DIM), 1)
    first = low(jnp.where(lane < HEAD_DIM, scale, 0.0))
    second = low(jnp.where(lane < HEAD_DIM, 0.0, scale))
    return first, second


def stacked(values, masks):
    return jnp.concatenate([values * masks[0], values * masks[1]], axis=0)


def merged(values):
    lane = lax.broadcasted_iota(jnp.int32, (STEP, 2 * HEAD_DIM), 1)
    return jnp.where(lane < HEAD_DIM, values[:STEP], values[STEP:])


def biased(scores, bias):
    return (scores.reshape(2, STEP, WINDOW) + bias[None]).reshape(2 * STEP, WINDOW)


def normalised(values):
    centred = values - jnp.mean(values, axis=-1, keepdims=True)
    factor = lax.rsqrt(jnp.mean(centred * centred, axis=-1, keepdims=True) + 1e-12)
    return centred * factor, factor


def norm_back(gradient, normed, factor, gain):
    inner = gradient * gain
    centred = inner - jnp.mean(inner, axis=-1, keepdims=True)
    return factor * (centred - normed * jnp.mean(inner * normed, axis=-1, keepdims=True))


def contrast_kernel(scale, sizes, numbers, lengths, own_ref, foreign_ref, pooled_ref, terms_ref, grad_ref, all_ref, digits_ref, totals_ref):
    half, texts, wide = own_ref.shape
    width = pooled_ref.shape[1]
    total = all_ref.shape[1]
    stream, batch = numbers[0], numbers[1]
    orders = gather_orders(sizes[1])

    def place(source, from_stream, from_batch, i):
        at = pl.multiple_of(from_batch * texts, texts)
        other = from_stream ^ stream
        all_ref[other, pl.ds(at, texts)] = source[i, :, :width]

        @pl.when(other == 1)
        def _():
            digits_ref[pl.ds(at, texts)] = source[i, :, width:]

    def place_both(i, carry):
        place(own_ref, *place_at(*orders, i, (stream, batch)), i)
        place(foreign_ref, *place_at(*orders, i, (stream, batch ^ 1)), i)
        return carry

    lax.fori_loop(0, half, place_both, 0)

    tile = min(TILE, total)
    totals_ref[...] = jnp.zeros_like(totals_ref)
    for column in range(total // tile):
        latter = all_ref[1, column * tile : (column + 1) * tile]

        def add(i, carry, latter=latter, column=column):
            former = all_ref[0, pl.ds(pl.multiple_of(i * tile, tile), tile)]
            sums = jnp.sum(jnp.exp(dots(former, latter) / 0.05), axis=0, keepdims=True)
            totals_ref[:, column * tile : (column + 1) * tile] += sums
            return carry

        lax.fori_loop(0, total // tile, add, 0)
    mine = all_ref[0, pl.ds(pl.multiple_of(batch * texts, texts), texts)]
    partners = all_ref[1]
    own_digits = own_ref[0, :, width:]
    logits = dots(mine, partners) / 0.05
    exponent = jnp.exp(logits)
    row_total = jnp.sum(exponent, axis=1, keepdims=True)
    own_target = (64.0 * own_digits[:, 0:1].astype(jnp.float32) + own_digits[:, 1:2].astype(jnp.float32)).astype(jnp.int32)
    lane = lax.broadcasted_iota(jnp.int32, (8, 128), 1)
    pick = jnp.where(lane == 0, 64.0, jnp.where(lane == 1, 1.0, 0.0)).astype(jnp.bfloat16)
    all_target = dots(pick, digits_ref[...])[0:1].astype(jnp.int32)
    columns = lax.broadcasted_iota(jnp.int32, (texts, total), 1)
    rows = batch * texts + lax.broadcasted_iota(jnp.int32, (texts, total), 0)
    query_hit = (own_target == columns).astype(jnp.float32)
    doc_hit = (all_target == rows).astype(jnp.float32)
    target = jnp.where(stream == 0, query_hit, doc_hit)
    chosen = jnp.sum(logits * target, axis=1, keepdims=True)
    terms_ref[...] = jnp.broadcast_to(jnp.log(row_total) - chosen, terms_ref.shape)
    own_low = ((exponent / row_total - target) * scale).astype(jnp.bfloat16)
    cross_low = ((exponent / totals_ref[0:1, :] - target) * scale).astype(jnp.bfloat16)
    gradient = (
        jnp.dot(own_low, partners, preferred_element_type=jnp.float32)
        + jnp.dot(cross_low, partners, preferred_element_type=jnp.float32)
    ) / 0.05
    gradient = gradient.astype(jnp.bfloat16).astype(jnp.float32)
    pooled = pooled_ref[...]
    inverse_norm = lax.rsqrt(jnp.sum(pooled * pooled, axis=1, keepdims=True) + 1e-06)
    embedding = pooled * inverse_norm
    inner = jnp.sum(gradient * embedding, axis=1, keepdims=True)
    count = texts // lengths.shape[0]
    divisor = jnp.concatenate([length_column(lengths, row, count) for row in range(lengths.shape[0])], axis=0)
    grad_ref[...] = inverse_norm * (gradient - embedding * inner) / divisor


def contrast(numbers, lengths, own, foreign, pooled, sizes):
    _, texts, wide = own.shape
    width = pooled.shape[1]
    total = sizes[1] * texts
    terms, gradient = whole(
        functools.partial(contrast_kernel, 1.0 / (2.0 * total), sizes),
        "contrast",
        (numbers, lengths),
        (own, foreign, pooled),
        [shaped((texts, 128), jnp.float32), shaped(pooled.shape, jnp.float32)],
        [
            pltpu.VMEM((2, total, width), jnp.bfloat16),
            pltpu.VMEM((total, wide - width), jnp.bfloat16),
            pltpu.VMEM((8, total), jnp.float32),
        ],
        2 * total * total * width,
        limit=max(12, 8 + total * width // 2**16),
    )
    return terms[:, 0], gradient


def attend_kernel(count, lengths, x_in, wq_in, wk_in, wv_in, wo_in, *refs):
    vectors_in, refs = refs[:9], refs[9:]
    q_out, k_out, v_out, ctx_out, aux_out, vec_ref, normed_ref, hidden_ref = refs[:8]
    x_ref, w_ref, wide_ref, q_ref, k_ref, v_ref, ctx_ref, aux_ref, bias_ref, sems = refs[8:]
    tokens, width = x_ref.shape
    row_count = lengths.shape[0]
    span = tokens // row_count
    places, at = [], 0
    for vector in vectors_in:
        places.append(at)
        at += vector.shape[0]
    loads = [pltpu.make_async_copy(x_in, x_ref, sems.at[0]), pltpu.make_async_copy(wq_in, w_ref.at[0], sems.at[1])]
    small = [
        pltpu.make_async_copy(vector, wide_ref.at[pl.ds(place, vector.shape[0])], sems.at[5 + i])
        for i, (vector, place) in enumerate(zip(vectors_in, places, strict=True))
    ]
    loads += [pltpu.make_async_copy(w, w_ref.at[i], sems.at[1 + i]) for i, w in ((1, wk_in), (2, wv_in), (3, wo_in))]
    for copy in loads[:2] + small + loads[2:]:
        copy.start()
    for row in range(row_count):
        fill_bias(lengths, row, count, span, bias_ref, row * (span // STEP))
    for copy in small:
        copy.wait()
    flat = wide_ref[...].astype(jnp.float32)
    for row in range(vec_ref.shape[0]):
        vec_ref[row : row + 1] = flat[row * width : (row + 1) * width].reshape(1, width)
    loads[0].wait()
    stores = [
        pltpu.make_async_copy(ref, out, sems.at[14 + i])
        for i, (ref, out) in enumerate(
            ((q_ref, q_out), (k_ref, k_out), (v_ref, v_out), (ctx_ref, ctx_out), (aux_ref, aux_out))
        )
    ]
    for i, (ref, bias) in enumerate(((q_ref, QUERY_BIAS), (k_ref, None), (v_ref, VALUE_BIAS))):
        loads[1 + i].wait()
        for row in range(row_count):
            rows = slice(row * span, (row + 1) * span)
            values = product(x_ref[rows], w_ref[i])
            ref[rows] = low(values if bias is None else values + vec_ref[bias : bias + 1])
        stores[i].start()
    masks = head_masks(HEAD_DIM**-0.5)
    aux_ref[...] = jnp.zeros_like(aux_ref)
    pairs = width // (2 * HEAD_DIM)

    def heads(step, carry):
        row, pair = step // pairs, step % pairs
        at = pl.ds(pl.multiple_of(pair * 2 * HEAD_DIM, 2 * HEAD_DIM), 2 * HEAD_DIM)
        lane = lax.broadcasted_iota(jnp.int32, (STEP, 128), 1)
        blocks = range(span // STEP)
        rows = [pl.ds(pl.multiple_of(row * span + block * STEP, STEP), STEP) for block in blocks]
        keys = [pl.ds(pl.multiple_of(row * span + window_start(block, span), BAND), WINDOW) for block in blocks]
        scores = [dots(stacked(q_ref[rows[b], at], masks), k_ref[keys[b], at]) for b in blocks]
        scores = [biased(scores[b], bias_ref[row * (span // STEP) + b]) for b in blocks]
        highest = [jnp.max(value, axis=1, keepdims=True) for value in scores]
        exponent = [jnp.exp(scores[b] - highest[b]) for b in blocks]
        total = [jnp.sum(value, axis=1, keepdims=True) for value in exponent]
        attention = [low(exponent[b] * (1.0 / total[b])) for b in blocks]
        for b in blocks:
            ctx_ref[rows[b], at] = low(merged(product(attention[b], v_ref[keys[b], at])))
        for b in blocks:
            log_total = highest[b] + jnp.log(total[b])
            kept = jnp.where(lane == 2 * pair, log_total[:STEP], aux_ref[rows[b]])
            aux_ref[rows[b]] = jnp.where(lane == 2 * pair + 1, log_total[STEP:], kept)
        return carry

    lax.fori_loop(0, row_count * pairs, heads, 0)
    stores[3].start()
    loads[4].wait()
    for row in range(row_count):
        rows = slice(row * span, (row + 1) * span)
        attended = product(ctx_ref[rows], w_ref[3]) + vec_ref[OUTPUT_BIAS : OUTPUT_BIAS + 1]
        normed, factor = normalised(x_ref[rows].astype(jnp.float32) + attended)
        normed_ref[rows] = normed
        hidden_ref[rows] = low(normed * vec_ref[FIRST_GAIN : FIRST_GAIN + 1] + vec_ref[FIRST_SHIFT : FIRST_SHIFT + 1])
        lane = lax.broadcasted_iota(jnp.int32, (span, 128), 1)
        aux_ref[rows] = jnp.where(lane == 127, factor, aux_ref[rows])
    stores[4].start()
    for copy in stores:
        copy.wait()


def attend(lengths, x, weights, vectors):
    tokens, width = x.shape
    row_count = lengths.shape[0]
    span = tokens // row_count
    vector_rows = sum(vector.shape[0] for vector in vectors) // width
    square = shaped((tokens, width), jnp.bfloat16)
    token_scratch = pltpu.VMEM((tokens, width), jnp.bfloat16)
    return whole(
        functools.partial(attend_kernel, lengths.shape[1]),
        "attend",
        (lengths,),
        (x, *weights, *vectors),
        [square] * 4
        + [
            shaped((tokens, 128), jnp.float32),
            shaped((vector_rows, width), jnp.float32),
            shaped((tokens, width), jnp.float32),
            square,
        ],
        [token_scratch, pltpu.VMEM((4, width, width), jnp.bfloat16), pltpu.VMEM((vector_rows * width,), jnp.bfloat16)]
        + [token_scratch] * 4
        + [pltpu.VMEM((tokens, 128), jnp.float32)]
        + [pltpu.VMEM((row_count * span // STEP, STEP, WINDOW), jnp.float32), pltpu.SemaphoreType.DMA((19,))],
        8 * tokens * width * width + 4 * tokens * WINDOW * width,
        far=range(5 + len(vectors)),
        far_outs=range(5),
        limit=24,
    )


def gelu_and_slope(values):
    size = jnp.abs(values)
    part = 1.0 / (1.0 + (0.3275911 * 0.5**0.5) * size)
    bell = jnp.exp(values * values * -0.5)
    series = part * (0.5 * 0.254829592 + part * (-0.5 * 0.284496736 + part * (0.5 * 1.421413741 + part * (-0.5 * 1.453152027 + part * (0.5 * 1.061405429)))))
    tail = series * bell
    share = jnp.where(values < 0.0, tail, 1.0 - tail)
    return values * share, share + values * bell * 0.3989422804014327


def two_parts(values):
    high = low(values)
    return high, low(values - high.astype(jnp.float32))


def membership(lengths, row, count, rows, offset):
    place = lax.broadcasted_iota(jnp.int32, (count, rows), 1) + offset
    text = lax.broadcasted_iota(jnp.int32, (count, rows), 0)
    total = 0
    inside = jnp.zeros((count, rows), jnp.float32)
    for j in range(count):
        start, total = total, total + lengths[row, j]
        inside = jnp.where((text == j) & (place >= start) & (place < total), 1.0, inside)
    return low(inside)


def length_column(lengths, row, count):
    text = lax.broadcasted_iota(jnp.int32, (count, 128), 0)
    column = jnp.zeros((count, 128), jnp.float32)
    for j in range(count):
        column = jnp.where(text == j, lengths[row, j].astype(jnp.float32), column)
    return column[:, 0:1]


def feed_kernel(count, lengths, positives, normed_ref, hidden_ref, up_ref, down_ref, vec_ref, act_out, slope_out, second_ref, factor_ref, pooled_ref, package_ref, act_ref, slope_ref, sems):
    tokens, width = normed_ref.shape
    row_count = lengths.shape[0]
    span = tokens // row_count
    rows = 256
    parts = span // rows
    pooled_ref[...] = jnp.zeros_like(pooled_ref)

    def copies(step, slot):
        here = pl.ds(pl.multiple_of(step * rows, rows), rows)
        return (
            pltpu.make_async_copy(act_ref.at[slot], act_out.at[here], sems.at[0, slot]),
            pltpu.make_async_copy(slope_ref.at[slot], slope_out.at[here], sems.at[1, slot]),
        )

    def block(step, carry):
        row, part = step // parts, step % parts
        here = pl.ds(pl.multiple_of(step * rows, rows), rows)
        slot = step % 2
        stores = copies(step, slot)

        @pl.when(step >= 2)
        def _():
            for copy in copies(step - 2, slot):
                copy.wait()

        hidden_low = hidden_ref[here]
        branch = jnp.zeros((rows, width), jnp.float32)
        pieces = up_ref.shape[1] // width
        spots = [slice(piece * width, (piece + 1) * width) for piece in range(pieces)]
        later = product(hidden_low, up_ref[:, spots[0]])
        done = None
        for piece, at in enumerate(spots):
            values = later + vec_ref[UP_BIAS + piece : UP_BIAS + piece + 1]
            if piece + 1 < pieces:
                later = product(hidden_low, up_ref[:, spots[piece + 1]])
            if done is not None:
                branch = branch + product(done, down_ref[spots[piece - 1]])
            activation, slope = gelu_and_slope(values)
            done = low(activation)
            act_ref[slot, :, at] = done
            slope_ref[slot, :, at] = low(slope)
        branch = branch + product(done, down_ref[spots[-1]])
        for copy in stores:
            copy.start()
        hidden = normed_ref[here] * vec_ref[FIRST_GAIN : FIRST_GAIN + 1] + vec_ref[FIRST_SHIFT : FIRST_SHIFT + 1]
        normed, factor = normalised(hidden + branch + vec_ref[DOWN_BIAS : DOWN_BIAS + 1])
        second_ref[here] = normed
        factor_ref[here] = jnp.broadcast_to(factor, (rows, 128))
        high, rest = two_parts(normed * vec_ref[SECOND_GAIN : SECOND_GAIN + 1] + vec_ref[SECOND_SHIFT : SECOND_SHIFT + 1])
        inside = membership(lengths, row, count, rows, part * rows)
        texts = pl.ds(pl.multiple_of(row * count, count), count)
        pooled_ref[texts] += product(inside, high) + product(inside, rest)
        return carry

    lax.fori_loop(0, tokens // rows, block, 0)
    text = lax.broadcasted_iota(jnp.int32, (count, 128), 0)
    lane = lax.broadcasted_iota(jnp.int32, (count, 128), 1)
    for row in range(row_count):
        texts = slice(row * count, (row + 1) * count)
        pooled = pooled_ref[texts] / length_column(lengths, row, count)
        pooled_ref[texts] = pooled
        inverse_norm = lax.rsqrt(jnp.sum(pooled * pooled, axis=1, keepdims=True) + 1e-06)
        package_ref[texts, :width] = low(pooled * inverse_norm)
        digits = jnp.zeros((count, 128), jnp.int32)
        for j in range(count):
            own = positives[row * count + j]
            digits = jnp.where(text == j, jnp.where(lane == 0, own >> 6, own & 63), digits)
        package_ref[texts, width:] = low(jnp.where(lane < 2, digits, 0).astype(jnp.float32))
    steps = tokens // rows
    for step in range(steps - 2, steps):
        for copy in copies(step, step % 2):
            copy.wait()


def feed(lengths, positives, normed, hidden_low, up, down, vec):
    tokens, width = normed.shape
    texts, hidden = lengths.size, up.shape[1]
    return whole(
        functools.partial(feed_kernel, lengths.shape[1]),
        "feed",
        (lengths, positives),
        (normed, hidden_low, up, down, vec),
        [
            shaped((tokens, hidden), jnp.bfloat16),
            shaped((tokens, hidden), jnp.bfloat16),
            shaped((tokens, width), jnp.float32),
            shaped((tokens, 128), jnp.float32),
            shaped((texts, width), jnp.float32),
            shaped((texts, width + 128), jnp.bfloat16),
        ],
        [pltpu.VMEM((2, 256, hidden), jnp.bfloat16)] * 2 + [pltpu.SemaphoreType.DMA((2, 2))],
        4 * tokens * width * hidden,
        far_outs=(0, 1),
        limit=16,
    )


def sums_of(values):
    return jnp.sum(values, axis=0, keepdims=True)


def second_back_kernel(count, lengths, grad_ref, normed_ref, factor_ref, vec_ref, sum_ref, low_ref, totals_ref):
    tokens, width = normed_ref.shape
    row_count = lengths.shape[0]
    span = tokens // row_count
    totals_ref[...] = jnp.zeros_like(totals_ref)
    for row in range(row_count):
        rows = slice(row * span, (row + 1) * span)
        inside = membership(lengths, row, count, span, 0)
        high, rest = two_parts(grad_ref[row * count : (row + 1) * count])
        result_grad = transposed(inside, high) + transposed(inside, rest)
        normed = normed_ref[rows]
        second_sum = norm_back(result_grad, normed, factor_ref[rows, 0:1], vec_ref[SECOND_GAIN : SECOND_GAIN + 1])
        branch_grad = low(second_sum)
        sum_ref[rows] = second_sum
        low_ref[rows] = branch_grad
        totals_ref[0:1] += sums_of(branch_grad.astype(jnp.float32))
        totals_ref[1:2] += sums_of(result_grad * normed)
        totals_ref[2:3] += sums_of(result_grad)


def second_back(lengths, grad, normed, factor, vec):
    tokens, width = normed.shape
    return whole(
        functools.partial(second_back_kernel, lengths.shape[1]),
        "second_norm_back",
        (lengths,),
        (grad, normed, factor, vec),
        [shaped((tokens, width), jnp.float32), shaped((tokens, width), jnp.bfloat16), shaped((8, width), jnp.float32)],
        [],
        8 * tokens * width,
    )


def matrix_at(place, foreign, numbers):
    return 2 * ((numbers[1] & 1) ^ foreign) + place


def put_rows(numbers, sizes, sides, out_ref, place, group=8):
    labels = labels_of(numbers[0], numbers[1], sizes[1])
    rows, third = out_ref.shape[2] // 2, out_ref.shape[3]
    for first in range(0, LABELS, group):
        piece = low(sum(transposed(left(first * rows, group * rows), right) for left, right in sides))
        for own in range(group):
            for part in range(THIRDS):
                value = piece[own * rows : (own + 1) * rows, part * third : (part + 1) * third]
                out_ref[part, (first + own) ^ labels[part], place * rows : (place + 1) * rows] = value


def columns(ref):
    return lambda at, size: ref[:, at : at + size]


def blocks_out(width):
    return shaped((THIRDS, LABELS, 2 * width // LABELS, width // THIRDS), jnp.bfloat16)


def column_loads(source, target, foreign, numbers, sems):
    width = target.shape[2]
    copies = []
    for place in range(2):
        at = pl.ds(pl.multiple_of(matrix_at(place, foreign, numbers) * width, width), width)
        copies.append(pltpu.make_async_copy(source.at[:, at], target.at[place], sems.at[place]))
    return copies


def down_weight_kernel(foreign, sizes, numbers, act_in, grad_ref, out_ref, act_ref, sems):
    loads = column_loads(act_in, act_ref, foreign, numbers, sems)
    for copy in loads:
        copy.start()
    for place in range(2):
        loads[place].wait()
        put_rows(numbers, sizes, [(columns(act_ref.at[place]), grad_ref[...])], out_ref, place)


def down_weight(numbers, activation, grad, foreign, sizes, name, **waits):
    tokens, width = grad.shape
    return whole(
        functools.partial(down_weight_kernel, foreign, sizes),
        name,
        (numbers,), (activation, grad), [blocks_out(width)],
        [pltpu.VMEM((2, tokens, width), jnp.bfloat16), pltpu.SemaphoreType.DMA((2,))],
        4 * tokens * width * width,
        far=(0,),
        **waits,
    )


def up_back_kernel(foreign, sizes, numbers, grad_ref, slope_in, hidden_ref, up_ref, down_ref, before_ref, *refs):
    if foreign:
        out_ref, after_ref, totals_ref, pre_ref, slope_ref, sems = refs
    else:
        normed_ref, aux_ref, vec_ref, out_ref, totals_ref, first_ref, low_ref, sums_ref, pre_ref, slope_ref, sems = refs
        after_ref = first_ref
    width = grad_ref.shape[1]
    loads = column_loads(slope_in, slope_ref, foreign, numbers, sems)
    for copy in loads:
        copy.start()
    for place in range(2):
        at = pl.ds(pl.multiple_of(matrix_at(place, foreign, numbers) * width, width), width)
        before = before_ref if place == 0 else after_ref
        total = jnp.zeros((1, width), jnp.float32)
        later = dots(grad_ref[:TILE], down_ref[at])
        loads[place].wait()
        for start in range(0, grad_ref.shape[0], TILE):
            rows = slice(start, start + TILE)
            active_grad = later
            if start + TILE < grad_ref.shape[0]:
                later = dots(grad_ref[start + TILE : start + 2 * TILE], down_ref[at])
            pre_grad = low(active_grad * slope_ref[place, rows].astype(jnp.float32))
            pre_ref[rows] = pre_grad
            total = total + sums_of(pre_grad.astype(jnp.float32))
            after_ref[rows] = before[rows] + dots(pre_grad, up_ref[:, at])
        totals_ref[place] = jnp.broadcast_to(total, totals_ref.shape[1:])
        put_rows(numbers, sizes, [(columns(hidden_ref), pre_ref[...])], out_ref, place)
    if foreign:
        return
    hidden_grad, normed = after_ref[...], normed_ref[...]
    first_sum = norm_back(hidden_grad, normed, aux_ref[:, 127:128], vec_ref[FIRST_GAIN : FIRST_GAIN + 1])
    attended_grad = low(first_sum)
    first_ref[...] = first_sum
    low_ref[...] = attended_grad
    sums_ref[...] = jnp.zeros_like(sums_ref)
    sums_ref[0:1] = sums_of(attended_grad.astype(jnp.float32))
    sums_ref[1:2] = sums_of(hidden_grad * normed)
    sums_ref[2:3] = sums_of(hidden_grad)


def up_back(numbers, grad, slope, hidden_low, up, down, before, foreign, sizes, name, rest=(), **waits):
    tokens, width = grad.shape
    wide = shaped((tokens, width), jnp.float32)
    totals = shaped((2, 8, width), jnp.float32)
    pre = [
        pltpu.VMEM((tokens, width), jnp.bfloat16),
        pltpu.VMEM((2, tokens, width), jnp.bfloat16),
        pltpu.SemaphoreType.DMA((2,)),
    ]
    if foreign:
        outs, scratch = [blocks_out(width), wide, totals], pre
    else:
        outs = [blocks_out(width), totals, wide, shaped((tokens, width), jnp.bfloat16), shaped((8, width), jnp.float32)]
        scratch = pre
    return whole(
        functools.partial(up_back_kernel, foreign, sizes),
        name,
        (numbers,), (grad, slope, hidden_low, up, down, before, *rest), outs, scratch,
        12 * tokens * width * width,
        far=(1,),
        limit=12,
        **waits,
    )


def attend_back_kernel(count, row, half, lengths, q_ref, k_ref, v_ref, grad_ref, wo_ref, aux_ref, *refs):
    out_ref, totals_ref, bias_ref, ctx_ref, dk_ref, dv_ref = refs[-6:]
    width = q_ref.shape[1]
    span = q_ref.shape[0] // lengths.shape[0]
    base = row * span
    grad = grad_ref[base : base + span]
    part = width // 2
    ctx_ref[...] = low(dots(grad, wo_ref[half * part : (half + 1) * part]))
    fill_bias(lengths, row, count, span, bias_ref)
    scale = HEAD_DIM**-0.5
    scaled, plain = head_masks(scale), head_masks(1.0)
    dk_ref[...] = jnp.zeros_like(dk_ref)
    dv_ref[...] = jnp.zeros_like(dv_ref)

    def heads(pair, carry):
        at = pl.ds(pl.multiple_of(pair * 2 * HEAD_DIM, 2 * HEAD_DIM), 2 * HEAD_DIM)
        own = pl.ds(pl.multiple_of(pair * 2 * HEAD_DIM - half * part, 2 * HEAD_DIM), 2 * HEAD_DIM)
        lane = lax.broadcasted_iota(jnp.int32, (STEP, 128), 1)
        blocks = range(span // STEP)
        rows = [pl.ds(block * STEP, STEP) for block in blocks]
        keys = [pl.ds(window_start(block, span), WINDOW) for block in blocks]
        own_rows = [pl.ds(base + block * STEP, STEP) for block in blocks]
        own_keys = [pl.ds(base + window_start(block, span), WINDOW) for block in blocks]
        queries = [stacked(q_ref[own_rows[b], at], scaled) for b in blocks]
        context_grad = [stacked(ctx_ref[rows[b], own], plain) for b in blocks]
        scores = [dots(queries[b], k_ref[own_keys[b], at]) for b in blocks]
        prob_grad = [dots(context_grad[b], v_ref[own_keys[b], at]) for b in blocks]
        log_total = [
            jnp.concatenate(
                [
                    jnp.sum(jnp.where(lane == 2 * pair + side, aux_ref[own_rows[b]], 0.0), axis=1, keepdims=True)
                    for side in range(2)
                ],
                axis=0,
            )
            for b in blocks
        ]
        attention = [jnp.exp(biased(scores[b], bias_ref[b]) - log_total[b]) for b in blocks]
        inner = [jnp.sum(attention[b] * prob_grad[b], axis=1, keepdims=True) for b in blocks]
        score_grad = [low(attention[b] * (prob_grad[b] - inner[b])) for b in blocks]
        for b in blocks:
            out_ref[0, rows[b], at] = low(merged(product(score_grad[b], k_ref[own_keys[b], at])) * scale)
        for b in blocks:
            dk_ref[keys[b], own] += transposed(score_grad[b], queries[b])
        for b in blocks:
            dv_ref[keys[b], own] += transposed(low(attention[b]), context_grad[b])
        return carry

    pairs = part // (2 * HEAD_DIM)
    lax.fori_loop(half * pairs, (half + 1) * pairs, heads, 0)
    out_ref[1, :, half * part : (half + 1) * part] = low(dk_ref[...])
    out_ref[2, :, half * part : (half + 1) * part] = low(dv_ref[...])
    if half == 0:
        return
    out_ref[:, :, :part] = refs[0][:, :, :part]

    totals_ref[...] = jnp.zeros_like(totals_ref)
    totals_ref[0:1] = sums_of(out_ref[0].astype(jnp.float32))
    totals_ref[1:2] = sums_of(out_ref[2].astype(jnp.float32))


def attend_back(lengths, q, k, v, grad, wo, aux, row, half, before=None, **waits):
    tokens, width = q.shape
    span = tokens // lengths.shape[0]
    return whole(
        functools.partial(attend_back_kernel, lengths.shape[1], row, half),
        "attend_back",
        (lengths,),
        (q, k, v, grad, wo, aux) + (() if before is None else (before,)),
        [shaped((3, span, width), jnp.bfloat16), shaped((8, width), jnp.float32)],
        [
            pltpu.VMEM((span // STEP, STEP, WINDOW), jnp.float32),
            pltpu.VMEM((span, width // 2), jnp.bfloat16),
            pltpu.VMEM((span, width // 2), jnp.float32),
            pltpu.VMEM((span, width // 2), jnp.float32),
        ],
        span * width * width + 5 * span * WINDOW * width,
        **waits,
    )


def mixed_weight_kernel(foreign, sizes, numbers, x_ref, ctx_ref, grad_ref, one_ref, other_ref, out_ref):
    span = one_ref.shape[1]

    def put(left, matrix, place):
        if matrix == 3:
            put_rows(numbers, sizes, [(columns(ctx_ref), grad_ref[...])], out_ref, place)
            return
        first = lambda at, size: left[:span, at : at + size]
        second = lambda at, size: left[span:, at : at + size]
        put_rows(numbers, sizes, [(first, one_ref[matrix]), (second, other_ref[matrix])], out_ref, place)

    for pair in range(2):

        @pl.when(matrix_at(0, foreign, numbers) == 2 * pair)
        def _(pair=pair):
            put(x_ref, 2 * pair, 0)
            put(x_ref, 2 * pair + 1, 1)


def mixed_weight(numbers, x, context, grad, grads, foreign, sizes, name, **waits):
    tokens, width = x.shape
    return whole(
        functools.partial(mixed_weight_kernel, foreign, sizes),
        name,
        (numbers,), (x, context, grad, *grads), [blocks_out(width)], [],
        4 * tokens * width * width,
        **waits,
    )


def input_kernel(steps, first_ref, one_ref, other_ref, wq_ref, wk_ref, wv_ref, out_ref):
    def put(grad_ref):
        out_ref[...] = first_ref[...] + dots(grad_ref[0], wq_ref[...]) + dots(grad_ref[1], wk_ref[...]) + dots(grad_ref[2], wv_ref[...])

    @pl.when(pl.program_id(0) < steps)
    def _():
        put(one_ref)

    @pl.when(pl.program_id(0) >= steps)
    def _():
        put(other_ref)


def input_back(first_sum, grads, weights, **waits):
    tokens, width = first_sum.shape
    rows = 256
    steps = grads[0].shape[1] // rows
    one = pl.BlockSpec((3, rows, width), lambda i, *_: (0, jnp.minimum(i, steps - 1), 0))
    other = pl.BlockSpec((3, rows, width), lambda i, *_: (0, jnp.maximum(i - steps, 0), 0))
    return call(
        functools.partial(input_kernel, steps),
        "input_grad",
        (tokens // rows,),
        [rows_spec(rows, width), one, other] + [full_spec((width, width))] * 3,
        [rows_spec(rows, width)],
        [shaped((tokens, width), jnp.float32)],
        [],
        6 * tokens * width * width,
        14 * tokens * width + 6 * width * width,
        (), first_sum, *grads, *weights, **waits,
    )


VECTOR_ROWS = 48


def encoded(values):
    high, rest = two_parts(values)
    return jnp.concatenate([high, rest], axis=0)


def decoded(block):
    block = block.astype(jnp.float32)
    return block[:VECTOR_ROWS] + block[VECTOR_ROWS:]


def bundle_kernel(numbers, first_ref, second_ref, one_ref, other_ref, send_ref, keep_ref, coded_ref, target_ref):
    width = first_ref.shape[1]
    third = target_ref.shape[1]
    pieces = width // third
    target_ref[...] = jnp.zeros_like(target_ref)

    def put(row, values):
        for piece in range(pieces):
            target_ref[pl.ds(row * pieces + piece, 1)] = values[:, piece * third : (piece + 1) * third]

    for row in range(2):
        put(row, one_ref[row : row + 1] + other_ref[row : row + 1])
    for row in range(3):
        put(2 + row, first_ref[row : row + 1])
        put(5 + row, second_ref[row : row + 1])
    for place in range(2):
        put(8 + matrix_at(place, 0, numbers), keep_ref[place, 0:1])
        put(8 + matrix_at(place, 1, numbers), send_ref[place, 0:1])
    coded_ref[0] = encoded(target_ref[...])


def bundle(numbers, first, second, one, other, send, keep, **waits):
    third = first.shape[1] // THIRDS
    return whole(
        bundle_kernel, "vector_grads", (numbers,), (first, second, one, other, send, keep),
        [shaped((1, 2 * VECTOR_ROWS, third), jnp.bfloat16)], [pltpu.VMEM((VECTOR_ROWS, third), jnp.float32)], 0, **waits,
    )


def unbundle_kernel(source_ref, *targets):
    third = source_ref.shape[2]
    values = decoded(source_ref[0])
    row = 0
    for target in targets:
        for piece in range(target.shape[0] // third):
            target[piece * third : (piece + 1) * third] = values[row : row + 1].reshape(third)
            row += 1


def unbundle(block, sizes_out, **waits):
    return whole(
        unbundle_kernel, "unbundle", (), (block,), [shaped((size,), jnp.float32) for size in sizes_out], [], 0, **waits
    )


def local(
    inputs,
    lengths,
    positives,
    query_weight,
    query_bias,
    key_weight,
    value_weight,
    value_bias,
    output_weight,
    output_bias,
    first_gain,
    first_shift,
    up_weight,
    up_bias,
    down_weight_,
    down_bias,
    second_gain,
    second_shift,
):
    row_count, row_span, width = inputs.shape[1:]
    seg_count = lengths.shape[2]
    tokens = row_count * row_span
    hidden_width = up_weight.shape[1]
    sizes = (lax.axis_size("stream"), lax.axis_size("batch"))
    rest = halving_orders(sizes[1])[1]
    x = inputs.reshape(tokens, width)
    lengths = lengths.reshape(row_count, seg_count)
    numbers = jnp.stack([lax.axis_index("stream"), lax.axis_index("batch")]).astype(jnp.int32)
    vectors = (query_bias, value_bias, output_bias, first_gain, first_shift, down_bias, second_gain, second_shift, up_bias)
    q, k, v, context, aux, vec, first_normed, hidden_low = attend(
        lengths, x, (query_weight, key_weight, value_weight, output_weight), vectors
    )
    activation, slope, second_normed, second_factor, pooled, package = feed(
        lengths, positives, first_normed, hidden_low, up_weight, down_weight_, vec
    )
    own, foreign = gather_embeddings(package, sizes)
    contrast_terms, pooled_grad = contrast(numbers, lengths, own, foreign, pooled, sizes)
    second_sum, branch_grad, second_totals = second_back(
        lengths, pooled_grad, second_normed, second_factor, vec
    )
    orders, rest = halving_orders(sizes[1])
    far = orders[0][3]
    parts = range(THIRDS)
    half = LABELS // 2

    def flat(value):
        return value.reshape((-1,) + value.shape[2:])

    def same_link(i, step, other):
        return [order[other] for order in orders].index(orders[i][step])

    def chip_sums(keep, arrived, start):
        return [[(half, (keep, i * LABELS + start), (arrived, i * LABELS + start))] for i in parts]

    def sums(kept, kept_at, arrived, arrived_at, size):
        send = (size, (kept, kept_at + size), (arrived, arrived_at + size))
        return [send], [(size, (kept, kept_at), (arrived, arrived_at))]

    def all_sums(kept, arrived, size):
        both = [sums(kept[i], 0, arrived[i], 0, size) for i in parts]
        return [one[0] for one in both], [one[1] for one in both]

    def joined(former, former_at, latter, latter_at, size):
        return [(size, (former, former_at)), (size, (latter, latter_at))]

    def for_rest(outs, order, name):
        for dim in rest:
            arrived = [exchange(array, dim, sizes) for array, _ in outs]
            *arrays, order = fold(
                [
                    [(size, (array, start), (other, start)) for size, start in terms]
                    for (array, terms), other in zip(outs, arrived, strict=True)
                ],
                order, name,
            )
            outs = [(array, terms) for array, (_, terms) in zip(arrays, outs, strict=True)]
        return [array for array, _ in outs], order

    order = second_totals
    down_send, order = down_weight(numbers, activation, branch_grad, 1, sizes, "down_weight_send", carry=(order,))
    down_in = exchange(down_send, CORE, sizes)
    down_keep, order = down_weight(numbers, activation, branch_grad, 0, sizes, "down_weight_keep", carry=(order,))
    keep, arrived = flat(down_keep), flat(down_in)
    *made, order = fold(chip_sums(keep, arrived, half) + chip_sums(keep, arrived, 0), order, "down_0")
    down_kept = made[THIRDS:]
    down_in = exchange_each(made[:THIRDS], 0, sizes)
    up_send, partial_grad, up_totals_send, order = up_back(
        numbers, branch_grad, slope, hidden_low, up_weight, down_weight_, second_sum, 1, sizes, "up_back_send",
        carry=(order,),
    )
    sends, keeps = all_sums(down_kept, down_in, 4)
    up_send = flat(up_send)
    *made, up_send, order = fold(sends + keeps + [[(THIRDS * LABELS, (up_send, 0))]], order, "down_1")
    up_in = exchange(up_send, CORE, sizes)
    down_kept = made[THIRDS:]
    down_in = exchange_each(made[:THIRDS], 1, sizes)
    up_keep, up_totals_keep, first_sum, attended_grad, first_totals, order = up_back(
        numbers, branch_grad, slope, hidden_low, up_weight, down_weight_, partial_grad, 0, sizes, "up_back_keep",
        (first_normed, aux, vec), carry=(order,),
    )
    keep, arrived = flat(up_keep), up_in
    pair = [same_link(i, 0, 2) for i in parts]
    down_sends, down_keeps = all_sums(down_kept, down_in, 2)
    sends = chip_sums(keep, arrived, half)
    *made, order = fold(
        [sends[i] + down_sends[pair[i]] for i in parts]
        + chip_sums(keep, arrived, 0)
        + [down_keeps[pair[i]] for i in parts],
        order, "up_0",
    )
    up_kept, down_kept = made[THIRDS : 2 * THIRDS], made[2 * THIRDS :]
    up_in = exchange_each(made[:THIRDS], 0, sizes)
    back = functools.partial(attend_back, lengths, q, k, v, attended_grad, output_weight, aux)
    grads_one, totals_one, order = back(0, 0, carry=(order,))
    grads_one, totals_one, order = back(0, 1, before=grads_one, carry=(order,))
    sends, keeps = all_sums(up_kept, up_in, 4)
    far_sums = [sums(down_kept[pair.index(i)], 0, up_in[pair.index(i)], half, 1) for i in parts]
    *made, down_far, down_kept, order = fold(
        sends + keeps + [sum([one[0] for one in far_sums], []), sum([one[1] for one in far_sums], [])], order, "up_1"
    )
    up_kept = made[THIRDS:]
    up_in = exchange_each(made[:THIRDS], 1, sizes)
    down_in = exchange(down_far, far, sizes)
    grads_other, totals_other, order = back(1, 0, carry=(order,))
    sends, keeps = all_sums(up_kept, up_in, 2)
    *made, down, order = fold(sends + keeps + [[(THIRDS, (down_kept, 0), (down_in, 0))]], order, "up_2")
    up_kept = made[THIRDS:]
    up_in = exchange_each(made[:THIRDS], 2, sizes)
    (down,), order = for_rest([(down, [(THIRDS, 0)])], order, "down_rest")
    down_in = exchange(down, far, sizes)
    grads_other, totals_other, order = back(1, 1, before=grads_other, carry=(order,))
    grads = (grads_one, grads_other)
    sends, keeps = all_sums(up_kept, up_in, 1)
    up_far, up_kept, *down, order = fold(
        [sum(sends, []), sum(keeps, [])] + [joined(down, i, down_in, i, 1) for i in parts], order, "up_3"
    )
    up_in = exchange(up_far, far, sizes)
    down_in = exchange_each(down, 2, sizes)
    mixed_send, order = mixed_weight(
        numbers, x, context, attended_grad, grads, 1, sizes, "mixed_weight_send", carry=(order,)
    )
    mixed_in = exchange(mixed_send, CORE, sizes)
    vector, order = bundle(
        numbers, first_totals, second_totals, totals_one, totals_other, up_totals_send, up_totals_keep, carry=(order,)
    )
    mixed_keep, order = mixed_weight(
        numbers, x, context, attended_grad, grads, 0, sizes, "mixed_weight_keep", carry=(order,)
    )
    keep, arrived = flat(mixed_keep), flat(mixed_in)
    code = [[(1, (vector, 0))], [], []]
    pair = [same_link(i, 0, 1) for i in parts]
    sends = chip_sums(keep, arrived, half)
    *made, up, order = fold(
        [sends[i] + code[i] + joined(down[pair[i]], 0, down_in[pair[i]], 0, 2) for i in parts]
        + chip_sums(keep, arrived, 0)
        + [[(THIRDS, (up_kept, 0), (up_in, 0))]],
        order, "mixed_0",
    )
    mixed, mixed_kept = made[:THIRDS], made[THIRDS:]
    mixed_in = exchange_each(mixed, 0, sizes)
    (up,), order = for_rest([(up, [(THIRDS, 0)])], order, "up_rest")
    up_in = exchange(up, far, sizes)
    input_grad, order = input_back(first_sum, grads, (query_weight, key_weight, value_weight), carry=(order,))
    sends, keeps = all_sums(mixed_kept, mixed_in, 4)
    code = [[(0, (mixed[0], half), (mixed_in[0], half))], [], []]
    skip = [half + 1, half, half]
    down = [joined(mixed[i], skip[i], mixed_in[i], skip[i], 4) for i in (pair.index(j) for j in parts)]
    pair = [same_link(i, 1, 2) for i in parts]
    other = [same_link(i, 1, 0) for i in parts]
    *made, order = fold(
        [sends[i] + code[i] + joined(up, pair[i], up_in, pair[i], 1) + down[other[i]] for i in parts] + keeps,
        order, "mixed_1",
    )
    mixed, mixed_kept = made[:THIRDS], made[THIRDS:]
    mixed_in = exchange_each(mixed, 1, sizes)
    at = [(other.index(j), 7 if other.index(j) == 0 else 6) for j in parts]
    down, down_in = [(mixed[i], start) for i, start in at], [(mixed_in[i], start) for i, start in at]
    sends, keeps = all_sums(mixed_kept, mixed_in, 2)
    code = [[(0, (mixed[0], 4), (mixed_in[0], 4))], [], []]
    skip = [5, 4, 4]
    up = [joined(mixed[i], skip[i], mixed_in[i], skip[i], 2) for i in (pair.index(j) for j in parts)]
    pair = [same_link(i, 2, 1) for i in parts]
    *made, order = fold([sends[i] + code[i] + up[pair[i]] for i in parts] + keeps, order, "mixed_2")
    mixed, mixed_kept = made[:THIRDS], made[THIRDS:]
    mixed_in = exchange_each(mixed, 2, sizes)
    down, order = fold([sum([[(half, down[i]), (half, down_in[i])] for i in parts], [])], order, "down_2")
    down = [down, exchange(down, CORE, sizes)]
    code = [(0, (mixed[0], 2), (mixed_in[0], 2))]
    skip = [3, 2, 2]
    up = [joined(mixed[i], skip[i], mixed_in[i], skip[i], 4) for i in (pair.index(j) for j in parts)]
    whole_sums = sum([[(2, (mixed_kept[i], 0), (mixed_in[i], 0))] for i in parts], [])
    mixed, *up, order = fold([whole_sums + code] + up, order, "mixed_3")
    mixed_in = exchange(mixed, far, sizes)
    up_in = exchange_each(up, 0, sizes)
    down_total, order = spread(numbers, down, "tall", "down_spread", sizes, carry=(order,))
    crossed = [[(1, (mixed, 2 * i), (mixed_in, 2 * i + 1)), (1, (mixed, 2 * i + 1), (mixed_in, 2 * i))] for i in parts]
    *mixed, vector, order = fold(crossed + [[(0, (mixed, 2 * THIRDS), (mixed_in, 2 * THIRDS))]], order, "mixed_4")
    (*mixed, vector), order = for_rest(
        [(value, [(2, 0)]) for value in mixed] + [(vector, [(0, 0)])], order, "mixed_rest"
    )
    mixed_in = exchange_each(mixed, 2, sizes)
    vector, order = fold([[(0, (vector, 0), (exchange(vector, CORE, sizes), 0))]], order, "vector_sums")
    *summed, order = unbundle(vector, [width] * 8 + [hidden_width], carry=(order,))
    up, order = fold([sum([joined(up[i], 0, up_in[i], 0, half) for i in parts], [])], order, "up_4")
    up = [up, exchange(up, CORE, sizes)]
    *mixed, order = fold([joined(mixed[i], 0, mixed_in[i], 0, 2) for i in parts], order, "mixed_5")
    mixed_in = exchange_each(mixed, 1, sizes)
    *mixed, order = fold([joined(mixed[i], 0, mixed_in[i], 0, 4) for i in parts], order, "mixed_6")
    mixed_in = exchange_each(mixed, 0, sizes)
    up_total, order = spread(numbers, up, "wide", "up_spread", sizes, carry=(order,))
    mixed, order = fold([sum([joined(mixed[i], 0, mixed_in[i], 0, half) for i in parts], [])], order, "mixed_7")
    blocks = [mixed, exchange(mixed, CORE, sizes)]
    query_total, key_total, value_total, output_total = spread(
        numbers, blocks, "separate", "mixed_spread", sizes, after=(order,)
    )
    return (
        contrast_terms.reshape(1, row_count * seg_count),
        input_grad.reshape(1, row_count, row_span, width),
        query_total,
        summed[0],
        key_total,
        value_total,
        summed[1],
        output_total,
        summed[2],
        summed[3],
        summed[4],
        up_total,
        summed[8],
        down_total.reshape(hidden_width, width),
        summed[5],
        summed[6],
        summed[7],
    )


def solution(mesh):
    return jax.shard_map(
        local,
        mesh=mesh,
        in_specs=(
            P("stream", "batch", None, None),
            P("stream", "batch", None),
            P("batch"),
            P(),
            P(),
            P(),
            P(),
            P(),
            P(),
            P(),
            P(),
            P(),
            P(),
            P(),
            P(),
            P(),
            P(),
            P(),
        ),
        out_specs=(
            P("stream", "batch"),
            P("stream", "batch", None, None),
            P(),
            P(),
            P(),
            P(),
            P(),
            P(),
            P(),
            P(),
            P(),
            P(),
            P(),
            P(),
            P(),
            P(),
            P(),
        ),
        check_vma=False,
    )
```

```python
import functools

import jax
import jax.numpy as jnp
import numpy as np
from jax import lax
from jax.experimental import pallas as pl
from jax.experimental.pallas import tpu as pltpu
from jax.sharding import PartitionSpec as P

HEAD_DIM = 64
MIB = 2**20
FOLD_LIMIT = 16
TILE = 512
LABELS = 16
THIRDS = 3
BOTH = ("stream", "batch")


def link_dims(batch_size):
    bits = batch_size.bit_length() - 1
    main = [("stream", 1), ("batch", 2), ("batch", 1 << (bits - 2)), ("batch", 3 << (bits - 2))]
    rest = [("batch", 1 << j) for j in range(2, bits - 2)]
    return main, rest


def coordinate(dim, stream, batch, batch_size):
    bits = batch_size.bit_length() - 1
    if dim[0] == "stream":
        return stream
    mask = dim[1]
    top = (batch >> (bits - 1)) & 1
    if mask == 3 << (bits - 2):
        return top
    if mask == 1 << (bits - 2):
        return ((batch >> (bits - 2)) & 1) ^ top
    return (batch >> (mask.bit_length() - 1)) & 1


def flipped(dim, stream, batch):
    return (stream ^ 1, batch) if dim[0] == "stream" else (stream, batch ^ dim[1])


def exchange(array, even_dim, sizes, odd_dim=None):
    odd_dim = odd_dim or even_dim
    pairs = []
    for stream in range(sizes[0]):
        for batch in range(sizes[1]):
            other = flipped(odd_dim if batch & 1 else even_dim, stream, batch)
            pairs.append((stream * sizes[1] + batch, other[0] * sizes[1] + other[1]))
    return lax.ppermute(array, BOTH, pairs)


CORE = ("batch", 1)


def halving_orders(batch_size):
    (x, y, a, b), rest = link_dims(batch_size)
    return ((x, y, a, b), (y, a, x, b), (a, x, y, b)), rest


def gather_orders(batch_size):
    (x, y, a, b), rest = link_dims(batch_size)
    return tuple(rest) + (b, a, x, y), tuple(rest) + (b, x, y, a)


def labels_of(stream, batch, batch_size):
    labels = []
    for order in halving_orders(batch_size)[0]:
        label = 0
        for dim in order:
            label = label * 2 + coordinate(dim, stream, batch, batch_size)
        labels.append(label)
    return labels


def place_at(order_even, order_odd, place, numbers):
    stream, batch = numbers[0], numbers[1]
    core = batch & 1
    for step, (even_dim, odd_dim) in enumerate(zip(order_even, order_odd, strict=True)):
        bit = (place >> step) & 1
        even = (bit, 0) if even_dim[0] == "stream" else (0, bit * even_dim[1])
        odd = (bit, 0) if odd_dim[0] == "stream" else (0, bit * odd_dim[1])
        stream = stream ^ jnp.where(core == 0, even[0], odd[0])
        batch = batch ^ jnp.where(core == 0, even[1], odd[1])
    return stream, batch


def full_spec(shape):
    return pl.BlockSpec(shape, lambda *_: (0,) * len(shape))


def added(former, latter):
    return (former.astype(jnp.float32) + latter.astype(jnp.float32)).astype(jnp.bfloat16)


def split(value):
    half = value.shape[0] // 2
    return value[half:], value[:half]


def fold_kernel(plan, *refs):
    count = len(refs) - len(plan)
    for terms, target in zip(plan, refs[count:], strict=True):
        for place, size, coded, sources in terms:
            if coded:
                values = sum(decoded(refs[number][start]) for number, start in sources)
                target[place] = encoded(values)
            elif len(sources) == 1:
                number, start = sources[0]
                target[place : place + size] = refs[number][start : start + size]
            else:
                values = sum(refs[number][start : start + size].astype(jnp.float32) for number, start in sources)
                target[place : place + size] = low(values)


def fold(outs, order, name):
    arrays, plan, shapes = [], [], []
    for out in outs:
        place, terms = 0, []
        for size, *sources in out:
            numbered = []
            for array, start in sources:
                found = [n for n, other in enumerate(arrays) if other is array]
                if not found:
                    arrays.append(array)
                numbered.append((found[0] if found else len(arrays) - 1, start))
            terms.append((place, max(size, 1), size == 0, tuple(numbered)))
            place += max(size, 1)
        plan.append(tuple(terms))
        shapes.append(shaped((place,) + arrays[0].shape[1:], jnp.bfloat16))
    return whole(functools.partial(fold_kernel, plan), name, (), arrays, shapes, [], 0, carry=(order,), limit=FOLD_LIMIT)


def exchange_each(values, step, sizes):
    orders, _ = halving_orders(sizes[1])
    return [exchange(values[i], orders[i][step], sizes) for i in range(THIRDS)]


def spread_kernel(kind, batch_size, numbers, *refs):
    sources, targets = refs[: 2 * THIRDS], refs[2 * THIRDS :]
    core = numbers[1] & 1
    labels = labels_of(numbers[0], numbers[1], batch_size)
    _, rows, third = sources[0].shape
    rows = rows // 2
    for matrix in range(4):

        def put(first, matrix=matrix):
            for part in range(THIRDS):
                for own in range(4):
                    value = sources[first + part][own ^ (labels[part] & 3), (matrix % 2) * rows : (matrix % 2 + 1) * rows]
                    value = value.astype(jnp.float32)
                    at, columns = slice(own * rows, (own + 1) * rows), slice(part * third, (part + 1) * third)
                    if kind == "tall":
                        targets[0][matrix, at, columns] = value
                    elif kind == "wide":
                        start = (matrix * THIRDS + part) * third
                        targets[0][at, start : start + third] = value
                    else:
                        targets[matrix][at, columns] = value

        @pl.when(core == matrix // 2)
        def _():
            put(0)

        @pl.when(core != matrix // 2)
        def _():
            put(THIRDS)


def spread(numbers, blocks, kind, name, sizes, **waits):
    third = blocks[0].shape[2]
    width = THIRDS * third
    rows = 2 * width // LABELS
    group = 2 * rows

    groups = LABELS // 4

    def source_spec(part):
        def at(i, numbers):
            return ((i ^ (labels_of(numbers[0], numbers[1], sizes[1])[part] >> 2)) + part * groups, 0, 0)

        return pl.BlockSpec((4, rows, third), at)

    if kind == "tall":
        specs = [pl.BlockSpec((4, group, width), lambda i, *_: (0, i, 0))]
        shapes = [shaped((4, width, width), jnp.float32)]
    elif kind == "wide":
        specs = [pl.BlockSpec((group, 4 * width), lambda i, *_: (i, 0))]
        shapes = [shaped((width, 4 * width), jnp.float32)]
    else:
        specs = [pl.BlockSpec((group, width), lambda i, *_: (i, 0))] * 4
        shapes = [shaped((width, width), jnp.float32)] * 4
    return call(
        functools.partial(spread_kernel, kind, sizes[1]),
        name,
        (LABELS // 4,),
        [source_spec(part % THIRDS) for part in range(2 * THIRDS)],
        specs, shapes, [],
        0,
        24 * width * width,
        (numbers,), *[blocks[0]] * THIRDS, *[blocks[1]] * THIRDS, **waits,
    )


def gather_embeddings(own, sizes):
    orders = gather_orders(sizes[1])
    value = own[None]
    for even_dim, odd_dim in zip(*orders, strict=True):
        value = jnp.concatenate([value, exchange(value, even_dim, sizes, odd_dim)], axis=0)
    return value, exchange(value, CORE, sizes)


BAND = 64
STEP = 128
WINDOW = STEP + 2 * BAND
QUERY_BIAS, VALUE_BIAS, OUTPUT_BIAS, FIRST_GAIN, FIRST_SHIFT, DOWN_BIAS, SECOND_GAIN, SECOND_SHIFT, UP_BIAS = range(9)


def dots(former, latter):
    return lax.dot_general(former, latter, (((1,), (1,)), ((), ())), preferred_element_type=jnp.float32)


def product(former, latter):
    return jnp.dot(former, latter, preferred_element_type=jnp.float32)


def transposed(former, latter):
    return lax.dot_general(former, latter, (((0,), (0,)), ((), ())), preferred_element_type=jnp.float32)


def low(values):
    return values.astype(jnp.bfloat16)


def call(kernel, name, grid, in_specs, out_specs, out_shape, scratch, flops, moved, scalars, *args, after=(), carry=(), limit=16):
    taken, given = len(scalars) + len(in_specs), len(out_specs)
    waits = len(after) + len(carry)

    def run(*refs):
        kernel(*refs[:taken], *refs[taken + waits : taken + waits + given], *refs[taken + waits + given + len(carry) :])

    anywhere = pl.BlockSpec(memory_space=pl.ANY)
    return pl.pallas_call(
        run,
        grid_spec=pltpu.PrefetchScalarGridSpec(
            num_scalar_prefetch=len(scalars),
            grid=grid,
            in_specs=list(in_specs) + [anywhere] * waits,
            out_specs=list(out_specs) + [anywhere] * len(carry),
            scratch_shapes=scratch,
        ),
        out_shape=list(out_shape) + [shaped(value.shape, value.dtype) for value in carry],
        input_output_aliases={taken + len(after) + i: given + i for i in range(len(carry))},
        compiler_params=pltpu.CompilerParams(vmem_limit_bytes=limit * MIB),
        cost_estimate=pl.CostEstimate(flops=flops, bytes_accessed=moved, transcendentals=0),
        name=name,
    )(*scalars, *args, *after, *carry)


def whole(kernel, name, scalars, args, outs, scratch, flops, after=(), carry=(), far=(), far_outs=(), limit=12):
    taken, given = len(scalars) + len(args), len(outs)
    waits = len(after) + len(carry)

    def run(*refs):
        kernel(*refs[:taken], *refs[taken + waits : taken + waits + given], *refs[taken + waits + given + len(carry) :])

    near, remote = pl.BlockSpec(memory_space=pltpu.VMEM), pl.BlockSpec(memory_space=pltpu.HBM)
    anywhere = pl.BlockSpec(memory_space=pl.ANY)
    moved = sum(a.size * a.dtype.itemsize for a in args) + sum(o.size * o.dtype.itemsize for o in outs)
    args = [pltpu.with_memory_space_constraint(a, pltpu.HBM) if i in far else a for i, a in enumerate(args)]
    out_shape = [pltpu.HBM(o.shape, o.dtype) if i in far_outs else o for i, o in enumerate(outs)]
    return pl.pallas_call(
        run,
        in_specs=[pl.BlockSpec(memory_space=pltpu.SMEM)] * len(scalars)
        + [remote if i in far else near for i in range(len(args))]
        + [anywhere] * waits,
        out_specs=[remote if i in far_outs else near for i in range(given)] + [anywhere] * len(carry),
        out_shape=out_shape + [shaped(value.shape, value.dtype) for value in carry],
        scratch_shapes=scratch,
        input_output_aliases={taken + len(after) + i: given + i for i in range(len(carry))},
        compiler_params=pltpu.CompilerParams(vmem_limit_bytes=limit * MIB),
        cost_estimate=pl.CostEstimate(flops=flops, bytes_accessed=moved, transcendentals=0),
        name=name,
    )(*scalars, *args, *after, *carry)


def shaped(shape, dtype):
    return jax.ShapeDtypeStruct(shape, dtype)


def rows_spec(rows, width):
    return pl.BlockSpec((rows, width), lambda i, *_: (i, 0))


def segment_of(lengths, row, count, shape, dim):
    place = lax.broadcasted_iota(jnp.int32, shape, dim)
    total, ids = 0, jnp.zeros(shape, jnp.int32)
    for j in range(count):
        total = total + lengths[row, j]
        ids = ids + (place >= total).astype(jnp.int32)
    return ids


def window_start(block, span):
    return min(max(block * STEP - BAND, 0), span - WINDOW)


def fill_bias(lengths, row, count, span, bias_ref, first=0):
    down = segment_of(lengths, row, count, (span, 128), 0)
    along = segment_of(lengths, row, count, (8, span), 1)
    for block in range(span // STEP):
        start = window_start(block, span)
        same = down[block * STEP : (block + 1) * STEP, 0:1] == along[0:1, start : start + WINDOW]
        bias_ref[first + block] = jnp.where(same, 0.0, -1e9)


def head_masks(scale):
    lane = lax.broadcasted_iota(jnp.int32, (1, 2 * HEAD_DIM), 1)
    first = low(jnp.where(lane < HEAD_DIM, scale, 0.0))
    second = low(jnp.where(lane < HEAD_DIM, 0.0, scale))
    return first, second


def stacked(values, masks):
    return jnp.concatenate([values * masks[0], values * masks[1]], axis=0)


def merged(values):
    lane = lax.broadcasted_iota(jnp.int32, (STEP, 2 * HEAD_DIM), 1)
    return jnp.where(lane < HEAD_DIM, values[:STEP], values[STEP:])


def biased(scores, bias):
    return (scores.reshape(2, STEP, WINDOW) + bias[None]).reshape(2 * STEP, WINDOW)


def normalised(values):
    centred = values - jnp.mean(values, axis=-1, keepdims=True)
    factor = lax.rsqrt(jnp.mean(centred * centred, axis=-1, keepdims=True) + 1e-12)
    return centred * factor, factor


def norm_back(gradient, normed, factor, gain):
    inner = gradient * gain
    centred = inner - jnp.mean(inner, axis=-1, keepdims=True)
    return factor * (centred - normed * jnp.mean(inner * normed, axis=-1, keepdims=True))


def contrast_kernel(scale, sizes, numbers, lengths, own_ref, foreign_ref, pooled_ref, terms_ref, grad_ref, all_ref, digits_ref, totals_ref):
    half, texts, wide = own_ref.shape
    width = pooled_ref.shape[1]
    total = all_ref.shape[1]
    stream, batch = numbers[0], numbers[1]
    orders = gather_orders(sizes[1])

    def place(source, from_stream, from_batch, i):
        at = pl.multiple_of(from_batch * texts, texts)
        other = from_stream ^ stream
        all_ref[other, pl.ds(at, texts)] = source[i, :, :width]

        @pl.when(other == 1)
        def _():
            digits_ref[pl.ds(at, texts)] = source[i, :, width:]

    def place_both(i, carry):
        place(own_ref, *place_at(*orders, i, (stream, batch)), i)
        place(foreign_ref, *place_at(*orders, i, (stream, batch ^ 1)), i)
        return carry

    lax.fori_loop(0, half, place_both, 0)

    tile = min(TILE, total)
    totals_ref[...] = jnp.zeros_like(totals_ref)
    for column in range(total // tile):
        latter = all_ref[1, column * tile : (column + 1) * tile]

        def add(i, carry, latter=latter, column=column):
            former = all_ref[0, pl.ds(pl.multiple_of(i * tile, tile), tile)]
            sums = jnp.sum(jnp.exp(dots(former, latter) / 0.05), axis=0, keepdims=True)
            totals_ref[:, column * tile : (column + 1) * tile] += sums
            return carry

        lax.fori_loop(0, total // tile, add, 0)
    mine = all_ref[0, pl.ds(pl.multiple_of(batch * texts, texts), texts)]
    partners = all_ref[1]
    own_digits = own_ref[0, :, width:]
    logits = dots(mine, partners) / 0.05
    exponent = jnp.exp(logits)
    row_total = jnp.sum(exponent, axis=1, keepdims=True)
    own_target = (64.0 * own_digits[:, 0:1].astype(jnp.float32) + own_digits[:, 1:2].astype(jnp.float32)).astype(jnp.int32)
    lane = lax.broadcasted_iota(jnp.int32, (8, 128), 1)
    pick = jnp.where(lane == 0, 64.0, jnp.where(lane == 1, 1.0, 0.0)).astype(jnp.bfloat16)
    all_target = dots(pick, digits_ref[...])[0:1].astype(jnp.int32)
    columns = lax.broadcasted_iota(jnp.int32, (texts, total), 1)
    rows = batch * texts + lax.broadcasted_iota(jnp.int32, (texts, total), 0)
    query_hit = (own_target == columns).astype(jnp.float32)
    doc_hit = (all_target == rows).astype(jnp.float32)
    target = jnp.where(stream == 0, query_hit, doc_hit)
    chosen = jnp.sum(logits * target, axis=1, keepdims=True)
    terms_ref[...] = jnp.broadcast_to(jnp.log(row_total) - chosen, terms_ref.shape)
    own_low = ((exponent / row_total - target) * scale).astype(jnp.bfloat16)
    cross_low = ((exponent / totals_ref[0:1, :] - target) * scale).astype(jnp.bfloat16)
    gradient = (
        jnp.dot(own_low, partners, preferred_element_type=jnp.float32)
        + jnp.dot(cross_low, partners, preferred_element_type=jnp.float32)
    ) / 0.05
    gradient = gradient.astype(jnp.bfloat16).astype(jnp.float32)
    pooled = pooled_ref[...]
    inverse_norm = lax.rsqrt(jnp.sum(pooled * pooled, axis=1, keepdims=True) + 1e-06)
    embedding = pooled * inverse_norm
    inner = jnp.sum(gradient * embedding, axis=1, keepdims=True)
    count = texts // lengths.shape[0]
    divisor = jnp.concatenate([length_column(lengths, row, count) for row in range(lengths.shape[0])], axis=0)
    grad_ref[...] = inverse_norm * (gradient - embedding * inner) / divisor


def contrast(numbers, lengths, own, foreign, pooled, sizes):
    _, texts, wide = own.shape
    width = pooled.shape[1]
    total = sizes[1] * texts
    terms, gradient = whole(
        functools.partial(contrast_kernel, 1.0 / (2.0 * total), sizes),
        "contrast",
        (numbers, lengths),
        (own, foreign, pooled),
        [shaped((texts, 128), jnp.float32), shaped(pooled.shape, jnp.float32)],
        [
            pltpu.VMEM((2, total, width), jnp.bfloat16),
            pltpu.VMEM((total, wide - width), jnp.bfloat16),
            pltpu.VMEM((8, total), jnp.float32),
        ],
        2 * total * total * width,
        limit=max(12, 8 + total * width // 2**16),
    )
    return terms[:, 0], gradient


def attend_kernel(count, lengths, x_in, wq_in, wk_in, wv_in, wo_in, *refs):
    vectors_in, refs = refs[:9], refs[9:]
    q_out, k_out, v_out, ctx_out, aux_out, vec_ref, normed_ref, hidden_ref = refs[:8]
    x_ref, w_ref, wide_ref, q_ref, k_ref, v_ref, ctx_ref, aux_ref, bias_ref, sems = refs[8:]
    tokens, width = x_ref.shape
    row_count = lengths.shape[0]
    span = tokens // row_count
    places, at = [], 0
    for vector in vectors_in:
        places.append(at)
        at += vector.shape[0]
    loads = [pltpu.make_async_copy(x_in, x_ref, sems.at[0]), pltpu.make_async_copy(wq_in, w_ref.at[0], sems.at[1])]
    small = [
        pltpu.make_async_copy(vector, wide_ref.at[pl.ds(place, vector.shape[0])], sems.at[5 + i])
        for i, (vector, place) in enumerate(zip(vectors_in, places, strict=True))
    ]
    loads += [pltpu.make_async_copy(w, w_ref.at[i], sems.at[1 + i]) for i, w in ((1, wk_in), (2, wv_in), (3, wo_in))]
    for copy in loads[:2] + small + loads[2:]:
        copy.start()
    for row in range(row_count):
        fill_bias(lengths, row, count, span, bias_ref, row * (span // STEP))
    for copy in small:
        copy.wait()
    flat = wide_ref[...].astype(jnp.float32)
    for row in range(vec_ref.shape[0]):
        vec_ref[row : row + 1] = flat[row * width : (row + 1) * width].reshape(1, width)
    loads[0].wait()
    stores = [
        pltpu.make_async_copy(ref, out, sems.at[14 + i])
        for i, (ref, out) in enumerate(
            ((q_ref, q_out), (k_ref, k_out), (v_ref, v_out), (ctx_ref, ctx_out), (aux_ref, aux_out))
        )
    ]
    for i, (ref, bias) in enumerate(((q_ref, QUERY_BIAS), (k_ref, None), (v_ref, VALUE_BIAS))):
        loads[1 + i].wait()
        for row in range(row_count):
            rows = slice(row * span, (row + 1) * span)
            values = product(x_ref[rows], w_ref[i])
            ref[rows] = low(values if bias is None else values + vec_ref[bias : bias + 1])
        stores[i].start()
    masks = head_masks(HEAD_DIM**-0.5)
    aux_ref[...] = jnp.zeros_like(aux_ref)
    pairs = width // (2 * HEAD_DIM)

    def heads(step, carry):
        row, pair = step // pairs, step % pairs
        at = pl.ds(pl.multiple_of(pair * 2 * HEAD_DIM, 2 * HEAD_DIM), 2 * HEAD_DIM)
        lane = lax.broadcasted_iota(jnp.int32, (STEP, 128), 1)
        blocks = range(span // STEP)
        rows = [pl.ds(pl.multiple_of(row * span + block * STEP, STEP), STEP) for block in blocks]
        keys = [pl.ds(pl.multiple_of(row * span + window_start(block, span), BAND), WINDOW) for block in blocks]
        scores = [dots(stacked(q_ref[rows[b], at], masks), k_ref[keys[b], at]) for b in blocks]
        scores = [biased(scores[b], bias_ref[row * (span // STEP) + b]) for b in blocks]
        highest = [jnp.max(value, axis=1, keepdims=True) for value in scores]
        exponent = [jnp.exp(scores[b] - highest[b]) for b in blocks]
        total = [jnp.sum(value, axis=1, keepdims=True) for value in exponent]
        attention = [low(exponent[b] * (1.0 / total[b])) for b in blocks]
        for b in blocks:
            ctx_ref[rows[b], at] = low(merged(product(attention[b], v_ref[keys[b], at])))
        for b in blocks:
            log_total = highest[b] + jnp.log(total[b])
            kept = jnp.where(lane == 2 * pair, log_total[:STEP], aux_ref[rows[b]])
            aux_ref[rows[b]] = jnp.where(lane == 2 * pair + 1, log_total[STEP:], kept)
        return carry

    lax.fori_loop(0, row_count * pairs, heads, 0)
    stores[3].start()
    loads[4].wait()
    for row in range(row_count):
        rows = slice(row * span, (row + 1) * span)
        attended = product(ctx_ref[rows], w_ref[3]) + vec_ref[OUTPUT_BIAS : OUTPUT_BIAS + 1]
        normed, factor = normalised(x_ref[rows].astype(jnp.float32) + attended)
        normed_ref[rows] = normed
        hidden_ref[rows] = low(normed * vec_ref[FIRST_GAIN : FIRST_GAIN + 1] + vec_ref[FIRST_SHIFT : FIRST_SHIFT + 1])
        lane = lax.broadcasted_iota(jnp.int32, (span, 128), 1)
        aux_ref[rows] = jnp.where(lane == 127, factor, aux_ref[rows])
    stores[4].start()
    for copy in stores:
        copy.wait()


def attend(lengths, x, weights, vectors):
    tokens, width = x.shape
    row_count = lengths.shape[0]
    span = tokens // row_count
    vector_rows = sum(vector.shape[0] for vector in vectors) // width
    square = shaped((tokens, width), jnp.bfloat16)
    token_scratch = pltpu.VMEM((tokens, width), jnp.bfloat16)
    return whole(
        functools.partial(attend_kernel, lengths.shape[1]),
        "attend",
        (lengths,),
        (x, *weights, *vectors),
        [square] * 4
        + [
            shaped((tokens, 128), jnp.float32),
            shaped((vector_rows, width), jnp.float32),
            shaped((tokens, width), jnp.float32),
            square,
        ],
        [token_scratch, pltpu.VMEM((4, width, width), jnp.bfloat16), pltpu.VMEM((vector_rows * width,), jnp.bfloat16)]
        + [token_scratch] * 4
        + [pltpu.VMEM((tokens, 128), jnp.float32)]
        + [pltpu.VMEM((row_count * span // STEP, STEP, WINDOW), jnp.float32), pltpu.SemaphoreType.DMA((19,))],
        8 * tokens * width * width + 4 * tokens * WINDOW * width,
        far=range(5 + len(vectors)),
        far_outs=range(5),
        limit=24,
    )


def gelu_and_slope(values):
    size = jnp.abs(values)
    part = 1.0 / (1.0 + (0.3275911 * 0.5**0.5) * size)
    bell = jnp.exp(values * values * -0.5)
    series = part * (0.5 * 0.254829592 + part * (-0.5 * 0.284496736 + part * (0.5 * 1.421413741 + part * (-0.5 * 1.453152027 + part * (0.5 * 1.061405429)))))
    tail = series * bell
    share = jnp.where(values < 0.0, tail, 1.0 - tail)
    return values * share, share + values * bell * 0.3989422804014327


def two_parts(values):
    high = low(values)
    return high, low(values - high.astype(jnp.float32))


def membership(lengths, row, count, rows, offset):
    place = lax.broadcasted_iota(jnp.int32, (count, rows), 1) + offset
    text = lax.broadcasted_iota(jnp.int32, (count, rows), 0)
    total = 0
    inside = jnp.zeros((count, rows), jnp.float32)
    for j in range(count):
        start, total = total, total + lengths[row, j]
        inside = jnp.where((text == j) & (place >= start) & (place < total), 1.0, inside)
    return low(inside)


def length_column(lengths, row, count):
    text = lax.broadcasted_iota(jnp.int32, (count, 128), 0)
    column = jnp.zeros((count, 128), jnp.float32)
    for j in range(count):
        column = jnp.where(text == j, lengths[row, j].astype(jnp.float32), column)
    return column[:, 0:1]


def feed_kernel(count, lengths, positives, normed_ref, hidden_ref, up_ref, down_ref, vec_ref, act_out, slope_out, second_ref, factor_ref, pooled_ref, package_ref, act_ref, slope_ref, sems):
    tokens, width = normed_ref.shape
    row_count = lengths.shape[0]
    span = tokens // row_count
    rows = 256
    parts = span // rows
    pooled_ref[...] = jnp.zeros_like(pooled_ref)

    def copies(step, slot):
        here = pl.ds(pl.multiple_of(step * rows, rows), rows)
        return (
            pltpu.make_async_copy(act_ref.at[slot], act_out.at[here], sems.at[0, slot]),
            pltpu.make_async_copy(slope_ref.at[slot], slope_out.at[here], sems.at[1, slot]),
        )

    def block(step, carry):
        row, part = step // parts, step % parts
        here = pl.ds(pl.multiple_of(step * rows, rows), rows)
        slot = step % 2
        stores = copies(step, slot)

        @pl.when(step >= 2)
        def _():
            for copy in copies(step - 2, slot):
                copy.wait()

        hidden_low = hidden_ref[here]
        branch = jnp.zeros((rows, width), jnp.float32)
        pieces = up_ref.shape[1] // width
        spots = [slice(piece * width, (piece + 1) * width) for piece in range(pieces)]
        later = product(hidden_low, up_ref[:, spots[0]])
        done = None
        for piece, at in enumerate(spots):
            values = later + vec_ref[UP_BIAS + piece : UP_BIAS + piece + 1]
            if piece + 1 < pieces:
                later = product(hidden_low, up_ref[:, spots[piece + 1]])
            if done is not None:
                branch = branch + product(done, down_ref[spots[piece - 1]])
            activation, slope = gelu_and_slope(values)
            done = low(activation)
            act_ref[slot, :, at] = done
            slope_ref[slot, :, at] = low(slope)
        branch = branch + product(done, down_ref[spots[-1]])
        for copy in stores:
            copy.start()
        hidden = normed_ref[here] * vec_ref[FIRST_GAIN : FIRST_GAIN + 1] + vec_ref[FIRST_SHIFT : FIRST_SHIFT + 1]
        normed, factor = normalised(hidden + branch + vec_ref[DOWN_BIAS : DOWN_BIAS + 1])
        second_ref[here] = normed
        factor_ref[here] = jnp.broadcast_to(factor, (rows, 128))
        high, rest = two_parts(normed * vec_ref[SECOND_GAIN : SECOND_GAIN + 1] + vec_ref[SECOND_SHIFT : SECOND_SHIFT + 1])
        inside = membership(lengths, row, count, rows, part * rows)
        texts = pl.ds(pl.multiple_of(row * count, count), count)
        pooled_ref[texts] += product(inside, high) + product(inside, rest)
        return carry

    lax.fori_loop(0, tokens // rows, block, 0)
    text = lax.broadcasted_iota(jnp.int32, (count, 128), 0)
    lane = lax.broadcasted_iota(jnp.int32, (count, 128), 1)
    for row in range(row_count):
        texts = slice(row * count, (row + 1) * count)
        pooled = pooled_ref[texts] / length_column(lengths, row, count)
        pooled_ref[texts] = pooled
        inverse_norm = lax.rsqrt(jnp.sum(pooled * pooled, axis=1, keepdims=True) + 1e-06)
        package_ref[texts, :width] = low(pooled * inverse_norm)
        digits = jnp.zeros((count, 128), jnp.int32)
        for j in range(count):
            own = positives[row * count + j]
            digits = jnp.where(text == j, jnp.where(lane == 0, own >> 6, own & 63), digits)
        package_ref[texts, width:] = low(jnp.where(lane < 2, digits, 0).astype(jnp.float32))
    steps = tokens // rows
    for step in range(steps - 2, steps):
        for copy in copies(step, step % 2):
            copy.wait()


def feed(lengths, positives, normed, hidden_low, up, down, vec):
    tokens, width = normed.shape
    texts, hidden = lengths.size, up.shape[1]
    return whole(
        functools.partial(feed_kernel, lengths.shape[1]),
        "feed",
        (lengths, positives),
        (normed, hidden_low, up, down, vec),
        [
            shaped((tokens, hidden), jnp.bfloat16),
            shaped((tokens, hidden), jnp.bfloat16),
            shaped((tokens, width), jnp.float32),
            shaped((tokens, 128), jnp.float32),
            shaped((texts, width), jnp.float32),
            shaped((texts, width + 128), jnp.bfloat16),
        ],
        [pltpu.VMEM((2, 256, hidden), jnp.bfloat16)] * 2 + [pltpu.SemaphoreType.DMA((2, 2))],
        4 * tokens * width * hidden,
        far_outs=(0, 1),
        limit=16,
    )


def sums_of(values):
    return jnp.sum(values, axis=0, keepdims=True)


def second_back_kernel(count, lengths, grad_ref, normed_ref, factor_ref, vec_ref, sum_ref, low_ref, totals_ref):
    tokens, width = normed_ref.shape
    row_count = lengths.shape[0]
    span = tokens // row_count
    totals_ref[...] = jnp.zeros_like(totals_ref)
    for row in range(row_count):
        rows = slice(row * span, (row + 1) * span)
        inside = membership(lengths, row, count, span, 0)
        high, rest = two_parts(grad_ref[row * count : (row + 1) * count])
        result_grad = transposed(inside, high) + transposed(inside, rest)
        normed = normed_ref[rows]
        second_sum = norm_back(result_grad, normed, factor_ref[rows, 0:1], vec_ref[SECOND_GAIN : SECOND_GAIN + 1])
        branch_grad = low(second_sum)
        sum_ref[rows] = second_sum
        low_ref[rows] = branch_grad
        totals_ref[0:1] += sums_of(branch_grad.astype(jnp.float32))
        totals_ref[1:2] += sums_of(result_grad * normed)
        totals_ref[2:3] += sums_of(result_grad)


def second_back(lengths, grad, normed, factor, vec):
    tokens, width = normed.shape
    return whole(
        functools.partial(second_back_kernel, lengths.shape[1]),
        "second_norm_back",
        (lengths,),
        (grad, normed, factor, vec),
        [shaped((tokens, width), jnp.float32), shaped((tokens, width), jnp.bfloat16), shaped((8, width), jnp.float32)],
        [],
        8 * tokens * width,
    )


def matrix_at(place, foreign, numbers):
    return 2 * ((numbers[1] & 1) ^ foreign) + place


def put_rows(numbers, sizes, sides, out_ref, place, group=8):
    labels = labels_of(numbers[0], numbers[1], sizes[1])
    rows, third = out_ref.shape[2] // 2, out_ref.shape[3]
    for first in range(0, LABELS, group):
        piece = low(sum(transposed(left(first * rows, group * rows), right) for left, right in sides))
        for own in range(group):
            for part in range(THIRDS):
                value = piece[own * rows : (own + 1) * rows, part * third : (part + 1) * third]
                out_ref[part, (first + own) ^ labels[part], place * rows : (place + 1) * rows] = value


def columns(ref):
    return lambda at, size: ref[:, at : at + size]


def blocks_out(width):
    return shaped((THIRDS, LABELS, 2 * width // LABELS, width // THIRDS), jnp.bfloat16)


def column_loads(source, target, foreign, numbers, sems):
    width = target.shape[2]
    copies = []
    for place in range(2):
        at = pl.ds(pl.multiple_of(matrix_at(place, foreign, numbers) * width, width), width)
        copies.append(pltpu.make_async_copy(source.at[:, at], target.at[place], sems.at[place]))
    return copies


def down_weight_kernel(foreign, sizes, numbers, act_in, grad_ref, out_ref, act_ref, sems):
    loads = column_loads(act_in, act_ref, foreign, numbers, sems)
    for copy in loads:
        copy.start()
    for place in range(2):
        loads[place].wait()
        put_rows(numbers, sizes, [(columns(act_ref.at[place]), grad_ref[...])], out_ref, place)


def down_weight(numbers, activation, grad, foreign, sizes, name, **waits):
    tokens, width = grad.shape
    return whole(
        functools.partial(down_weight_kernel, foreign, sizes),
        name,
        (numbers,), (activation, grad), [blocks_out(width)],
        [pltpu.VMEM((2, tokens, width), jnp.bfloat16), pltpu.SemaphoreType.DMA((2,))],
        4 * tokens * width * width,
        far=(0,),
        **waits,
    )


def up_back_kernel(foreign, sizes, numbers, grad_ref, slope_in, hidden_ref, up_ref, down_ref, before_ref, *refs):
    if foreign:
        out_ref, after_ref, totals_ref, pre_ref, slope_ref, sems = refs
    else:
        normed_ref, aux_ref, vec_ref, out_ref, totals_ref, first_ref, low_ref, sums_ref, pre_ref, slope_ref, sems = refs
        after_ref = first_ref
    width = grad_ref.shape[1]
    loads = column_loads(slope_in, slope_ref, foreign, numbers, sems)
    for copy in loads:
        copy.start()
    for place in range(2):
        at = pl.ds(pl.multiple_of(matrix_at(place, foreign, numbers) * width, width), width)
        before = before_ref if place == 0 else after_ref
        total = jnp.zeros((1, width), jnp.float32)
        later = dots(grad_ref[:TILE], down_ref[at])
        loads[place].wait()
        for start in range(0, grad_ref.shape[0], TILE):
            rows = slice(start, start + TILE)
            active_grad = later
            if start + TILE < grad_ref.shape[0]:
                later = dots(grad_ref[start + TILE : start + 2 * TILE], down_ref[at])
            pre_grad = low(active_grad * slope_ref[place, rows].astype(jnp.float32))
            pre_ref[rows] = pre_grad
            total = total + sums_of(pre_grad.astype(jnp.float32))
            after_ref[rows] = before[rows] + dots(pre_grad, up_ref[:, at])
        totals_ref[place] = jnp.broadcast_to(total, totals_ref.shape[1:])
        put_rows(numbers, sizes, [(columns(hidden_ref), pre_ref[...])], out_ref, place)
    if foreign:
        return
    hidden_grad, normed = after_ref[...], normed_ref[...]
    first_sum = norm_back(hidden_grad, normed, aux_ref[:, 127:128], vec_ref[FIRST_GAIN : FIRST_GAIN + 1])
    attended_grad = low(first_sum)
    first_ref[...] = first_sum
    low_ref[...] = attended_grad
    sums_ref[...] = jnp.zeros_like(sums_ref)
    sums_ref[0:1] = sums_of(attended_grad.astype(jnp.float32))
    sums_ref[1:2] = sums_of(hidden_grad * normed)
    sums_ref[2:3] = sums_of(hidden_grad)


def up_back(numbers, grad, slope, hidden_low, up, down, before, foreign, sizes, name, rest=(), **waits):
    tokens, width = grad.shape
    wide = shaped((tokens, width), jnp.float32)
    totals = shaped((2, 8, width), jnp.float32)
    pre = [
        pltpu.VMEM((tokens, width), jnp.bfloat16),
        pltpu.VMEM((2, tokens, width), jnp.bfloat16),
        pltpu.SemaphoreType.DMA((2,)),
    ]
    if foreign:
        outs, scratch = [blocks_out(width), wide, totals], pre
    else:
        outs = [blocks_out(width), totals, wide, shaped((tokens, width), jnp.bfloat16), shaped((8, width), jnp.float32)]
        scratch = pre
    return whole(
        functools.partial(up_back_kernel, foreign, sizes),
        name,
        (numbers,), (grad, slope, hidden_low, up, down, before, *rest), outs, scratch,
        12 * tokens * width * width,
        far=(1,),
        limit=12,
        **waits,
    )


def attend_back_kernel(count, row, half, lengths, q_ref, k_ref, v_ref, grad_ref, wo_ref, aux_ref, *refs):
    out_ref, totals_ref, bias_ref, ctx_ref, dk_ref, dv_ref = refs[-6:]
    width = q_ref.shape[1]
    span = q_ref.shape[0] // lengths.shape[0]
    base = row * span
    grad = grad_ref[base : base + span]
    part = width // 2
    ctx_ref[...] = low(dots(grad, wo_ref[half * part : (half + 1) * part]))
    fill_bias(lengths, row, count, span, bias_ref)
    scale = HEAD_DIM**-0.5
    scaled, plain = head_masks(scale), head_masks(1.0)
    dk_ref[...] = jnp.zeros_like(dk_ref)
    dv_ref[...] = jnp.zeros_like(dv_ref)

    def heads(pair, carry):
        at = pl.ds(pl.multiple_of(pair * 2 * HEAD_DIM, 2 * HEAD_DIM), 2 * HEAD_DIM)
        own = pl.ds(pl.multiple_of(pair * 2 * HEAD_DIM - half * part, 2 * HEAD_DIM), 2 * HEAD_DIM)
        lane = lax.broadcasted_iota(jnp.int32, (STEP, 128), 1)
        blocks = range(span // STEP)
        rows = [pl.ds(block * STEP, STEP) for block in blocks]
        keys = [pl.ds(window_start(block, span), WINDOW) for block in blocks]
        own_rows = [pl.ds(base + block * STEP, STEP) for block in blocks]
        own_keys = [pl.ds(base + window_start(block, span), WINDOW) for block in blocks]
        queries = [stacked(q_ref[own_rows[b], at], scaled) for b in blocks]
        context_grad = [stacked(ctx_ref[rows[b], own], plain) for b in blocks]
        scores = [dots(queries[b], k_ref[own_keys[b], at]) for b in blocks]
        prob_grad = [dots(context_grad[b], v_ref[own_keys[b], at]) for b in blocks]
        log_total = [
            jnp.concatenate(
                [
                    jnp.sum(jnp.where(lane == 2 * pair + side, aux_ref[own_rows[b]], 0.0), axis=1, keepdims=True)
                    for side in range(2)
                ],
                axis=0,
            )
            for b in blocks
        ]
        attention = [jnp.exp(biased(scores[b], bias_ref[b]) - log_total[b]) for b in blocks]
        inner = [jnp.sum(attention[b] * prob_grad[b], axis=1, keepdims=True) for b in blocks]
        score_grad = [low(attention[b] * (prob_grad[b] - inner[b])) for b in blocks]
        for b in blocks:
            out_ref[0, rows[b], at] = low(merged(product(score_grad[b], k_ref[own_keys[b], at])) * scale)
        for b in blocks:
            dk_ref[keys[b], own] += transposed(score_grad[b], queries[b])
        for b in blocks:
            dv_ref[keys[b], own] += transposed(low(attention[b]), context_grad[b])
        return carry

    pairs = part // (2 * HEAD_DIM)
    lax.fori_loop(half * pairs, (half + 1) * pairs, heads, 0)
    out_ref[1, :, half * part : (half + 1) * part] = low(dk_ref[...])
    out_ref[2, :, half * part : (half + 1) * part] = low(dv_ref[...])
    if half == 0:
        return
    out_ref[:, :, :part] = refs[0][:, :, :part]

    totals_ref[...] = jnp.zeros_like(totals_ref)
    totals_ref[0:1] = sums_of(out_ref[0].astype(jnp.float32))
    totals_ref[1:2] = sums_of(out_ref[2].astype(jnp.float32))


def attend_back(lengths, q, k, v, grad, wo, aux, row, half, before=None, **waits):
    tokens, width = q.shape
    span = tokens // lengths.shape[0]
    return whole(
        functools.partial(attend_back_kernel, lengths.shape[1], row, half),
        "attend_back",
        (lengths,),
        (q, k, v, grad, wo, aux) + (() if before is None else (before,)),
        [shaped((3, span, width), jnp.bfloat16), shaped((8, width), jnp.float32)],
        [
            pltpu.VMEM((span // STEP, STEP, WINDOW), jnp.float32),
            pltpu.VMEM((span, width // 2), jnp.bfloat16),
            pltpu.VMEM((span, width // 2), jnp.float32),
            pltpu.VMEM((span, width // 2), jnp.float32),
        ],
        span * width * width + 5 * span * WINDOW * width,
        **waits,
    )


def mixed_weight_kernel(foreign, sizes, numbers, x_ref, ctx_ref, grad_ref, one_ref, other_ref, out_ref):
    span = one_ref.shape[1]

    def put(left, matrix, place):
        if matrix == 3:
            put_rows(numbers, sizes, [(columns(ctx_ref), grad_ref[...])], out_ref, place)
            return
        first = lambda at, size: left[:span, at : at + size]
        second = lambda at, size: left[span:, at : at + size]
        put_rows(numbers, sizes, [(first, one_ref[matrix]), (second, other_ref[matrix])], out_ref, place)

    for pair in range(2):

        @pl.when(matrix_at(0, foreign, numbers) == 2 * pair)
        def _(pair=pair):
            put(x_ref, 2 * pair, 0)
            put(x_ref, 2 * pair + 1, 1)


def mixed_weight(numbers, x, context, grad, grads, foreign, sizes, name, **waits):
    tokens, width = x.shape
    return whole(
        functools.partial(mixed_weight_kernel, foreign, sizes),
        name,
        (numbers,), (x, context, grad, *grads), [blocks_out(width)], [],
        4 * tokens * width * width,
        **waits,
    )


def input_kernel(steps, first_ref, one_ref, other_ref, wq_ref, wk_ref, wv_ref, out_ref):
    def put(grad_ref):
        out_ref[...] = first_ref[...] + dots(grad_ref[0], wq_ref[...]) + dots(grad_ref[1], wk_ref[...]) + dots(grad_ref[2], wv_ref[...])

    @pl.when(pl.program_id(0) < steps)
    def _():
        put(one_ref)

    @pl.when(pl.program_id(0) >= steps)
    def _():
        put(other_ref)


def input_back(first_sum, grads, weights, **waits):
    tokens, width = first_sum.shape
    rows = 256
    steps = grads[0].shape[1] // rows
    one = pl.BlockSpec((3, rows, width), lambda i, *_: (0, jnp.minimum(i, steps - 1), 0))
    other = pl.BlockSpec((3, rows, width), lambda i, *_: (0, jnp.maximum(i - steps, 0), 0))
    return call(
        functools.partial(input_kernel, steps),
        "input_grad",
        (tokens // rows,),
        [rows_spec(rows, width), one, other] + [full_spec((width, width))] * 3,
        [rows_spec(rows, width)],
        [shaped((tokens, width), jnp.float32)],
        [],
        6 * tokens * width * width,
        14 * tokens * width + 6 * width * width,
        (), first_sum, *grads, *weights, **waits,
    )


VECTOR_ROWS = 48


def encoded(values):
    high, rest = two_parts(values)
    return jnp.concatenate([high, rest], axis=0)


def decoded(block):
    block = block.astype(jnp.float32)
    return block[:VECTOR_ROWS] + block[VECTOR_ROWS:]


def bundle_kernel(numbers, first_ref, second_ref, one_ref, other_ref, send_ref, keep_ref, coded_ref, target_ref):
    width = first_ref.shape[1]
    third = target_ref.shape[1]
    pieces = width // third
    target_ref[...] = jnp.zeros_like(target_ref)

    def put(row, values):
        for piece in range(pieces):
            target_ref[pl.ds(row * pieces + piece, 1)] = values[:, piece * third : (piece + 1) * third]

    for row in range(2):
        put(row, one_ref[row : row + 1] + other_ref[row : row + 1])
    for row in range(3):
        put(2 + row, first_ref[row : row + 1])
        put(5 + row, second_ref[row : row + 1])
    for place in range(2):
        put(8 + matrix_at(place, 0, numbers), keep_ref[place, 0:1])
        put(8 + matrix_at(place, 1, numbers), send_ref[place, 0:1])
    coded_ref[0] = encoded(target_ref[...])


def bundle(numbers, first, second, one, other, send, keep, **waits):
    third = first.shape[1] // THIRDS
    return whole(
        bundle_kernel, "vector_grads", (numbers,), (first, second, one, other, send, keep),
        [shaped((1, 2 * VECTOR_ROWS, third), jnp.bfloat16)], [pltpu.VMEM((VECTOR_ROWS, third), jnp.float32)], 0, **waits,
    )


def unbundle_kernel(source_ref, *targets):
    third = source_ref.shape[2]
    values = decoded(source_ref[0])
    row = 0
    for target in targets:
        for piece in range(target.shape[0] // third):
            target[piece * third : (piece + 1) * third] = values[row : row + 1].reshape(third)
            row += 1


def unbundle(block, sizes_out, **waits):
    return whole(
        unbundle_kernel, "unbundle", (), (block,), [shaped((size,), jnp.float32) for size in sizes_out], [], 0, **waits
    )


def local(
    inputs,
    lengths,
    positives,
    query_weight,
    query_bias,
    key_weight,
    value_weight,
    value_bias,
    output_weight,
    output_bias,
    first_gain,
    first_shift,
    up_weight,
    up_bias,
    down_weight_,
    down_bias,
    second_gain,
    second_shift,
):
    row_count, row_span, width = inputs.shape[1:]
    seg_count = lengths.shape[2]
    tokens = row_count * row_span
    hidden_width = up_weight.shape[1]
    sizes = (lax.axis_size("stream"), lax.axis_size("batch"))
    rest = halving_orders(sizes[1])[1]
    x = inputs.reshape(tokens, width)
    lengths = lengths.reshape(row_count, seg_count)
    numbers = jnp.stack([lax.axis_index("stream"), lax.axis_index("batch")]).astype(jnp.int32)
    vectors = (query_bias, value_bias, output_bias, first_gain, first_shift, down_bias, second_gain, second_shift, up_bias)
    q, k, v, context, aux, vec, first_normed, hidden_low = attend(
        lengths, x, (query_weight, key_weight, value_weight, output_weight), vectors
    )
    activation, slope, second_normed, second_factor, pooled, package = feed(
        lengths, positives, first_normed, hidden_low, up_weight, down_weight_, vec
    )
    own, foreign = gather_embeddings(package, sizes)
    contrast_terms, pooled_grad = contrast(numbers, lengths, own, foreign, pooled, sizes)
    second_sum, branch_grad, second_totals = second_back(
        lengths, pooled_grad, second_normed, second_factor, vec
    )
    orders, rest = halving_orders(sizes[1])
    far = orders[0][3]
    parts = range(THIRDS)
    half = LABELS // 2

    def flat(value):
        return value.reshape((-1,) + value.shape[2:])

    def same_link(i, step, other):
        return [order[other] for order in orders].index(orders[i][step])

    def chip_sums(keep, arrived, start):
        return [[(half, (keep, i * LABELS + start), (arrived, i * LABELS + start))] for i in parts]

    def sums(kept, kept_at, arrived, arrived_at, size):
        send = (size, (kept, kept_at + size), (arrived, arrived_at + size))
        return [send], [(size, (kept, kept_at), (arrived, arrived_at))]

    def all_sums(kept, arrived, size):
        both = [sums(kept[i], 0, arrived[i], 0, size) for i in parts]
        return [one[0] for one in both], [one[1] for one in both]

    def joined(former, former_at, latter, latter_at, size):
        return [(size, (former, former_at)), (size, (latter, latter_at))]

    def for_rest(outs, order, name):
        for dim in rest:
            arrived = [exchange(array, dim, sizes) for array, _ in outs]
            *arrays, order = fold(
                [
                    [(size, (array, start), (other, start)) for size, start in terms]
                    for (array, terms), other in zip(outs, arrived, strict=True)
                ],
                order, name,
            )
            outs = [(array, terms) for array, (_, terms) in zip(arrays, outs, strict=True)]
        return [array for array, _ in outs], order

    order = second_totals
    down_send, order = down_weight(numbers, activation, branch_grad, 1, sizes, "down_weight_send", carry=(order,))
    down_in = exchange(down_send, CORE, sizes)
    down_keep, order = down_weight(numbers, activation, branch_grad, 0, sizes, "down_weight_keep", carry=(order,))
    keep, arrived = flat(down_keep), flat(down_in)
    *made, order = fold(chip_sums(keep, arrived, half) + chip_sums(keep, arrived, 0), order, "down_0")
    down_kept = made[THIRDS:]
    down_in = exchange_each(made[:THIRDS], 0, sizes)
    up_send, partial_grad, up_totals_send, order = up_back(
        numbers, branch_grad, slope, hidden_low, up_weight, down_weight_, second_sum, 1, sizes, "up_back_send",
        carry=(order,),
    )
    sends, keeps = all_sums(down_kept, down_in, 4)
    up_send = flat(up_send)
    *made, up_send, order = fold(sends + keeps + [[(THIRDS * LABELS, (up_send, 0))]], order, "down_1")
    up_in = exchange(up_send, CORE, sizes)
    down_kept = made[THIRDS:]
    down_in = exchange_each(made[:THIRDS], 1, sizes)
    up_keep, up_totals_keep, first_sum, attended_grad, first_totals, order = up_back(
        numbers, branch_grad, slope, hidden_low, up_weight, down_weight_, partial_grad, 0, sizes, "up_back_keep",
        (first_normed, aux, vec), carry=(order,),
    )
    keep, arrived = flat(up_keep), up_in
    pair = [same_link(i, 0, 2) for i in parts]
    down_sends, down_keeps = all_sums(down_kept, down_in, 2)
    sends = chip_sums(keep, arrived, half)
    *made, order = fold(
        [sends[i] + down_sends[pair[i]] for i in parts]
        + chip_sums(keep, arrived, 0)
        + [down_keeps[pair[i]] for i in parts],
        order, "up_0",
    )
    up_kept, down_kept = made[THIRDS : 2 * THIRDS], made[2 * THIRDS :]
    up_in = exchange_each(made[:THIRDS], 0, sizes)
    back = functools.partial(attend_back, lengths, q, k, v, attended_grad, output_weight, aux)
    grads_one, totals_one, order = back(0, 0, carry=(order,))
    grads_one, totals_one, order = back(0, 1, before=grads_one, carry=(order,))
    sends, keeps = all_sums(up_kept, up_in, 4)
    far_sums = [sums(down_kept[pair.index(i)], 0, up_in[pair.index(i)], half, 1) for i in parts]
    *made, down_far, down_kept, order = fold(
        sends + keeps + [sum([one[0] for one in far_sums], []), sum([one[1] for one in far_sums], [])], order, "up_1"
    )
    up_kept = made[THIRDS:]
    up_in = exchange_each(made[:THIRDS], 1, sizes)
    down_in = exchange(down_far, far, sizes)
    grads_other, totals_other, order = back(1, 0, carry=(order,))
    sends, keeps = all_sums(up_kept, up_in, 2)
    *made, down, order = fold(sends + keeps + [[(THIRDS, (down_kept, 0), (down_in, 0))]], order, "up_2")
    up_kept = made[THIRDS:]
    up_in = exchange_each(made[:THIRDS], 2, sizes)
    (down,), order = for_rest([(down, [(THIRDS, 0)])], order, "down_rest")
    down_in = exchange(down, far, sizes)
    grads_other, totals_other, order = back(1, 1, before=grads_other, carry=(order,))
    grads = (grads_one, grads_other)
    sends, keeps = all_sums(up_kept, up_in, 1)
    up_far, up_kept, *down, order = fold(
        [sum(sends, []), sum(keeps, [])] + [joined(down, i, down_in, i, 1) for i in parts], order, "up_3"
    )
    up_in = exchange(up_far, far, sizes)
    down_in = exchange_each(down, 2, sizes)
    mixed_send, order = mixed_weight(
        numbers, x, context, attended_grad, grads, 1, sizes, "mixed_weight_send", carry=(order,)
    )
    mixed_in = exchange(mixed_send, CORE, sizes)
    vector, order = bundle(
        numbers, first_totals, second_totals, totals_one, totals_other, up_totals_send, up_totals_keep, carry=(order,)
    )
    mixed_keep, order = mixed_weight(
        numbers, x, context, attended_grad, grads, 0, sizes, "mixed_weight_keep", carry=(order,)
    )
    keep, arrived = flat(mixed_keep), flat(mixed_in)
    code = [[(1, (vector, 0))], [], []]
    pair = [same_link(i, 0, 1) for i in parts]
    sends = chip_sums(keep, arrived, half)
    *made, up, order = fold(
        [sends[i] + code[i] + joined(down[pair[i]], 0, down_in[pair[i]], 0, 2) for i in parts]
        + chip_sums(keep, arrived, 0)
        + [[(THIRDS, (up_kept, 0), (up_in, 0))]],
        order, "mixed_0",
    )
    mixed, mixed_kept = made[:THIRDS], made[THIRDS:]
    mixed_in = exchange_each(mixed, 0, sizes)
    (up,), order = for_rest([(up, [(THIRDS, 0)])], order, "up_rest")
    up_in = exchange(up, far, sizes)
    input_grad, order = input_back(first_sum, grads, (query_weight, key_weight, value_weight), carry=(order,))
    sends, keeps = all_sums(mixed_kept, mixed_in, 4)
    code = [[(0, (mixed[0], half), (mixed_in[0], half))], [], []]
    skip = [half + 1, half, half]
    down = [joined(mixed[i], skip[i], mixed_in[i], skip[i], 4) for i in (pair.index(j) for j in parts)]
    pair = [same_link(i, 1, 2) for i in parts]
    other = [same_link(i, 1, 0) for i in parts]
    *made, order = fold(
        [sends[i] + code[i] + joined(up, pair[i], up_in, pair[i], 1) + down[other[i]] for i in parts] + keeps,
        order, "mixed_1",
    )
    mixed, mixed_kept = made[:THIRDS], made[THIRDS:]
    mixed_in = exchange_each(mixed, 1, sizes)
    at = [(other.index(j), 7 if other.index(j) == 0 else 6) for j in parts]
    down, down_in = [(mixed[i], start) for i, start in at], [(mixed_in[i], start) for i, start in at]
    sends, keeps = all_sums(mixed_kept, mixed_in, 2)
    code = [[(0, (mixed[0], 4), (mixed_in[0], 4))], [], []]
    skip = [5, 4, 4]
    up = [joined(mixed[i], skip[i], mixed_in[i], skip[i], 2) for i in (pair.index(j) for j in parts)]
    pair = [same_link(i, 2, 1) for i in parts]
    *made, order = fold([sends[i] + code[i] + up[pair[i]] for i in parts] + keeps, order, "mixed_2")
    mixed, mixed_kept = made[:THIRDS], made[THIRDS:]
    mixed_in = exchange_each(mixed, 2, sizes)
    down, order = fold([sum([[(half, down[i]), (half, down_in[i])] for i in parts], [])], order, "down_2")
    down = [down, exchange(down, CORE, sizes)]
    code = [(0, (mixed[0], 2), (mixed_in[0], 2))]
    skip = [3, 2, 2]
    up = [joined(mixed[i], skip[i], mixed_in[i], skip[i], 4) for i in (pair.index(j) for j in parts)]
    whole_sums = sum([[(2, (mixed_kept[i], 0), (mixed_in[i], 0))] for i in parts], [])
    mixed, *up, order = fold([whole_sums + code] + up, order, "mixed_3")
    mixed_in = exchange(mixed, far, sizes)
    up_in = exchange_each(up, 0, sizes)
    down_total, order = spread(numbers, down, "tall", "down_spread", sizes, carry=(order,))
    crossed = [[(1, (mixed, 2 * i), (mixed_in, 2 * i + 1)), (1, (mixed, 2 * i + 1), (mixed_in, 2 * i))] for i in parts]
    *mixed, vector, order = fold(crossed + [[(0, (mixed, 2 * THIRDS), (mixed_in, 2 * THIRDS))]], order, "mixed_4")
    (*mixed, vector), order = for_rest(
        [(value, [(2, 0)]) for value in mixed] + [(vector, [(0, 0)])], order, "mixed_rest"
    )
    mixed_in = exchange_each(mixed, 2, sizes)
    up, order = fold([sum([joined(up[i], 0, up_in[i], 0, half) for i in parts], [])], order, "up_4")
    up = [up, exchange(up, CORE, sizes)]
    *mixed, order = fold([joined(mixed[i], 0, mixed_in[i], 0, 2) for i in parts], order, "mixed_5")
    mixed_in = exchange_each(mixed, 1, sizes)
    vector, order = fold([[(0, (vector, 0), (exchange(vector, CORE, sizes), 0))]], order, "vector_sums")
    *summed, order = unbundle(vector, [width] * 8 + [hidden_width], carry=(order,))
    *mixed, order = fold([joined(mixed[i], 0, mixed_in[i], 0, 4) for i in parts], order, "mixed_6")
    mixed_in = exchange_each(mixed, 0, sizes)
    up_total, order = spread(numbers, up, "wide", "up_spread", sizes, carry=(order,))
    mixed, order = fold([sum([joined(mixed[i], 0, mixed_in[i], 0, half) for i in parts], [])], order, "mixed_7")
    blocks = [mixed, exchange(mixed, CORE, sizes)]
    query_total, key_total, value_total, output_total = spread(
        numbers, blocks, "separate", "mixed_spread", sizes, after=(order,)
    )
    return (
        contrast_terms.reshape(1, row_count * seg_count),
        input_grad.reshape(1, row_count, row_span, width),
        query_total,
        summed[0],
        key_total,
        value_total,
        summed[1],
        output_total,
        summed[2],
        summed[3],
        summed[4],
        up_total,
        summed[8],
        down_total.reshape(hidden_width, width),
        summed[5],
        summed[6],
        summed[7],
    )


def solution(mesh):
    return jax.shard_map(
        local,
        mesh=mesh,
        in_specs=(
            P("stream", "batch", None, None),
            P("stream", "batch", None),
            P("batch"),
            P(),
            P(),
            P(),
            P(),
            P(),
            P(),
            P(),
            P(),
            P(),
            P(),
            P(),
            P(),
            P(),
            P(),
            P(),
        ),
        out_specs=(
            P("stream", "batch"),
            P("stream", "batch", None, None),
            P(),
            P(),
            P(),
            P(),
            P(),
            P(),
            P(),
            P(),
            P(),
            P(),
            P(),
            P(),
            P(),
            P(),
            P(),
        ),
        check_vma=False,
    )
```
